32 devices in a mesh: grp: 2 (over y), feat: 4 (over z), node: 4 (over x, core).
Axes of the slice: x: 2, y: 2, z: 4, core: 2. Of those that a mesh axis runs over, the one named last changes fastest.
Arguments:
- feat_t: bfloat16 [2048, 65536], P('feat', ('grp', 'node')), parts along dimension 1, may hold values from -6 to 6
- src_blocks: int32 [512, 16], P(('grp', 'node')), parts along dimension 0, may hold values from 0 to 255
- nbr_rows: int32 [512, 16, 128], P(('grp', 'node')), parts along dimension 0, may hold values from 0 to 127
- tile_counts: int32 [512], P(('grp', 'node')), parts along dimension 0, may hold values from 1 to 16, as said below
- w_neigh: bfloat16 [2048, 256], P('feat'), may hold values from -0.125 to 0.125
- w_self: bfloat16 [2048, 256], P('feat'), may hold values from -0.125 to 0.125
- bias: float32 [256], replicated, may hold values from -3 to 3
- cotangent: bfloat16 [8, 8192, 256], P(('grp', 'node'), 'feat'), parts along dimension 0, may hold values from -6 to 6
Outputs:
- hidden: bfloat16 [8, 8192, 256], P(('grp', 'node'), 'feat'), parts along dimension 0
- grad_neigh: float32 [4096, 256], P(('grp', 'feat')), parts along dimension 0
- grad_self: float32 [4096, 256], P(('grp', 'feat')), parts along dimension 0
- grad_bias: float32 [512], P('grp'), parts along dimension 0
The draws below stay inside these ranges and needn't reach their ends.
There are 2 independent parts, one for each index of `grp`. The reference program is written for one: setup_inputs(seed, part) draws one part's arguments, and reference() takes and returns one part's arrays. A program takes and returns all parts, laid end to end along the dimension named above; an argument that names none is the same for every part. Nothing has to cross between parts.
Inputs may be any that keep to these rules, and one draw needn't show every extreme that they name: `tile_counts`: valid slots come first in each block's list; every block has at least one.
All inputs are finite; a program needn't handle non-finite values.
Results may differ from the reference program's by a relative error of at most 0.006.
Values may be sent and summed in bfloat16 or wider, within the bound.
No kernel may reach another device: no remote copies, remote signals or barrier semaphores. Data moves between devices by JAX's collectives and lax.ppermute only.
A program may use at most 192 MiB of HBM per device.

```python
import jax
import jax.numpy as jnp
from jax import lax

F = 2048
HID = 256
BLK = 128
MAXT = 16
ROWS_DEV = 8192
NDST = 32768
NBLK = 256
N_NODE = 4


def draw_tile_counts(key, part):
    key = jax.random.fold_in(key, 11)
    k_heavy, k_light, k_high, k_place = jax.random.split(key, 4)
    ranks = jnp.arange(NBLK, dtype=jnp.int32)
    heavy = jax.random.randint(k_heavy, (NBLK,), 0, NBLK) < ranks
    light = jax.random.randint(k_light, (NBLK,), MAXT // 4, MAXT // 2 + 1)
    high = jax.random.randint(k_high, (NBLK,), 3 * MAXT // 4, MAXT + 1)
    counts = jnp.where(heavy, high, light)
    counts = jnp.maximum(counts, 1)
    place = jax.random.randint(k_place, (), 0, NBLK)
    counts = counts.at[place].set(MAXT)
    return counts.astype(jnp.int32)


def with_ends(values, rng, low, top_value):
    dims = values.shape
    spot = [jax.random.randint(jax.random.fold_in(rng, axis), (), 0, dims[axis]) for axis in range(len(dims))]
    values = values.at[tuple(spot)].set(low)
    longest = dims.index(max(dims))
    spot[longest] = (spot[longest] + 1) % dims[longest]
    return values.at[tuple(spot)].set(top_value)


def level_of(stream_key, extent, cuts, smallest, top_value):
    loudness, own = 1.0, jax.random.fold_in(stream_key, 6)
    for position, shards_of in cuts:
        steps = jnp.exp(jax.random.uniform(jax.random.fold_in(own, position), (shards_of,), jnp.float32, smallest / len(cuts), top_value / len(cuts)))
        loudness = loudness * jnp.repeat(steps, extent[position] // shards_of).reshape([-1 if axis == position else 1 for axis in range(len(extent))])
    return loudness


def bell_draw(stream_key, dims, width, reach, cuts=(), kind=jnp.bfloat16):
    entries = width * jax.random.normal(stream_key, dims, jnp.float32)
    if cuts:
        entries = entries * level_of(stream_key, dims, cuts, -0.22, 0.18)
    return jnp.clip(entries, -reach, reach).astype(kind)


def setup_inputs(seed: int = 0, part: int = 0) -> dict:
    seeds = jax.random.split(jax.random.key(seed), 9)
    part_splits = jax.random.split(jax.random.fold_in(seeds[8], part), 9)
    feat_t = bell_draw(part_splits[0], (F, NDST), 1.0, 6.0, ((0, 4), (1, 4)))
    src_blocks = with_ends(jax.random.randint(part_splits[1], (NBLK, MAXT), 0, NBLK), jax.random.fold_in(part_splits[1], 1), 0, NBLK - 1).astype(jnp.int32)
    nbr_rows = with_ends(jax.random.randint(part_splits[2], (NBLK, MAXT, BLK), 0, BLK), jax.random.fold_in(part_splits[2], 1), 0, BLK - 1).astype(jnp.int32)
    tile_counts = draw_tile_counts(jax.random.fold_in(jax.random.fold_in(seeds[8], part), 71), part)
    w_neigh = bell_draw(seeds[4], (F, HID), F ** -0.5, 0.125, ((0, 4),))
    w_self = bell_draw(seeds[5], (F, HID), F ** -0.5, 0.125, ((0, 4),))
    bias = bell_draw(seeds[6], (HID,), 0.5, 3.0, (), jnp.float32)
    cotangent = bell_draw(part_splits[7], (N_NODE, ROWS_DEV, HID), 1.0, 6.0, ((0, 4), (1, 4)))
    return dict(feat_t=feat_t, src_blocks=src_blocks, nbr_rows=nbr_rows, tile_counts=tile_counts, w_neigh=w_neigh, w_self=w_self, bias=bias, cotangent=cotangent)


def reference(feat_t, src_blocks, nbr_rows, tile_counts, w_neigh, w_self, bias, cotangent):
    sources = feat_t.reshape(F, NBLK, BLK)
    slot_ids = jnp.arange(MAXT, dtype=jnp.int32)

    def one_block(args):
        source_ids, neighbours, count = args
        picked = jnp.take(sources, source_ids, axis=1).astype(jnp.float32)
        gathered = jnp.take_along_axis(picked, neighbours[None, :, :], axis=2)
        keep = (slot_ids < count).astype(jnp.float32)
        total = jnp.sum(gathered * keep[None, :, None], axis=1)
        return total * (1.0 / count.astype(jnp.float32))

    sums = lax.map(one_block, (src_blocks, nbr_rows, tile_counts))
    neigh_t = jnp.transpose(sums, (1, 0, 2)).reshape(F, NDST).astype(jnp.bfloat16)
    pre = jnp.dot(neigh_t.T, w_neigh, preferred_element_type=jnp.float32)
    pre = pre + jnp.dot(feat_t.T, w_self, preferred_element_type=jnp.float32) + bias[None, :]
    hidden = jax.nn.silu(pre).astype(jnp.bfloat16).reshape(N_NODE, ROWS_DEV, HID)
    sigma = jax.nn.sigmoid(pre)
    slope = sigma * (1.0 + pre * (1.0 - sigma))
    grad_pre = (cotangent.reshape(NDST, HID).astype(jnp.float32) * slope).astype(jnp.bfloat16)
    grad_neigh = jnp.dot(neigh_t, grad_pre, preferred_element_type=jnp.float32)
    grad_self = jnp.dot(feat_t, grad_pre, preferred_element_type=jnp.float32)
    grad_bias = jnp.sum(grad_pre.astype(jnp.float32), axis=0)
    return hidden, grad_neigh, grad_self, grad_bias
```

```python
import functools

import jax
import jax.numpy as jnp
from jax import lax
from jax.experimental import pallas as pl
from jax.experimental.pallas import tpu as pltpu
from jax.sharding import PartitionSpec as P

CHUNKS = 2
VMEM_BYTES = 56 * 1024 * 1024


def activation_slope(pre):
    sigma = jax.nn.sigmoid(pre)
    return sigma * (1.0 + pre * (1.0 - sigma))


def swap(value, mask, n):
    return lax.ppermute(value, "node", [(i, i ^ mask) for i in range(n)])


def onehot_tile(rows, side):
    ids = lax.broadcasted_iota(jnp.int32, (side, side), 0)
    return jnp.where(ids == rows, 1.0, 0.0).astype(jnp.bfloat16)


def mean_tiles(src, inv, nbr, parts, self_term, n_feat):
    n = len(parts)
    hid, rows = self_term.shape
    blocks, slots, side = nbr.shape
    share = rows // n_feat
    per_share = share // side

    def kernel(src_ref, inv_ref, nbr_ref, self_ref, *rest):
        part_refs = rest[:n]
        out_ref, table, sems = rest[n:]
        copies = [
            pltpu.make_async_copy(ref, table.at[:, pl.ds(k * rows, rows)], sems.at[k])
            for k, ref in enumerate(part_refs)
        ]
        for copy in copies:
            copy.start()
        for copy in copies:
            copy.wait()

        @pl.loop(0, blocks)
        def _(b):
            picked = []
            tiles = []
            for t in range(slots):
                at = pl.multiple_of(src_ref[b, t] * side, side)
                picked.append(table[:, pl.ds(at, side)])
                tiles.append(onehot_tile(nbr_ref[b, t : t + 1, :], side))
            total = jnp.dot(
                jnp.concatenate(picked, axis=1),
                jnp.concatenate(tiles, axis=0),
                preferred_element_type=jnp.float32,
            )
            own = self_ref[:, pl.ds(pl.multiple_of(b * side, side), side)]
            lane = pl.multiple_of((b % per_share) * side, side)
            out_ref[b // per_share, :, pl.ds(lane, side)] = (
                total * inv_ref[b] + own
            ).astype(jnp.bfloat16)

    vmem = pl.BlockSpec(memory_space=pltpu.VMEM)
    smem = pl.BlockSpec(memory_space=pltpu.SMEM)
    hbm = pl.BlockSpec(memory_space=pl.ANY)
    return pl.pallas_call(
        kernel,
        out_shape=jax.ShapeDtypeStruct((n_feat, hid, share), jnp.bfloat16),
        in_specs=[smem, smem, vmem, vmem] + [hbm] * n,
        out_specs=vmem,
        scratch_shapes=[
            pltpu.VMEM((hid, n * rows), jnp.bfloat16),
            pltpu.SemaphoreType.DMA((n,)),
        ],
        compiler_params=pltpu.CompilerParams(vmem_limit_bytes=VMEM_BYTES),
        cost_estimate=pl.CostEstimate(
            flops=4 * blocks * slots * side * side * hid,
            bytes_accessed=2 * n * rows * hid + 6 * rows * hid,
            transcendentals=0,
        ),
        name="mean_tiles",
    )(src, inv, nbr, self_term, *parts)


def spread_tiles(src, inv, nbr, grad, n):
    rows, hid = grad.shape
    blocks, slots, side = nbr.shape
    step = 512

    def kernel(src_ref, inv_ref, nbr_ref, grad_ref, out_ref, table):
        @pl.loop(0, n * rows // step)
        def _(i):
            table[pl.ds(pl.multiple_of(i * step, step), step), :] = jnp.zeros(
                (step, hid), jnp.float32
            )

        @pl.loop(0, blocks)
        def _(b):
            g = grad_ref[pl.ds(pl.multiple_of(b * side, side), side), :]
            scale = inv_ref[b]
            tiles = [onehot_tile(nbr_ref[b, t : t + 1, :], side) for t in range(slots)]
            terms = jnp.dot(
                jnp.concatenate(tiles, axis=0), g, preferred_element_type=jnp.float32
            )
            for t in range(slots):
                at = pl.ds(pl.multiple_of(src_ref[b, t] * side, side), side)
                table[at, :] += terms[t * side : (t + 1) * side, :] * scale

        for k in range(n):

            @pl.loop(0, rows // step)
            def _(i, k=k):
                at = pl.multiple_of(i * step, step)
                out_ref[k, pl.ds(at, step), :] = table[
                    pl.ds(k * rows + at, step), :
                ].astype(jnp.bfloat16)

    vmem = pl.BlockSpec(memory_space=pltpu.VMEM)
    smem = pl.BlockSpec(memory_space=pltpu.SMEM)
    return pl.pallas_call(
        kernel,
        out_shape=jax.ShapeDtypeStruct((n, rows, hid), jnp.bfloat16),
        in_specs=[smem, smem, vmem, vmem],
        out_specs=vmem,
        scratch_shapes=[pltpu.VMEM((n * rows, hid), jnp.float32)],
        compiler_params=pltpu.CompilerParams(vmem_limit_bytes=VMEM_BYTES),
        cost_estimate=pl.CostEstimate(
            flops=4 * blocks * slots * side * side * hid,
            bytes_accessed=2 * n * rows * hid + 2 * rows * hid,
            transcendentals=0,
        ),
        name="spread_tiles",
    )(src, inv, nbr, grad)


def on_device(n_node, n_feat, feat_t, src_blocks, nbr_rows, tile_counts, w_neigh, w_self, bias, cotangent):
    rows = feat_t.shape[1]
    hid = w_neigh.shape[1]
    blocks, slots = src_blocks.shape
    share = cotangent.shape[1]
    wide = hid // CHUNKS
    me = lax.axis_index("node")
    src = jnp.bitwise_xor(src_blocks // blocks, me) * blocks + src_blocks % blocks
    valid = jnp.arange(slots, dtype=jnp.int32)[None, :] < tile_counts[:, None]
    nbr = jnp.where(valid[:, :, None], nbr_rows, -1)
    inv = 1.0 / tile_counts.astype(jnp.float32)
    cot_rows = cotangent.reshape(share, hid)
    first = (((0,), (0,)), ((), ()))

    hiddens, grads_n, grads_s, sums = [], [], [], []
    gathered = []
    for c in range(CHUNKS):
        cols = slice(c * wide, (c + 1) * wide)
        own = lax.dot_general(
            w_neigh[:, cols], feat_t, first, preferred_element_type=jnp.float32
        ).astype(jnp.bfloat16)
        parts = [own]
        mask = 1
        masks = []
        while mask < n_node:
            masks.append(mask)
            mask *= 2
        held = {0: own}
        for mask in reversed(masks):
            for k in list(held):
                held[k ^ mask] = swap(held[k], mask, n_node)
        parts = [held[k] for k in range(n_node)]
        own_self = lax.dot_general(
            w_self[:, cols], feat_t, first, preferred_element_type=jnp.float32
        )
        gathered.append((parts, own_self))
    for c in range(CHUNKS):
        cols = slice(c * wide, (c + 1) * wide)
        parts, own_self = gathered[c]
        part_pre = mean_tiles(src, inv, nbr, parts, own_self, n_feat)
        pre_t = lax.psum_scatter(part_pre, "feat", scatter_dimension=0, tiled=True)
        pre = pre_t.reshape(wide, share).T.astype(jnp.float32) + bias[cols][None, :]
        hiddens.append(jax.nn.silu(pre).astype(jnp.bfloat16))
        grad_pre = (cot_rows[:, cols].astype(jnp.float32) * activation_slope(pre)).astype(
            jnp.bfloat16
        )
        piece = lax.all_gather(grad_pre, "feat", axis=0, tiled=True)
        table = spread_tiles(src, inv, nbr, piece, n_node)
        held = {k: table[k] for k in range(n_node)}
        mask = 1
        while mask < n_node:
            left = {}
            for k in list(held):
                if k & mask:
                    got = swap(held[k], mask, n_node)
                    left[k ^ mask] = (
                        held[k ^ mask].astype(jnp.float32) + got.astype(jnp.float32)
                    ).astype(jnp.bfloat16)
            held = left
            mask *= 2
        back = held[0]
        part_neigh = jnp.dot(feat_t, back, preferred_element_type=jnp.float32)
        part_self = jnp.dot(feat_t, piece, preferred_element_type=jnp.float32)
        part_bias = jnp.sum(piece.astype(jnp.float32), axis=0)
        g_n, g_s, g_b = lax.psum((part_neigh, part_self, part_bias), "node")
        grads_n.append(g_n)
        grads_s.append(g_s)
        sums.append(g_b)
    return (
        jnp.concatenate(hiddens, axis=1).reshape(1, share, hid),
        jnp.concatenate(grads_n, axis=1),
        jnp.concatenate(grads_s, axis=1),
        jnp.concatenate(sums, axis=0),
    )


def solution(mesh):
    return jax.shard_map(
        functools.partial(on_device, mesh.shape["node"], mesh.shape["feat"]),
        mesh=mesh,
        in_specs=(
            P("feat", ("grp", "node")),
            P(("grp", "node"), None),
            P(("grp", "node"), None, None),
            P(("grp", "node")),
            P("feat", None),
            P("feat", None),
            P(),
            P(("grp", "node"), "feat", None),
        ),
        out_specs=(
            P(("grp", "node"), "feat", None),
            P(("grp", "feat"), None),
            P(("grp", "feat"), None),
            P("grp"),
        ),
        check_vma=False,
    )
```

```python
import functools

import jax
import jax.numpy as jnp
from jax import lax
from jax.experimental import pallas as pl
from jax.experimental.pallas import tpu as pltpu
from jax.sharding import PartitionSpec as P

CHUNKS = 2
VMEM_BYTES = 56 * 1024 * 1024
HBM = pl.BlockSpec(memory_space=pl.ANY)
VMEM = pl.BlockSpec(memory_space=pltpu.VMEM)
SMEM = pl.BlockSpec(memory_space=pltpu.SMEM)
PARAMS = pltpu.CompilerParams(vmem_limit_bytes=VMEM_BYTES)


def cost(flops, moved):
    return pl.CostEstimate(flops=flops, bytes_accessed=moved, transcendentals=0)


def swap(value, mask, n):
    return lax.ppermute(value, "node", [(i, i ^ mask) for i in range(n)])


def masks_of(n):
    assert n & (n - 1) == 0
    return [1 << i for i in range(n.bit_length() - 1)]


def sum_over_node(value, n):
    for mask in masks_of(n):
        value = value + swap(value, mask, n)
    return value


def onehot_tile(row, ids):
    side = ids.shape[0]
    some = jnp.broadcast_to(row.astype(jnp.float32), (16, side)).astype(jnp.bfloat16)
    rows = jnp.concatenate([some] * (side // 16), axis=0)
    return jnp.where(ids == rows, jnp.bfloat16(1.0), jnp.bfloat16(0.0))


def side_ids(side):
    return lax.broadcasted_iota(jnp.int32, (side, side), 0).astype(jnp.float32).astype(jnp.bfloat16)


def project(feat_t, weights_t, n):
    width, rows = feat_t.shape
    wide = weights_t.shape[0] // (2 * n)
    step = min(1024, rows)

    def kernel(feat_ref, w_ref, *outs):
        for c in range(2 * n):
            outs[c][...] = jnp.dot(
                w_ref[c * wide : (c + 1) * wide, :],
                feat_ref[...],
                preferred_element_type=jnp.float32,
            ).astype(outs[c].dtype)

    return pl.pallas_call(
        kernel,
        grid=(rows // step,),
        in_specs=[
            pl.BlockSpec((width, step), lambda i: (0, i)),
            pl.BlockSpec(weights_t.shape, lambda i: (0, 0)),
        ],
        out_specs=[pl.BlockSpec((wide, step), lambda i: (0, i))] * (2 * n),
        out_shape=[jax.ShapeDtypeStruct((wide, rows), jnp.bfloat16)] * n
        + [jax.ShapeDtypeStruct((wide, rows), jnp.float32)] * n,
        compiler_params=PARAMS,
        cost_estimate=cost(
            2 * width * rows * weights_t.shape[0], 2 * width * rows + 6 * n * wide * rows
        ),
        name="project",
    )(feat_t, weights_t)


def mean_tiles(src, inv, nbr, parts, self_term):
    n = len(parts)
    wide, rows = self_term.shape
    blocks, slots, side = nbr.shape

    def kernel(src_ref, inv_ref, nbr_ref, self_ref, *rest):
        part_refs = rest[:n]
        out_ref, table, sems = rest[n:]
        copies = [
            pltpu.make_async_copy(ref, table.at[:, pl.ds(k * rows, rows)], sems.at[k])
            for k, ref in enumerate(part_refs)
        ]
        for copy in copies:
            copy.start()
        for copy in copies:
            copy.wait()
        ids = side_ids(side)

        @pl.loop(0, blocks)
        def _(b):
            picked = []
            tiles = []
            for t in range(slots):
                at = pl.multiple_of(src_ref[b, t] * side, side)
                picked.append(table[:, pl.ds(at, side)])
                tiles.append(onehot_tile(nbr_ref[b, t : t + 1, :], ids))
            total = jnp.dot(
                jnp.concatenate(picked, axis=1),
                jnp.concatenate(tiles, axis=0),
                preferred_element_type=jnp.float32,
            )
            at = pl.ds(pl.multiple_of(b * side, side), side)
            pre_t = total * inv_ref[b] + self_ref[:, at]
            out_ref[at, :] = pre_t.T.astype(jnp.bfloat16)

    return pl.pallas_call(
        kernel,
        out_shape=jax.ShapeDtypeStruct((rows, wide), jnp.bfloat16),
        in_specs=[SMEM, SMEM, VMEM, VMEM] + [HBM] * n,
        out_specs=VMEM,
        scratch_shapes=[
            pltpu.VMEM((wide, n * rows), jnp.bfloat16),
            pltpu.SemaphoreType.DMA((n,)),
        ],
        compiler_params=PARAMS,
        cost_estimate=cost(
            8 * blocks * slots * side * side * wide, 2 * n * rows * wide + 6 * rows * wide
        ),
        name="mean_tiles",
    )(src, inv, nbr, self_term, *parts)


def activate(pre, bias, cot, hidden, c):
    share, wide = pre.shape
    hid = cot.shape[1]
    chunk = pl.BlockSpec((share, wide), lambda i: (0, c))
    whole = pl.BlockSpec((share, wide), lambda i: (0, 0))
    held = [] if hidden is None else [hidden]

    def kernel(pre_ref, bias_ref, cot_ref, *rest):
        hidden_ref, grad_ref = rest[-2:]
        value = pre_ref[...].astype(jnp.float32) + bias_ref[...]
        sigma = jax.nn.sigmoid(value)
        hidden_ref[...] = (value * sigma).astype(jnp.bfloat16)
        slope = sigma * (1.0 + value * (1.0 - sigma))
        grad_ref[...] = (cot_ref[...].astype(jnp.float32) * slope).astype(jnp.bfloat16)

    return pl.pallas_call(
        kernel,
        grid=(1,),
        in_specs=[whole, pl.BlockSpec((1, wide), lambda i: (0, c)), chunk] + [HBM] * len(held),
        out_specs=[chunk, whole],
        out_shape=[
            jax.ShapeDtypeStruct((share, hid), jnp.bfloat16),
            jax.ShapeDtypeStruct((share, wide), jnp.bfloat16),
        ],
        input_output_aliases={3: 0} if held else {},
        compiler_params=PARAMS,
        cost_estimate=cost(20 * share * wide, 8 * share * wide),
        name="activate",
    )(pre, bias, cot, *held)


def spread_tiles(src, inv, nbr, grad, n):
    rows, wide = grad.shape
    blocks, slots, side = nbr.shape
    step = 512

    def kernel(src_ref, inv_ref, nbr_ref, grad_ref, *rest):
        outs, table = rest[:n], rest[n]
        ids = side_ids(side)

        @pl.loop(0, n * rows // step)
        def _(i):
            table[pl.ds(pl.multiple_of(i * step, step), step), :] = jnp.zeros(
                (step, wide), jnp.float32
            )

        @pl.loop(0, blocks)
        def _(b):
            g = grad_ref[pl.ds(pl.multiple_of(b * side, side), side), :]
            scale = inv_ref[b]
            tiles = [onehot_tile(nbr_ref[b, t : t + 1, :], ids) for t in range(slots)]
            terms = jnp.dot(
                jnp.concatenate(tiles, axis=0), g, preferred_element_type=jnp.float32
            )
            for t in range(slots):
                at = pl.ds(pl.multiple_of(src_ref[b, t] * side, side), side)
                table[at, :] += terms[t * side : (t + 1) * side, :] * scale

        for k in range(n):

            @pl.loop(0, rows // step)
            def _(i, k=k):
                at = pl.multiple_of(i * step, step)
                outs[k][pl.ds(at, step), :] = table[pl.ds(k * rows + at, step), :].astype(
                    jnp.bfloat16
                )

    return pl.pallas_call(
        kernel,
        out_shape=[jax.ShapeDtypeStruct((rows, wide), jnp.bfloat16)] * n,
        in_specs=[SMEM, SMEM, VMEM, VMEM],
        out_specs=[VMEM] * n,
        scratch_shapes=[pltpu.VMEM((n * rows, wide), jnp.float32)],
        compiler_params=PARAMS,
        cost_estimate=cost(
            8 * blocks * slots * side * side * wide, 2 * n * rows * wide + 2 * rows * wide
        ),
        name="spread_tiles",
    )(src, inv, nbr, grad)


def weight_grad(feat_t, grad, with_sum):
    width, rows = feat_t.shape
    wide = grad.shape[1]
    step = min(1024, rows)
    extra = 8 if with_sum else 0

    def kernel(feat_ref, grad_ref, out_ref):
        @pl.when(pl.program_id(0) == 0)
        def _():
            out_ref[...] = jnp.zeros_like(out_ref)

        out_ref[:width, :] += jnp.dot(
            feat_ref[...], grad_ref[...], preferred_element_type=jnp.float32
        )
        if with_sum:
            out_ref[width : width + 1, :] += jnp.sum(
                grad_ref[...].astype(jnp.float32), axis=0, keepdims=True
            )

    return pl.pallas_call(
        kernel,
        grid=(rows // step,),
        in_specs=[
            pl.BlockSpec((width, step), lambda i: (0, i)),
            pl.BlockSpec((step, wide), lambda i: (i, 0)),
        ],
        out_specs=pl.BlockSpec((width + extra, wide), lambda i: (0, 0)),
        out_shape=jax.ShapeDtypeStruct((width + extra, wide), jnp.float32),
        compiler_params=PARAMS,
        cost_estimate=cost(2 * width * rows * wide, 2 * rows * (width + wide)),
        name="weight_grad",
    )(feat_t, grad)


def on_device(n_node, n_feat, feat_t, src_blocks, nbr_rows, tile_counts, w_neigh, w_self, bias, cotangent):
    width, rows = feat_t.shape
    hid = w_neigh.shape[1]
    blocks, slots = src_blocks.shape
    share = cotangent.shape[1]
    me = lax.axis_index("node")
    src = jnp.bitwise_xor(src_blocks // blocks, me) * blocks + src_blocks % blocks
    valid = jnp.arange(slots, dtype=jnp.int32)[None, :] < tile_counts[:, None]
    nbr = jnp.where(valid[:, :, None], nbr_rows, -1)
    inv = 1.0 / tile_counts.astype(jnp.float32)
    cot_rows = cotangent.reshape(share, hid)
    bias_row = bias[None, :]

    weights_t = jnp.concatenate([w_neigh.T, w_self.T], axis=0)
    projected = project(feat_t, weights_t, CHUNKS)

    gathered = []
    for c in range(CHUNKS):
        held = {0: projected[c]}
        for mask in reversed(masks_of(n_node)):
            for k in list(held):
                held[k ^ mask] = swap(held[k], mask, n_node)
        gathered.append([held[k] for k in range(n_node)])

    hidden = None
    pieces = []
    for c in range(CHUNKS):
        part_pre = mean_tiles(src, inv, nbr, gathered[c], projected[CHUNKS + c])
        pre = lax.psum_scatter(part_pre, "feat", scatter_dimension=0, tiled=True)
        hidden, grad_pre = activate(pre, bias_row, cot_rows, hidden, c)
        pieces.append(lax.all_gather(grad_pre, "feat", axis=0, tiled=True))

    grads_n, grads_s, sums = [], [], []
    for c in range(CHUNKS):
        held = dict(enumerate(spread_tiles(src, inv, nbr, pieces[c], n_node)))
        for mask in masks_of(n_node):
            left = {}
            for k in held:
                if k & mask:
                    got = swap(held[k], mask, n_node)
                    left[k ^ mask] = (
                        held[k ^ mask].astype(jnp.float32) + got.astype(jnp.float32)
                    ).astype(jnp.bfloat16)
            held = left
        grads_n.append(sum_over_node(weight_grad(feat_t, held[0], False), n_node))
        both = sum_over_node(weight_grad(feat_t, pieces[c], True), n_node)
        grads_s.append(both[:width])
        sums.append(both[width])
    return (
        hidden.reshape(1, share, hid),
        jnp.concatenate(grads_n, axis=1),
        jnp.concatenate(grads_s, axis=1),
        jnp.concatenate(sums, axis=0),
    )


def solution(mesh):
    return jax.shard_map(
        functools.partial(on_device, mesh.shape["node"], mesh.shape["feat"]),
        mesh=mesh,
        in_specs=(
            P("feat", ("grp", "node")),
            P(("grp", "node"), None),
            P(("grp", "node"), None, None),
            P(("grp", "node")),
            P("feat", None),
            P("feat", None),
            P(),
            P(("grp", "node"), "feat", None),
        ),
        out_specs=(
            P(("grp", "node"), "feat", None),
            P(("grp", "feat"), None),
            P(("grp", "feat"), None),
            P("grp"),
        ),
        check_vma=False,
    )
```

```python
import functools

import jax
import jax.numpy as jnp
from jax import lax
from jax.experimental import pallas as pl
from jax.experimental.pallas import tpu as pltpu
from jax.sharding import PartitionSpec as P

CHUNKS = 2
MIB = 1024 * 1024
HBM = pl.BlockSpec(memory_space=pl.ANY)
VMEM = pl.BlockSpec(memory_space=pltpu.VMEM)
SMEM = pl.BlockSpec(memory_space=pltpu.SMEM)
PARAMS = pltpu.CompilerParams(vmem_limit_bytes=24 * MIB)


def cost(flops, moved):
    return pl.CostEstimate(flops=flops, bytes_accessed=moved, transcendentals=0)


def swap(value, mask, n):
    return lax.ppermute(value, "node", [(i, i ^ mask) for i in range(n)])


def masks_of(n):
    assert n & (n - 1) == 0
    return [1 << i for i in range(n.bit_length() - 1)]


def sum_over_node(value, n):
    for mask in masks_of(n):
        value = value + swap(value, mask, n)
    return value


def total_of(values):
    if len(values) == 1:
        return values[0]
    return sum(v.astype(jnp.float32) for v in values).astype(jnp.bfloat16)


def onehot_tile(row, ids):
    side = ids.shape[0]
    some = jnp.broadcast_to(row.astype(jnp.float32), (16, side)).astype(jnp.bfloat16)
    rows = jnp.concatenate([some] * (side // 16), axis=0)
    return jnp.where(ids == rows, jnp.bfloat16(1.0), jnp.bfloat16(0.0))


def side_ids(side):
    return lax.broadcasted_iota(jnp.int32, (side, side), 0).astype(jnp.float32).astype(jnp.bfloat16)


def project(feat_t, weights_t, n):
    width, rows = feat_t.shape
    wide = weights_t.shape[0] // (2 * n)
    step = min(1024, rows)

    def kernel(feat_ref, w_ref, *outs):
        value = jnp.dot(w_ref[...], feat_ref[...], preferred_element_type=jnp.float32)
        for c in range(2 * n):
            outs[c][...] = value[c * wide : (c + 1) * wide, :].astype(outs[c].dtype)

    return pl.pallas_call(
        kernel,
        grid=(rows // step,),
        in_specs=[
            pl.BlockSpec((width, step), lambda i: (0, i)),
            pl.BlockSpec(weights_t.shape, lambda i: (0, 0)),
        ],
        out_specs=[pl.BlockSpec((wide, step), lambda i: (0, i))] * (2 * n),
        out_shape=[jax.ShapeDtypeStruct((wide, rows), jnp.bfloat16)] * n
        + [jax.ShapeDtypeStruct((wide, rows), jnp.float32)] * n,
        compiler_params=PARAMS,
        cost_estimate=cost(
            2 * width * rows * weights_t.shape[0], 2 * width * rows + 6 * n * wide * rows
        ),
        name="project",
    )(feat_t, weights_t)


def mean_tiles(order, src, inv, nbr, parts, self_term, n_feat):
    n = len(parts)
    wide, rows = self_term.shape
    blocks, slots, side = nbr.shape
    share = rows // n_feat
    per_share = blocks // n_feat

    def kernel(order_ref, src_ref, inv_ref, nbr_ref, self_hbm, *rest):
        part_refs = rest[:n]
        out_hbm, table, self_ref, ready, sems, out_sems = rest[n:]
        copies = [
            pltpu.make_async_copy(ref, table.at[:, pl.ds(k * rows, rows)], sems.at[k])
            for k, ref in enumerate(part_refs)
        ]
        copies.append(pltpu.make_async_copy(self_hbm, self_ref, sems.at[n]))
        for copy in copies:
            copy.start()
        for copy in copies:
            copy.wait()
        ids = side_ids(side)

        def out_copy(s):
            at = pl.ds(pl.multiple_of(s * share, share), share)
            return pltpu.make_async_copy(ready.at[at, :], out_hbm.at[at, :], out_sems.at[s])

        @pl.loop(0, n_feat)
        def _(s):
            first = lax.rem(order_ref[0] + s, n_feat) * per_share

            @pl.loop(0, per_share, unroll=2)
            def _(i):
                b = first + i
                picked = []
                tiles = []
                for t in range(slots):
                    at = pl.multiple_of(src_ref[b, t] * side, side)
                    picked.append(table[:, pl.ds(at, side)])
                    tiles.append(onehot_tile(nbr_ref[b, t : t + 1, :], ids))
                total = jnp.dot(
                    jnp.concatenate(picked, axis=1),
                    jnp.concatenate(tiles, axis=0),
                    preferred_element_type=jnp.float32,
                )
                own = self_ref[:, pl.ds(pl.multiple_of(b * side, side), side)]
                pre_t = total * inv_ref[b] + own
                at = pl.multiple_of((s * per_share + i) * side, side)
                ready[pl.ds(at, side), :] = pre_t.T.astype(jnp.bfloat16)

            out_copy(s).start()

        @pl.loop(0, n_feat)
        def _(s):
            out_copy(s).wait()

    return pl.pallas_call(
        kernel,
        out_shape=jax.ShapeDtypeStruct((rows, wide), jnp.bfloat16),
        in_specs=[SMEM, SMEM, SMEM, VMEM, HBM] + [HBM] * n,
        out_specs=HBM,
        scratch_shapes=[
            pltpu.VMEM((wide, n * rows), jnp.bfloat16),
            pltpu.VMEM((wide, rows), jnp.float32),
            pltpu.VMEM((rows, wide), jnp.bfloat16),
            pltpu.SemaphoreType.DMA((n + 1,)),
            pltpu.SemaphoreType.DMA((n_feat,)),
        ],
        compiler_params=pltpu.CompilerParams(vmem_limit_bytes=24 * MIB),
        cost_estimate=cost(
            8 * blocks * slots * side * side * wide, 2 * n * rows * wide + 6 * rows * wide
        ),
        name="mean_tiles",
    )(order, src, inv, nbr, self_term, *parts)


def activate(shares, bias, cot, hidden, c, after):
    share, wide = shares[0].shape
    hid = cot.shape[1]
    chunk = pl.BlockSpec((share, wide), lambda i: (0, c))
    whole = pl.BlockSpec((share, wide), lambda i: (0, 0))
    held = [] if hidden is None else [hidden]
    n = len(shares)

    def kernel(bias_ref, cot_ref, *rest):
        hidden_ref, grad_ref = rest[-2:]
        value = bias_ref[...]
        for ref in rest[:n]:
            value = value + ref[...].astype(jnp.float32)
        sigma = jax.nn.sigmoid(value)
        hidden_ref[...] = (value * sigma).astype(jnp.bfloat16)
        slope = sigma * (1.0 + value * (1.0 - sigma))
        grad_ref[...] = (cot_ref[...].astype(jnp.float32) * slope).astype(jnp.bfloat16)

    return pl.pallas_call(
        kernel,
        grid=(1,),
        in_specs=[pl.BlockSpec((1, wide), lambda i: (0, c)), chunk] + [whole] * n + [HBM] * len(held + after),
        out_specs=[chunk, whole],
        out_shape=[
            jax.ShapeDtypeStruct((share, hid), jnp.bfloat16),
            jax.ShapeDtypeStruct((share, wide), jnp.bfloat16),
        ],
        input_output_aliases={2 + n: 0} if held else {},
        compiler_params=pltpu.CompilerParams(vmem_limit_bytes=24 * MIB),
        cost_estimate=cost(20 * share * wide, (6 + 2 * n) * share * wide),
        name="activate",
    )(bias, cot, *shares, *held, *after)


def spread_tiles(order, src, inv, nbr, pieces, n, after):
    wide = pieces[0].shape[1]
    share = pieces[0].shape[0]
    m = len(pieces)
    rows = m * share
    blocks, slots, side = nbr.shape
    step = 512
    assert slots % 2 == 0

    def kernel(order_ref, src_ref, inv_ref, nbr_ref, *rest):
        outs = rest[m + len(after) : m + len(after) + n + 1]
        table, grad_ref, ready, sems, out_sems = rest[m + len(after) + n + 1 :]
        loads = []
        for s in range(m):
            at = pl.multiple_of(lax.rem(order_ref[0] + s, m) * share, share)
            loads.append(
                pltpu.make_async_copy(rest[s], grad_ref.at[pl.ds(at, share), :], sems.at[s])
            )
        for load in loads:
            load.start()
        ids = side_ids(side)

        @pl.loop(0, n * rows // step)
        def _(i):
            table[pl.ds(pl.multiple_of(i * step, step), step), :] = jnp.zeros(
                (step, wide), jnp.float32
            )

        for load in loads:
            load.wait()
        copies = [pltpu.make_async_copy(grad_ref, outs[n], out_sems.at[n])]
        copies[0].start()

        @pl.loop(0, blocks, unroll=2)
        def _(b):
            g = grad_ref[pl.ds(pl.multiple_of(b * side, side), side), :]
            scale = inv_ref[b]
            tiles = [onehot_tile(nbr_ref[b, t : t + 1, :], ids) for t in range(slots)]
            terms = jnp.dot(
                jnp.concatenate(tiles, axis=0), g, preferred_element_type=jnp.float32
            )
            for t in range(0, slots, 2):
                one, two = src_ref[b, t], src_ref[b, t + 1]
                same = jnp.where(one == two, scale, 0.0)
                at_one = pl.ds(pl.multiple_of(one * side, side), side)
                at_two = pl.ds(pl.multiple_of(two * side, side), side)
                term_one = terms[t * side : (t + 1) * side, :]
                term_two = terms[(t + 1) * side : (t + 2) * side, :]
                new_one = table[at_one, :] + (term_one * scale + term_two * same)
                new_two = table[at_two, :] + (term_two * scale + term_one * same)
                table[at_one, :] = new_one
                table[at_two, :] = new_two

        for k in reversed(range(n)):

            @pl.loop(0, rows // step)
            def _(i, k=k):
                at = pl.multiple_of(i * step, step)
                ready[k, pl.ds(at, step), :] = table[pl.ds(k * rows + at, step), :].astype(
                    jnp.bfloat16
                )

            copies.append(pltpu.make_async_copy(ready.at[k], outs[k], out_sems.at[k]))
            copies[-1].start()
        for copy in copies:
            copy.wait()

    return pl.pallas_call(
        kernel,
        out_shape=[jax.ShapeDtypeStruct((rows, wide), jnp.bfloat16)] * (n + 1),
        in_specs=[SMEM, SMEM, SMEM, VMEM] + [HBM] * (m + len(after)),
        out_specs=[HBM] * (n + 1),
        scratch_shapes=[
            pltpu.VMEM((n * rows, wide), jnp.float32),
            pltpu.VMEM((rows, wide), jnp.bfloat16),
            pltpu.VMEM((n, rows, wide), jnp.bfloat16),
            pltpu.SemaphoreType.DMA((m,)),
            pltpu.SemaphoreType.DMA((n + 1,)),
        ],
        compiler_params=pltpu.CompilerParams(vmem_limit_bytes=40 * MIB),
        cost_estimate=cost(
            8 * blocks * slots * side * side * wide, 2 * n * rows * wide + 2 * rows * wide
        ),
        name="spread_tiles",
    )(order, src, inv, nbr, *pieces, *after)


def weight_grad(feat_t, grads, with_sum):
    width, rows = feat_t.shape
    wide = grads[0].shape[1]
    step = min(2048, rows)
    extra = 8 if with_sum else 0

    def kernel(feat_ref, *rest):
        out_ref = rest[-1]

        @pl.when(pl.program_id(0) == 0)
        def _():
            out_ref[...] = jnp.zeros_like(out_ref)

        value = rest[0][...]
        if len(grads) > 1:
            value = sum(ref[...].astype(jnp.float32) for ref in rest[:-1]).astype(jnp.bfloat16)
        out_ref[:width, :] += jnp.dot(feat_ref[...], value, preferred_element_type=jnp.float32)
        if with_sum:
            out_ref[width : width + 1, :] += jnp.sum(
                value.astype(jnp.float32), axis=0, keepdims=True
            )

    return pl.pallas_call(
        kernel,
        grid=(rows // step,),
        in_specs=[pl.BlockSpec((width, step), lambda i: (0, i))]
        + [pl.BlockSpec((step, wide), lambda i: (i, 0))] * len(grads),
        out_specs=pl.BlockSpec((width + extra, wide), lambda i: (0, 0)),
        out_shape=jax.ShapeDtypeStruct((width + extra, wide), jnp.float32),
        compiler_params=pltpu.CompilerParams(vmem_limit_bytes=16 * MIB),
        cost_estimate=cost(2 * width * rows * wide, 2 * rows * (width + wide)),
        name="weight_grad",
    )(feat_t, *grads)


def reduce_shares(part, n, direct):
    share = part.shape[0] // n
    if not direct:
        return [lax.psum_scatter(part, "feat", scatter_dimension=0, tiled=True)]
    got = [part[:share]]
    for s in range(1, n):
        got.append(
            lax.ppermute(
                part[s * share : (s + 1) * share], "feat", [(i, (i + s) % n) for i in range(n)]
            )
        )
    return got


def gather_shares(value, n, direct):
    if not direct:
        return [lax.all_gather(value, "feat", axis=0, tiled=True)]
    got = [value]
    for s in range(1, n):
        got.append(lax.ppermute(value, "feat", [((i + s) % n, i) for i in range(n)]))
    return got


def on_device(n_node, n_feat, feat_t, src_blocks, nbr_rows, tile_counts, w_neigh, w_self, bias, cotangent):
    width, rows = feat_t.shape
    hid = w_neigh.shape[1]
    blocks, slots = src_blocks.shape
    share = cotangent.shape[1]
    me = lax.axis_index("node")
    src = jnp.bitwise_xor(src_blocks // blocks, me) * blocks + src_blocks % blocks
    valid = jnp.arange(slots, dtype=jnp.int32)[None, :] < tile_counts[:, None]
    nbr = jnp.where(valid[:, :, None], nbr_rows, -1)
    inv = 1.0 / tile_counts.astype(jnp.float32)
    cot_rows = cotangent.reshape(share, hid)
    bias_row = bias[None, :]

    weights_t = jnp.concatenate([w_neigh.T, w_self.T], axis=0)
    projected = project(feat_t, weights_t, CHUNKS)

    gathered = []
    for c in range(CHUNKS):
        held = {0: projected[c]}
        for mask in reversed(masks_of(n_node)):
            for k in list(held):
                held[k ^ mask] = swap(held[k], mask, n_node)
        gathered.append([held[k] for k in range(n_node)])

    direct = n_feat <= 4
    order = jnp.reshape(lax.axis_index("feat") if direct else 0, (1,)).astype(jnp.int32)
    part_pres = [
        mean_tiles(order, src, inv, nbr, gathered[c], projected[CHUNKS + c], n_feat)
        for c in range(CHUNKS)
    ]
    hidden = None
    grad_pres, pieces = [], []
    for c in range(CHUNKS):
        shares = reduce_shares(part_pres[c], n_feat, direct)
        hidden, grad_pre = activate(
            shares, bias_row, cot_rows, hidden, c, part_pres[c + 1 : c + 2]
        )
        grad_pres.append(grad_pre)
        pieces.append(gather_shares(grad_pre, n_feat, direct and c == CHUNKS - 1))

    grads_n, grads_s, sums = [], [], []
    after = [grad_pres[-1]]
    for c in range(CHUNKS):
        *tables, piece = spread_tiles(order, src, inv, nbr, pieces[c], n_node, after)
        held = {k: [v] for k, v in enumerate(tables)}
        for mask in masks_of(n_node):
            left = {}
            for k in reversed(list(held)):
                if k & mask:
                    mine = held[k ^ mask]
                    left[k ^ mask] = mine + [swap(total_of(held[k]), mask, n_node)]
            held = left
            if mask == 1:
                after = [total_of(v) for k, v in held.items() if k]
                held = {k: [total_of(v)] if k else v for k, v in held.items()}
        grads_n.append(sum_over_node(weight_grad(feat_t, held[0], False), n_node))
        both = sum_over_node(weight_grad(feat_t, [piece], True), n_node)
        grads_s.append(both[:width])
        sums.append(both[width])
    return (
        hidden.reshape(1, share, hid),
        jnp.concatenate(grads_n, axis=1),
        jnp.concatenate(grads_s, axis=1),
        jnp.concatenate(sums, axis=0),
    )


def solution(mesh):
    return jax.shard_map(
        functools.partial(on_device, mesh.shape["node"], mesh.shape["feat"]),
        mesh=mesh,
        in_specs=(
            P("feat", ("grp", "node")),
            P(("grp", "node"), None),
            P(("grp", "node"), None, None),
            P(("grp", "node")),
            P("feat", None),
            P("feat", None),
            P(),
            P(("grp", "node"), "feat", None),
        ),
        out_specs=(
            P(("grp", "node"), "feat", None),
            P(("grp", "feat"), None),
            P(("grp", "feat"), None),
            P("grp"),
        ),
        check_vma=False,
    )
```

```python
import functools

import jax
import jax.numpy as jnp
from jax import lax
from jax.experimental import pallas as pl
from jax.experimental.pallas import tpu as pltpu
from jax.sharding import PartitionSpec as P

CHUNKS = 2
NEAR_PIECES = 4
MIB = 1024 * 1024
HBM = pl.BlockSpec(memory_space=pl.ANY)
VMEM = pl.BlockSpec(memory_space=pltpu.VMEM)
SMEM = pl.BlockSpec(memory_space=pltpu.SMEM)
PARAMS = pltpu.CompilerParams(vmem_limit_bytes=24 * MIB)


def cost(flops, moved):
    return pl.CostEstimate(flops=flops, bytes_accessed=moved, transcendentals=0)


def swap(value, mask, n):
    return lax.ppermute(value, "node", [(i, i ^ mask) for i in range(n)])


def masks_of(n):
    assert n & (n - 1) == 0
    return [1 << i for i in range(n.bit_length() - 1)]


def sum_over_node(value, n):
    for mask in masks_of(n):
        value = value + swap(value, mask, n)
    return value


def total_of(values):
    if len(values) == 1:
        return values[0]
    return sum(v.astype(jnp.float32) for v in values).astype(jnp.bfloat16)


def onehot_tile(row, ids):
    side = ids.shape[0]
    some = jnp.broadcast_to(row.astype(jnp.float32), (16, side)).astype(jnp.bfloat16)
    rows = jnp.concatenate([some] * (side // 16), axis=0)
    return jnp.where(ids == rows, jnp.bfloat16(1.0), jnp.bfloat16(0.0))


def side_ids(side):
    return lax.broadcasted_iota(jnp.int32, (side, side), 0).astype(jnp.float32).astype(jnp.bfloat16)


def project(feat_t, weights_t, n):
    width, rows = feat_t.shape
    wide = weights_t.shape[0] // (2 * n)
    step = min(1024, rows)

    def kernel(feat_ref, w_ref, *outs):
        value = jnp.dot(w_ref[...], feat_ref[...], preferred_element_type=jnp.float32)
        for c in range(2 * n):
            outs[c][...] = value[c * wide : (c + 1) * wide, :].astype(outs[c].dtype)

    return pl.pallas_call(
        kernel,
        grid=(rows // step,),
        in_specs=[
            pl.BlockSpec((width, step), lambda i: (0, i)),
            pl.BlockSpec(weights_t.shape, lambda i: (0, 0)),
        ],
        out_specs=[pl.BlockSpec((wide, step), lambda i: (0, i))] * (2 * n),
        out_shape=[jax.ShapeDtypeStruct((wide, rows), jnp.bfloat16)] * n
        + [jax.ShapeDtypeStruct((wide, rows), jnp.float32)] * n,
        compiler_params=PARAMS,
        cost_estimate=cost(
            2 * width * rows * weights_t.shape[0], 2 * width * rows + 6 * n * wide * rows
        ),
        name="project",
    )(feat_t, weights_t)


def mean_tiles(order, src, inv, nbr, parts, self_term, n_feat):
    n = len(parts)
    wide, rows = self_term.shape
    blocks, slots, side = nbr.shape
    share = rows // n_feat
    per_share = blocks // n_feat

    def kernel(order_ref, src_ref, inv_ref, nbr_ref, self_hbm, *rest):
        part_refs = rest[:n]
        out_hbm, table, self_ref, ready, sems, out_sems = rest[n:]
        copies = [
            pltpu.make_async_copy(ref, table.at[:, pl.ds(k * rows, rows)], sems.at[k])
            for k, ref in enumerate(part_refs)
        ]
        copies.append(pltpu.make_async_copy(self_hbm, self_ref, sems.at[n]))
        for copy in copies:
            copy.start()
        for copy in copies:
            copy.wait()
        ids = side_ids(side)

        def out_copy(s):
            at = pl.ds(pl.multiple_of(s * share, share), share)
            return pltpu.make_async_copy(ready.at[at, :], out_hbm.at[at, :], out_sems.at[s])

        @pl.loop(0, n_feat)
        def _(s):
            first = lax.rem(order_ref[0] + s, n_feat) * per_share

            @pl.loop(0, per_share, unroll=2)
            def _(i):
                b = first + i
                picked = []
                tiles = []
                for t in range(slots):
                    at = pl.multiple_of(src_ref[b, t] * side, side)
                    picked.append(table[:, pl.ds(at, side)])
                    tiles.append(onehot_tile(nbr_ref[b, t : t + 1, :], ids))
                total = jnp.dot(
                    jnp.concatenate(picked, axis=1),
                    jnp.concatenate(tiles, axis=0),
                    preferred_element_type=jnp.float32,
                )
                own = self_ref[:, pl.ds(pl.multiple_of(b * side, side), side)]
                pre_t = total * inv_ref[b] + own
                at = pl.multiple_of((s * per_share + i) * side, side)
                ready[pl.ds(at, side), :] = pre_t.T.astype(jnp.bfloat16)

            out_copy(s).start()

        @pl.loop(0, n_feat)
        def _(s):
            out_copy(s).wait()

    return pl.pallas_call(
        kernel,
        out_shape=jax.ShapeDtypeStruct((rows, wide), jnp.bfloat16),
        in_specs=[SMEM, SMEM, SMEM, VMEM, HBM] + [HBM] * n,
        out_specs=HBM,
        scratch_shapes=[
            pltpu.VMEM((wide, n * rows), jnp.bfloat16),
            pltpu.VMEM((wide, rows), jnp.float32),
            pltpu.VMEM((rows, wide), jnp.bfloat16),
            pltpu.SemaphoreType.DMA((n + 1,)),
            pltpu.SemaphoreType.DMA((n_feat,)),
        ],
        compiler_params=pltpu.CompilerParams(vmem_limit_bytes=24 * MIB),
        cost_estimate=cost(
            8 * blocks * slots * side * side * wide, 2 * n * rows * wide + 6 * rows * wide
        ),
        name="mean_tiles",
    )(order, src, inv, nbr, self_term, *parts)


def activate(shares, bias, cot, hidden, c, after):
    share, wide = shares[0].shape
    hid = cot.shape[1]
    chunk = pl.BlockSpec((share, wide), lambda i: (0, c))
    whole = pl.BlockSpec((share, wide), lambda i: (0, 0))
    held = [] if hidden is None else [hidden]
    n = len(shares)

    def kernel(bias_ref, cot_ref, *rest):
        hidden_ref, grad_ref = rest[-2:]
        value = bias_ref[...]
        for ref in rest[:n]:
            value = value + ref[...].astype(jnp.float32)
        sigma = jax.nn.sigmoid(value)
        hidden_ref[...] = (value * sigma).astype(jnp.bfloat16)
        slope = sigma * (1.0 + value * (1.0 - sigma))
        grad_ref[...] = (cot_ref[...].astype(jnp.float32) * slope).astype(jnp.bfloat16)

    return pl.pallas_call(
        kernel,
        grid=(1,),
        in_specs=[pl.BlockSpec((1, wide), lambda i: (0, c)), chunk] + [whole] * n + [HBM] * len(held + after),
        out_specs=[chunk, whole],
        out_shape=[
            jax.ShapeDtypeStruct((share, hid), jnp.bfloat16),
            jax.ShapeDtypeStruct((share, wide), jnp.bfloat16),
        ],
        input_output_aliases={2 + n: 0} if held else {},
        compiler_params=pltpu.CompilerParams(vmem_limit_bytes=24 * MIB),
        cost_estimate=cost(20 * share * wide, (6 + 2 * n) * share * wide),
        name="activate",
    )(bias, cot, *shares, *held, *after)


def spread_tiles(order, src, inv, nbr, pieces, n, after):
    wide = pieces[0].shape[1]
    share = pieces[0].shape[0]
    m = len(pieces)
    rows = m * share
    blocks, slots, side = nbr.shape
    step = 512
    assert slots % 2 == 0

    def kernel(order_ref, src_ref, inv_ref, nbr_ref, *rest):
        outs = rest[m + len(after) : m + len(after) + n + 1]
        table, grad_ref, ready, sems, out_sems = rest[m + len(after) + n + 1 :]
        loads = []
        for s in range(m):
            at = pl.multiple_of(lax.rem(order_ref[0] + s, m) * share, share)
            loads.append(
                pltpu.make_async_copy(rest[s], grad_ref.at[pl.ds(at, share), :], sems.at[s])
            )
        for load in loads:
            load.start()
        ids = side_ids(side)

        @pl.loop(0, n * rows // step)
        def _(i):
            table[pl.ds(pl.multiple_of(i * step, step), step), :] = jnp.zeros(
                (step, wide), jnp.float32
            )

        for load in loads:
            load.wait()
        copies = [pltpu.make_async_copy(grad_ref, outs[n], out_sems.at[n])]
        copies[0].start()

        @pl.loop(0, blocks, unroll=2)
        def _(b):
            g = grad_ref[pl.ds(pl.multiple_of(b * side, side), side), :]
            scale = inv_ref[b]
            tiles = [onehot_tile(nbr_ref[b, t : t + 1, :], ids) for t in range(slots)]
            terms = jnp.dot(
                jnp.concatenate(tiles, axis=0), g, preferred_element_type=jnp.float32
            )
            for t in range(0, slots, 2):
                one, two = src_ref[b, t], src_ref[b, t + 1]
                same = jnp.where(one == two, scale, 0.0)
                at_one = pl.ds(pl.multiple_of(one * side, side), side)
                at_two = pl.ds(pl.multiple_of(two * side, side), side)
                term_one = terms[t * side : (t + 1) * side, :]
                term_two = terms[(t + 1) * side : (t + 2) * side, :]
                new_one = table[at_one, :] + (term_one * scale + term_two * same)
                new_two = table[at_two, :] + (term_two * scale + term_one * same)
                table[at_one, :] = new_one
                table[at_two, :] = new_two

        for k in reversed(range(n)):

            @pl.loop(0, rows // step)
            def _(i, k=k):
                at = pl.multiple_of(i * step, step)
                ready[k, pl.ds(at, step), :] = table[pl.ds(k * rows + at, step), :].astype(
                    jnp.bfloat16
                )

            copies.append(pltpu.make_async_copy(ready.at[k], outs[k], out_sems.at[k]))
            copies[-1].start()
        for copy in copies:
            copy.wait()

    return pl.pallas_call(
        kernel,
        out_shape=[jax.ShapeDtypeStruct((rows, wide), jnp.bfloat16)] * (n + 1),
        in_specs=[SMEM, SMEM, SMEM, VMEM] + [HBM] * (m + len(after)),
        out_specs=[HBM] * (n + 1),
        scratch_shapes=[
            pltpu.VMEM((n * rows, wide), jnp.float32),
            pltpu.VMEM((rows, wide), jnp.bfloat16),
            pltpu.VMEM((n, rows, wide), jnp.bfloat16),
            pltpu.SemaphoreType.DMA((m,)),
            pltpu.SemaphoreType.DMA((n + 1,)),
        ],
        compiler_params=pltpu.CompilerParams(vmem_limit_bytes=40 * MIB),
        cost_estimate=cost(
            8 * blocks * slots * side * side * wide, 2 * n * rows * wide + 2 * rows * wide
        ),
        name="spread_tiles",
    )(order, src, inv, nbr, *pieces, *after)


def weight_grad(feat_t, grads, with_sum):
    width, rows = feat_t.shape
    wide = grads[0].shape[1]
    step = min(2048, rows)
    extra = 8 if with_sum else 0

    def kernel(feat_ref, *rest):
        out_ref = rest[-1]

        @pl.when(pl.program_id(0) == 0)
        def _():
            out_ref[...] = jnp.zeros_like(out_ref)

        value = rest[0][...]
        if len(grads) > 1:
            value = sum(ref[...].astype(jnp.float32) for ref in rest[:-1]).astype(jnp.bfloat16)
        out_ref[:width, :] += jnp.dot(feat_ref[...], value, preferred_element_type=jnp.float32)
        if with_sum:
            out_ref[width : width + 1, :] += jnp.sum(
                value.astype(jnp.float32), axis=0, keepdims=True
            )

    return pl.pallas_call(
        kernel,
        grid=(rows // step,),
        in_specs=[pl.BlockSpec((width, step), lambda i: (0, i))]
        + [pl.BlockSpec((step, wide), lambda i: (i, 0))] * len(grads),
        out_specs=pl.BlockSpec((width + extra, wide), lambda i: (0, 0)),
        out_shape=jax.ShapeDtypeStruct((width + extra, wide), jnp.float32),
        compiler_params=pltpu.CompilerParams(vmem_limit_bytes=16 * MIB),
        cost_estimate=cost(2 * width * rows * wide, 2 * rows * (width + wide)),
        name="weight_grad",
    )(feat_t, *grads)


def reduce_shares(part, n, direct):
    share = part.shape[0] // n
    if not direct:
        return [lax.psum_scatter(part, "feat", scatter_dimension=0, tiled=True)]
    got = [part[:share]]
    for s in range(1, n):
        got.append(
            lax.ppermute(
                part[s * share : (s + 1) * share], "feat", [(i, (i + s) % n) for i in range(n)]
            )
        )
    return got


def gather_shares(value, n, direct):
    if not direct:
        return [lax.all_gather(value, "feat", axis=0, tiled=True)]
    got = [value]
    for s in range(1, n):
        got.append(lax.ppermute(value, "feat", [((i + s) % n, i) for i in range(n)]))
    return got


def on_device(n_node, n_feat, feat_t, src_blocks, nbr_rows, tile_counts, w_neigh, w_self, bias, cotangent):
    width, rows = feat_t.shape
    hid = w_neigh.shape[1]
    blocks, slots = src_blocks.shape
    share = cotangent.shape[1]
    me = lax.axis_index("node")
    src = jnp.bitwise_xor(src_blocks // blocks, me) * blocks + src_blocks % blocks
    valid = jnp.arange(slots, dtype=jnp.int32)[None, :] < tile_counts[:, None]
    nbr = jnp.where(valid[:, :, None], nbr_rows, -1)
    inv = 1.0 / tile_counts.astype(jnp.float32)
    cot_rows = cotangent.reshape(share, hid)
    bias_row = bias[None, :]

    weights_t = jnp.concatenate([w_neigh.T, w_self.T], axis=0)
    projected = project(feat_t, weights_t, CHUNKS)

    direct = False
    order = jnp.reshape(lax.axis_index("feat") if direct else 0, (1,)).astype(jnp.int32)
    part_pres = []
    for c in range(CHUNKS):
        held = {0: projected[c]}
        for mask in reversed(masks_of(n_node)):
            for k in list(held):
                value = held[k]
                if k and part_pres:
                    value, _ = lax.optimization_barrier((value, part_pres[-1]))
                held[k ^ mask] = swap(value, mask, n_node)
        gathered = [held[k] for k in range(n_node)]
        part_pres.append(
            mean_tiles(order, src, inv, nbr, gathered, projected[CHUNKS + c], n_feat)
        )
    hidden = None
    grad_pres, pieces = [], []
    for c in range(CHUNKS):
        part_pre = part_pres[c]
        if pieces:
            part_pre, pieces[-1][-1] = lax.optimization_barrier((part_pre, pieces[-1][-1]))
        shares = reduce_shares(part_pre, n_feat, direct)
        hidden, grad_pre = activate(
            shares, bias_row, cot_rows, hidden, c, part_pres[c + 1 : c + 2]
        )
        grad_pres.append(grad_pre)
        pieces.append(gather_shares(grad_pre, n_feat, direct and c == CHUNKS - 1))

    grads_n, grads_s, sums = [], [], []
    after = []
    arrived = None
    sent = []
    for c in range(CHUNKS):
        *tables, piece = spread_tiles(order, src, inv, nbr, pieces[c], n_node, after)
        held = {k: [v] for k, v in enumerate(tables)}
        for mask in masks_of(n_node):
            left = {}
            for k in reversed(list(held)):
                if k & mask:
                    mine = held[k ^ mask]
                    theirs = total_of(held[k])
                    if arrived is not None and mask == 1 and k != mask:
                        theirs, arrived = lax.optimization_barrier((theirs, arrived))
                        sent[c - 1][-1] = arrived
                    cut = rows // (NEAR_PIECES if mask == 1 and k != mask else 1)
                    got = [
                        swap(theirs[at : at + cut], mask, n_node) for at in range(0, rows, cut)
                    ]
                    left[k ^ mask] = mine + [got[0] if len(got) == 1 else jnp.concatenate(got)]
            held = left
            if mask == 1:
                after = [total_of(v) for k, v in held.items() if k]
                held = {k: [total_of(v)] if k else v for k, v in held.items()}
        arrived = held[0][-1]
        sent.append(held[0])
        both = sum_over_node(weight_grad(feat_t, [piece], True), n_node)
        grads_s.append(both[:width])
        sums.append(both[width])
    for terms in sent:
        grads_n.append(sum_over_node(weight_grad(feat_t, terms, False), n_node))
    return (
        hidden.reshape(1, share, hid),
        jnp.concatenate(grads_n, axis=1),
        jnp.concatenate(grads_s, axis=1),
        jnp.concatenate(sums, axis=0),
    )


def solution(mesh):
    return jax.shard_map(
        functools.partial(on_device, mesh.shape["node"], mesh.shape["feat"]),
        mesh=mesh,
        in_specs=(
            P("feat", ("grp", "node")),
            P(("grp", "node"), None),
            P(("grp", "node"), None, None),
            P(("grp", "node")),
            P("feat", None),
            P("feat", None),
            P(),
            P(("grp", "node"), "feat", None),
        ),
        out_specs=(
            P(("grp", "node"), "feat", None),
            P(("grp", "feat"), None),
            P(("grp", "feat"), None),
            P("grp"),
        ),
        check_vma=False,
    )
```

```python
import functools

import jax
import jax.numpy as jnp
from jax import lax
from jax.experimental import pallas as pl
from jax.experimental.pallas import tpu as pltpu
from jax.sharding import PartitionSpec as P

CHUNKS = 2
NEAR_PIECES = 4
RING_CUTS = 2
MIB = 1024 * 1024
HBM = pl.BlockSpec(memory_space=pl.ANY)
VMEM = pl.BlockSpec(memory_space=pltpu.VMEM)
SMEM = pl.BlockSpec(memory_space=pltpu.SMEM)
PARAMS = pltpu.CompilerParams(vmem_limit_bytes=24 * MIB)


def cost(flops, moved):
    return pl.CostEstimate(flops=flops, bytes_accessed=moved, transcendentals=0)


def swap(value, mask, n):
    return lax.ppermute(value, "node", [(i, i ^ mask) for i in range(n)])


def masks_of(n):
    assert n & (n - 1) == 0
    return [1 << i for i in range(n.bit_length() - 1)]


def sum_over_node(value, n):
    for mask in masks_of(n):
        value = value + swap(value, mask, n)
    return value


def total_of(values):
    if len(values) == 1:
        return values[0]
    return sum(v.astype(jnp.float32) for v in values).astype(jnp.bfloat16)


def onehot_tile(row, ids):
    side = ids.shape[0]
    some = jnp.broadcast_to(row.astype(jnp.float32), (16, side)).astype(jnp.bfloat16)
    rows = jnp.concatenate([some] * (side // 16), axis=0)
    return jnp.where(ids == rows, jnp.bfloat16(1.0), jnp.bfloat16(0.0))


def side_ids(side):
    return lax.broadcasted_iota(jnp.int32, (side, side), 0).astype(jnp.float32).astype(jnp.bfloat16)


def project(feat_t, weight, n, dtype, after):
    width, rows = feat_t.shape
    hid = weight.shape[1]
    wide = hid // n
    step = min(1024, rows)

    def kernel(feat_ref, w_ref, *rest):
        outs, turned = rest[len(after) : len(after) + n], rest[-1]

        @pl.when(pl.program_id(0) == 0)
        def _():
            turned[...] = w_ref[...].astype(jnp.float32).T.astype(jnp.bfloat16)

        value = jnp.dot(turned[...], feat_ref[...], preferred_element_type=jnp.float32)
        for c in range(n):
            outs[c][...] = value[c * wide : (c + 1) * wide, :].astype(dtype)

    return pl.pallas_call(
        kernel,
        grid=(rows // step,),
        in_specs=[
            pl.BlockSpec((width, step), lambda i: (0, i)),
            pl.BlockSpec(weight.shape, lambda i: (0, 0)),
        ]
        + [HBM] * len(after),
        out_specs=[pl.BlockSpec((wide, step), lambda i: (0, i))] * n,
        out_shape=[jax.ShapeDtypeStruct((wide, rows), dtype)] * n,
        scratch_shapes=[pltpu.VMEM((hid, width), jnp.bfloat16)],
        compiler_params=pltpu.CompilerParams(vmem_limit_bytes=24 * MIB),
        cost_estimate=cost(2 * width * rows * hid, 2 * width * rows + 4 * hid * rows),
        name="project",
    )(feat_t, weight, *after)


def mean_tiles(src, inv, nbr, parts, self_term, n_feat):
    n = len(parts)
    wide, rows = self_term.shape
    blocks, slots, side = nbr.shape
    share = rows // n_feat
    per_share = blocks // n_feat

    def kernel(src_ref, inv_ref, nbr_ref, self_ref, *rest):
        part_refs = rest[:n]
        out_hbm, table, ready, out_sems = rest[n:]
        for k, ref in enumerate(part_refs):

            @pl.loop(0, rows // side, unroll=4)
            def _(i, k=k, ref=ref):
                at = pl.multiple_of(i * side, side)
                table[:, pl.ds(k * rows + at, side)] = ref[:, pl.ds(at, side)]

        ids = side_ids(side)

        def out_copy(s):
            at = pl.ds(pl.multiple_of(s * share, share), share)
            return pltpu.make_async_copy(ready.at[at, :], out_hbm.at[at, :], out_sems.at[s])

        @pl.loop(0, n_feat)
        def _(s):
            @pl.loop(0, per_share, unroll=2)
            def _(i):
                b = s * per_share + i
                picked = []
                tiles = []
                for t in range(slots):
                    at = pl.multiple_of(src_ref[b, t] * side, side)
                    picked.append(table[:, pl.ds(at, side)])
                    tiles.append(onehot_tile(nbr_ref[b, t : t + 1, :], ids))
                total = jnp.dot(
                    jnp.concatenate(picked, axis=1),
                    jnp.concatenate(tiles, axis=0),
                    preferred_element_type=jnp.float32,
                )
                own = self_ref[:, pl.ds(pl.multiple_of(b * side, side), side)]
                pre_t = total * inv_ref[b] + own
                at = pl.multiple_of(b * side, side)
                ready[pl.ds(at, side), :] = pre_t.T.astype(jnp.bfloat16)

            out_copy(s).start()

        @pl.loop(0, n_feat)
        def _(s):
            out_copy(s).wait()

    return pl.pallas_call(
        kernel,
        out_shape=jax.ShapeDtypeStruct((rows, wide), jnp.bfloat16),
        in_specs=[SMEM, SMEM, VMEM, VMEM] + [VMEM] * n,
        out_specs=HBM,
        scratch_shapes=[
            pltpu.VMEM((wide, n * rows), jnp.bfloat16),
            pltpu.VMEM((rows, wide), jnp.bfloat16),
            pltpu.SemaphoreType.DMA((n_feat,)),
        ],
        compiler_params=pltpu.CompilerParams(vmem_limit_bytes=32 * MIB),
        cost_estimate=cost(
            8 * blocks * slots * side * side * wide, 2 * n * rows * wide + 6 * rows * wide
        ),
        name="mean_tiles",
    )(src, inv, nbr, self_term, *parts)


def activate(shares, bias, cot, hidden, c, after):
    share, wide = shares[0].shape
    hid = cot.shape[1]
    chunk = pl.BlockSpec((share, wide), lambda i: (0, c))
    whole = pl.BlockSpec((share, wide), lambda i: (0, 0))
    held = [] if hidden is None else [hidden]
    n = len(shares)

    def kernel(bias_ref, cot_ref, *rest):
        hidden_ref, grad_ref = rest[-2:]
        value = bias_ref[...]
        for ref in rest[:n]:
            value = value + ref[...].astype(jnp.float32)
        sigma = jax.nn.sigmoid(value)
        hidden_ref[...] = (value * sigma).astype(jnp.bfloat16)
        slope = sigma * (1.0 + value * (1.0 - sigma))
        grad_ref[...] = (cot_ref[...].astype(jnp.float32) * slope).astype(jnp.bfloat16)

    return pl.pallas_call(
        kernel,
        grid=(1,),
        in_specs=[pl.BlockSpec((1, wide), lambda i: (0, c)), chunk] + [whole] * n + [HBM] * len(held + after),
        out_specs=[chunk, whole],
        out_shape=[
            jax.ShapeDtypeStruct((share, hid), jnp.bfloat16),
            jax.ShapeDtypeStruct((share, wide), jnp.bfloat16),
        ],
        input_output_aliases={2 + n: 0} if held else {},
        compiler_params=pltpu.CompilerParams(vmem_limit_bytes=24 * MIB),
        cost_estimate=cost(20 * share * wide, (6 + 2 * n) * share * wide),
        name="activate",
    )(bias, cot, *shares, *held, *after)


def spread_tiles(order, src, inv, nbr, pieces, n, after):
    cut, wide = pieces[0][0].shape
    shares, cuts = len(pieces), len(pieces[0])
    m = shares * cuts
    rows = m * cut
    pieces = [piece for share in pieces for piece in share]
    blocks, slots, side = nbr.shape
    step = 512
    assert slots % 2 == 0

    def kernel(order_ref, src_ref, inv_ref, nbr_ref, *rest):
        outs = rest[m + len(after) : m + len(after) + n + 1]
        table, grad_ref, ready, sems, out_sems = rest[m + len(after) + n + 1 :]
        loads = []
        for s in range(m):
            at = lax.rem(order_ref[0] + s // cuts, shares) * (cuts * cut) + s % cuts * cut
            place = pl.ds(pl.multiple_of(at, cut), cut)
            loads.append(pltpu.make_async_copy(rest[s], grad_ref.at[place, :], sems.at[s]))
        for load in loads:
            load.start()
        ids = side_ids(side)

        @pl.loop(0, n * rows // step)
        def _(i):
            table[pl.ds(pl.multiple_of(i * step, step), step), :] = jnp.zeros(
                (step, wide), jnp.float32
            )

        for load in loads:
            load.wait()
        copies = [pltpu.make_async_copy(grad_ref, outs[n], out_sems.at[n])]
        copies[0].start()

        @pl.loop(0, blocks, unroll=2)
        def _(b):
            g = grad_ref[pl.ds(pl.multiple_of(b * side, side), side), :]
            scale = inv_ref[b]
            tiles = [onehot_tile(nbr_ref[b, t : t + 1, :], ids) for t in range(slots)]
            terms = jnp.dot(
                jnp.concatenate(tiles, axis=0), g, preferred_element_type=jnp.float32
            )
            for t in range(0, slots, 2):
                one, two = src_ref[b, t], src_ref[b, t + 1]
                same = jnp.where(one == two, scale, 0.0)
                at_one = pl.ds(pl.multiple_of(one * side, side), side)
                at_two = pl.ds(pl.multiple_of(two * side, side), side)
                term_one = terms[t * side : (t + 1) * side, :]
                term_two = terms[(t + 1) * side : (t + 2) * side, :]
                new_one = table[at_one, :] + (term_one * scale + term_two * same)
                new_two = table[at_two, :] + (term_two * scale + term_one * same)
                table[at_one, :] = new_one
                table[at_two, :] = new_two

        for k in reversed(range(n)):

            @pl.loop(0, rows // step)
            def _(i, k=k):
                at = pl.multiple_of(i * step, step)
                ready[k, pl.ds(at, step), :] = table[pl.ds(k * rows + at, step), :].astype(
                    jnp.bfloat16
                )

            copies.append(pltpu.make_async_copy(ready.at[k], outs[k], out_sems.at[k]))
            copies[-1].start()
        for copy in copies:
            copy.wait()

    return pl.pallas_call(
        kernel,
        out_shape=[jax.ShapeDtypeStruct((rows, wide), jnp.bfloat16)] * (n + 1),
        in_specs=[SMEM, SMEM, SMEM, VMEM] + [HBM] * (m + len(after)),
        out_specs=[HBM] * (n + 1),
        scratch_shapes=[
            pltpu.VMEM((n * rows, wide), jnp.float32),
            pltpu.VMEM((rows, wide), jnp.bfloat16),
            pltpu.VMEM((n, rows, wide), jnp.bfloat16),
            pltpu.SemaphoreType.DMA((m,)),
            pltpu.SemaphoreType.DMA((n + 1,)),
        ],
        compiler_params=pltpu.CompilerParams(vmem_limit_bytes=40 * MIB),
        cost_estimate=cost(
            8 * blocks * slots * side * side * wide, 2 * n * rows * wide + 2 * rows * wide
        ),
        name="spread_tiles",
    )(order, src, inv, nbr, *pieces, *after)


def weight_grad(feat_t, grads, with_sum):
    width, rows = feat_t.shape
    wide = grads[0].shape[1]
    step = min(2048, rows)
    extra = 8 if with_sum else 0

    def kernel(feat_ref, *rest):
        out_ref = rest[-1]

        @pl.when(pl.program_id(0) == 0)
        def _():
            out_ref[...] = jnp.zeros_like(out_ref)

        value = rest[0][...]
        if len(grads) > 1:
            value = sum(ref[...].astype(jnp.float32) for ref in rest[:-1]).astype(jnp.bfloat16)
        out_ref[:width, :] += jnp.dot(feat_ref[...], value, preferred_element_type=jnp.float32)
        if with_sum:
            out_ref[width : width + 1, :] += jnp.sum(
                value.astype(jnp.float32), axis=0, keepdims=True
            )

    return pl.pallas_call(
        kernel,
        grid=(rows // step,),
        in_specs=[pl.BlockSpec((width, step), lambda i: (0, i))]
        + [pl.BlockSpec((step, wide), lambda i: (i, 0))] * len(grads),
        out_specs=pl.BlockSpec((width + extra, wide), lambda i: (0, 0)),
        out_shape=jax.ShapeDtypeStruct((width + extra, wide), jnp.float32),
        compiler_params=pltpu.CompilerParams(vmem_limit_bytes=16 * MIB),
        cost_estimate=cost(2 * width * rows * wide, 2 * rows * (width + wide)),
        name="weight_grad",
    )(feat_t, *grads)


def gather_shares(value, n, ring):
    if not ring:
        return [[lax.all_gather(value, "feat", axis=0, tiled=True)]]
    cut = value.shape[0] // RING_CUTS
    steps = [[value[h * cut : (h + 1) * cut] for h in range(RING_CUTS)]]
    for _ in range(n - 1):
        steps.append(
            [lax.ppermute(v, "feat", [(i, (i - 1) % n) for i in range(n)]) for v in steps[-1]]
        )
    return steps


def on_device(n_node, n_feat, feat_t, src_blocks, nbr_rows, tile_counts, w_neigh, w_self, bias, cotangent):
    width, rows = feat_t.shape
    hid = w_neigh.shape[1]
    blocks, slots = src_blocks.shape
    share = cotangent.shape[1]
    me = lax.axis_index("node")
    src = jnp.bitwise_xor(src_blocks // blocks, me) * blocks + src_blocks % blocks
    valid = jnp.arange(slots, dtype=jnp.int32)[None, :] < tile_counts[:, None]
    nbr = jnp.where(valid[:, :, None], nbr_rows, -1)
    inv = 1.0 / tile_counts.astype(jnp.float32)
    cot_rows = cotangent.reshape(share, hid)
    bias_row = bias[None, :]

    projected = project(feat_t, w_neigh, CHUNKS, jnp.bfloat16, [])
    own_terms = project(feat_t, w_self, CHUNKS, jnp.float32, projected[:1])

    ring = n_feat <= 4
    feat_index = jnp.reshape(lax.axis_index("feat"), (1,)).astype(jnp.int32)
    in_place = jnp.zeros((1,), jnp.int32)
    part_pres = []
    for c in range(CHUNKS):
        held = {0: projected[c]}
        for mask in reversed(masks_of(n_node)):
            for k in list(held):
                value = held[k]
                if k:
                    behind = part_pres[-1] if part_pres else own_terms[0]
                    value, _ = lax.optimization_barrier((value, behind))
                held[k ^ mask] = swap(value, mask, n_node)
        gathered = [held[k] for k in range(n_node)]
        part_pres.append(
            mean_tiles(src, inv, nbr, gathered, own_terms[c], n_feat)
        )
    hidden = None
    grad_pres, pieces = [], []
    for c in range(CHUNKS):
        part_pre = part_pres[c]
        shares = [lax.psum_scatter(part_pre, "feat", scatter_dimension=0, tiled=True)]
        hidden, grad_pre = activate(
            shares, bias_row, cot_rows, hidden, c, part_pres[c + 1 : c + 2]
        )
        grad_pres.append(grad_pre)
        pieces.append(gather_shares(grad_pre, n_feat, ring))

    grads_n, grads_s, sums = [], [], []
    after = [grad_pres[-1]]
    arrived = None
    sent = []
    for c in range(CHUNKS):
        *tables, piece = spread_tiles(
            feat_index if len(pieces[c]) > 1 else in_place,
            src,
            inv,
            nbr,
            pieces[c],
            n_node,
            after,
        )
        held = {k: [v] for k, v in enumerate(tables)}
        for mask in masks_of(n_node):
            left = {}
            for k in reversed(list(held)):
                if k & mask:
                    mine = held[k ^ mask]
                    theirs = total_of(held[k])
                    if arrived is not None and mask == 1 and k != mask:
                        theirs, arrived = lax.optimization_barrier((theirs, arrived))
                        sent[c - 1][-1] = arrived
                    cut = rows // (NEAR_PIECES if mask == 1 and k != mask else 1)
                    got = [
                        swap(theirs[at : at + cut], mask, n_node) for at in range(0, rows, cut)
                    ]
                    left[k ^ mask] = mine + [got[0] if len(got) == 1 else jnp.concatenate(got)]
            held = left
            if mask == 1:
                after = [total_of(v) for k, v in held.items() if k]
                held = {k: [total_of(v)] if k else v for k, v in held.items()}
        arrived = held[0][-1]
        sent.append(held[0])
        both = sum_over_node(weight_grad(feat_t, [piece], True), n_node)
        grads_s.append(both[:width])
        sums.append(both[width])
    for terms in sent:
        grads_n.append(sum_over_node(weight_grad(feat_t, terms, False), n_node))
    return (
        hidden.reshape(1, share, hid),
        jnp.concatenate(grads_n, axis=1),
        jnp.concatenate(grads_s, axis=1),
        jnp.concatenate(sums, axis=0),
    )


def solution(mesh):
    return jax.shard_map(
        functools.partial(on_device, mesh.shape["node"], mesh.shape["feat"]),
        mesh=mesh,
        in_specs=(
            P("feat", ("grp", "node")),
            P(("grp", "node"), None),
            P(("grp", "node"), None, None),
            P(("grp", "node")),
            P("feat", None),
            P("feat", None),
            P(),
            P(("grp", "node"), "feat", None),
        ),
        out_specs=(
            P(("grp", "node"), "feat", None),
            P(("grp", "feat"), None),
            P(("grp", "feat"), None),
            P("grp"),
        ),
        check_vma=False,
    )
```

```python
import functools

import jax
import jax.numpy as jnp
from jax import lax
from jax.experimental import pallas as pl
from jax.experimental.pallas import tpu as pltpu
from jax.sharding import PartitionSpec as P

CHUNKS = 2
NEAR_PIECES = 4
RING_CUTS = 2
MIB = 1024 * 1024
HBM = pl.BlockSpec(memory_space=pl.ANY)
VMEM = pl.BlockSpec(memory_space=pltpu.VMEM)
SMEM = pl.BlockSpec(memory_space=pltpu.SMEM)
PARAMS = pltpu.CompilerParams(vmem_limit_bytes=24 * MIB)


def cost(flops, moved):
    return pl.CostEstimate(flops=flops, bytes_accessed=moved, transcendentals=0)


def swap(value, mask, n):
    return lax.ppermute(value, "node", [(i, i ^ mask) for i in range(n)])


def masks_of(n):
    assert n & (n - 1) == 0
    return [1 << i for i in range(n.bit_length() - 1)]


def sum_over_node(keep, send, low, n):
    near, *far = masks_of(n)
    total = keep + swap(send, near, n)
    for mask in far:
        total = total + swap(total, mask, n)
    other = swap(total, near, n)
    return jnp.where(
        low[0] == 0,
        jnp.concatenate([total, other], axis=0),
        jnp.concatenate([other, total], axis=0),
    )


def total_of(values):
    if len(values) == 1:
        return values[0]
    return sum(v.astype(jnp.float32) for v in values).astype(jnp.bfloat16)


def onehot_tile(row, ids):
    side = ids.shape[0]
    some = jnp.broadcast_to(row.astype(jnp.float32), (16, side)).astype(jnp.bfloat16)
    rows = jnp.concatenate([some] * (side // 16), axis=0)
    return jnp.where(ids == rows, jnp.bfloat16(1.0), jnp.bfloat16(0.0))


def side_ids(side):
    return lax.broadcasted_iota(jnp.int32, (side, side), 0).astype(jnp.float32).astype(jnp.bfloat16)


def project(feat_t, weight, n, dtype, after):
    width, rows = feat_t.shape
    hid = weight.shape[1]
    wide = hid // n
    step = min(1024, rows)

    def kernel(feat_ref, w_ref, *rest):
        outs, turned = rest[len(after) : len(after) + n], rest[-1]

        @pl.when(pl.program_id(0) == 0)
        def _():
            turned[...] = w_ref[...].astype(jnp.float32).T.astype(jnp.bfloat16)

        value = jnp.dot(turned[...], feat_ref[...], preferred_element_type=jnp.float32)
        for c in range(n):
            outs[c][...] = value[c * wide : (c + 1) * wide, :].astype(dtype)

    return pl.pallas_call(
        kernel,
        grid=(rows // step,),
        in_specs=[
            pl.BlockSpec((width, step), lambda i: (0, i)),
            pl.BlockSpec(weight.shape, lambda i: (0, 0)),
        ]
        + [HBM] * len(after),
        out_specs=[pl.BlockSpec((wide, step), lambda i: (0, i))] * n,
        out_shape=[jax.ShapeDtypeStruct((wide, rows), dtype)] * n,
        scratch_shapes=[pltpu.VMEM((hid, width), jnp.bfloat16)],
        compiler_params=pltpu.CompilerParams(vmem_limit_bytes=24 * MIB),
        cost_estimate=cost(2 * width * rows * hid, 2 * width * rows + 4 * hid * rows),
        name="project",
    )(feat_t, weight, *after)


def mean_tiles(src, inv, nbr, parts, self_term, n_feat):
    n = len(parts)
    wide, rows = self_term.shape
    blocks, slots, side = nbr.shape
    share = rows // n_feat
    per_share = blocks // n_feat

    def kernel(src_ref, inv_ref, nbr_ref, self_hbm, *rest):
        part_refs = rest[:n]
        out_hbm, table, self_ref, ready, sems, out_sems = rest[n:]
        copies = [
            pltpu.make_async_copy(ref, table.at[:, pl.ds(k * rows, rows)], sems.at[k])
            for k, ref in enumerate(part_refs)
        ]
        copies.append(pltpu.make_async_copy(self_hbm, self_ref, sems.at[n]))
        for copy in copies:
            copy.start()
        for copy in copies:
            copy.wait()
        ids = side_ids(side)

        def out_copy(s):
            at = pl.ds(pl.multiple_of(s * share, share), share)
            return pltpu.make_async_copy(ready.at[at, :], out_hbm.at[at, :], out_sems.at[s])

        @pl.loop(0, n_feat)
        def _(s):
            @pl.loop(0, per_share, unroll=2)
            def _(i):
                b = s * per_share + i
                picked = []
                tiles = []
                for t in range(slots):
                    at = pl.multiple_of(src_ref[b, t] * side, side)
                    picked.append(table[:, pl.ds(at, side)])
                    tiles.append(onehot_tile(nbr_ref[b, t : t + 1, :], ids))
                total = jnp.dot(
                    jnp.concatenate(picked, axis=1),
                    jnp.concatenate(tiles, axis=0),
                    preferred_element_type=jnp.float32,
                )
                own = self_ref[:, pl.ds(pl.multiple_of(b * side, side), side)]
                pre_t = total * inv_ref[b] + own
                at = pl.multiple_of(b * side, side)
                ready[pl.ds(at, side), :] = pre_t.T.astype(jnp.bfloat16)

            out_copy(s).start()

        @pl.loop(0, n_feat)
        def _(s):
            out_copy(s).wait()

    return pl.pallas_call(
        kernel,
        out_shape=jax.ShapeDtypeStruct((rows, wide), jnp.bfloat16),
        in_specs=[SMEM, SMEM, VMEM, HBM] + [HBM] * n,
        out_specs=HBM,
        scratch_shapes=[
            pltpu.VMEM((wide, n * rows), jnp.bfloat16),
            pltpu.VMEM((wide, rows), jnp.float32),
            pltpu.VMEM((rows, wide), jnp.bfloat16),
            pltpu.SemaphoreType.DMA((n + 1,)),
            pltpu.SemaphoreType.DMA((n_feat,)),
        ],
        compiler_params=pltpu.CompilerParams(vmem_limit_bytes=56 * MIB),
        cost_estimate=cost(
            8 * blocks * slots * side * side * wide, 2 * n * rows * wide + 6 * rows * wide
        ),
        name="mean_tiles",
    )(src, inv, nbr, self_term, *parts)


def activate(shares, bias, cot, hidden, c, after):
    share, wide = shares[0].shape
    hid = cot.shape[1]
    chunk = pl.BlockSpec((share, wide), lambda i: (0, c))
    whole = pl.BlockSpec((share, wide), lambda i: (0, 0))
    held = [] if hidden is None else [hidden]
    n = len(shares)

    def kernel(bias_ref, cot_ref, *rest):
        hidden_ref, grad_ref = rest[-2:]
        value = bias_ref[...]
        for ref in rest[:n]:
            value = value + ref[...].astype(jnp.float32)
        sigma = jax.nn.sigmoid(value)
        hidden_ref[...] = (value * sigma).astype(jnp.bfloat16)
        slope = sigma * (1.0 + value * (1.0 - sigma))
        grad_ref[...] = (cot_ref[...].astype(jnp.float32) * slope).astype(jnp.bfloat16)

    return pl.pallas_call(
        kernel,
        grid=(1,),
        in_specs=[pl.BlockSpec((1, wide), lambda i: (0, c)), chunk] + [whole] * n + [HBM] * len(held + after),
        out_specs=[chunk, whole],
        out_shape=[
            jax.ShapeDtypeStruct((share, hid), jnp.bfloat16),
            jax.ShapeDtypeStruct((share, wide), jnp.bfloat16),
        ],
        input_output_aliases={2 + n: 0} if held else {},
        compiler_params=pltpu.CompilerParams(vmem_limit_bytes=24 * MIB),
        cost_estimate=cost(20 * share * wide, (6 + 2 * n) * share * wide),
        name="activate",
    )(bias, cot, *shares, *held, *after)


def spread_tiles(order, src, inv, nbr, pieces, n, after):
    cut, wide = pieces[0][0].shape
    shares, cuts = len(pieces), len(pieces[0])
    m = shares * cuts
    rows = m * cut
    pieces = [piece for share in pieces for piece in share]
    blocks, slots, side = nbr.shape
    step = 512
    assert slots % 2 == 0

    def kernel(order_ref, src_ref, inv_ref, nbr_ref, *rest):
        outs = rest[m + len(after) : m + len(after) + n + 1]
        table, grad_ref, ready, sems, out_sems = rest[m + len(after) + n + 1 :]
        loads = []
        for s in range(m):
            at = lax.rem(order_ref[0] + s // cuts, shares) * (cuts * cut) + s % cuts * cut
            place = pl.ds(pl.multiple_of(at, cut), cut)
            loads.append(pltpu.make_async_copy(rest[s], grad_ref.at[place, :], sems.at[s]))
        for load in loads:
            load.start()
        ids = side_ids(side)

        @pl.loop(0, n * rows // step)
        def _(i):
            table[pl.ds(pl.multiple_of(i * step, step), step), :] = jnp.zeros(
                (step, wide), jnp.float32
            )

        for load in loads:
            load.wait()
        copies = [pltpu.make_async_copy(grad_ref, outs[n], out_sems.at[n])]
        copies[0].start()

        @pl.loop(0, blocks, unroll=2)
        def _(b):
            g = grad_ref[pl.ds(pl.multiple_of(b * side, side), side), :]
            scale = inv_ref[b]
            tiles = [onehot_tile(nbr_ref[b, t : t + 1, :], ids) for t in range(slots)]
            terms = jnp.dot(
                jnp.concatenate(tiles, axis=0), g, preferred_element_type=jnp.float32
            )
            for t in range(0, slots, 2):
                one, two = src_ref[b, t], src_ref[b, t + 1]
                same = jnp.where(one == two, scale, 0.0)
                at_one = pl.ds(pl.multiple_of(one * side, side), side)
                at_two = pl.ds(pl.multiple_of(two * side, side), side)
                term_one = terms[t * side : (t + 1) * side, :]
                term_two = terms[(t + 1) * side : (t + 2) * side, :]
                new_one = table[at_one, :] + (term_one * scale + term_two * same)
                new_two = table[at_two, :] + (term_two * scale + term_one * same)
                table[at_one, :] = new_one
                table[at_two, :] = new_two

        for k in reversed(range(n)):

            @pl.loop(0, rows // step)
            def _(i, k=k):
                at = pl.multiple_of(i * step, step)
                ready[k, pl.ds(at, step), :] = table[pl.ds(k * rows + at, step), :].astype(
                    jnp.bfloat16
                )

            copies.append(pltpu.make_async_copy(ready.at[k], outs[k], out_sems.at[k]))
            copies[-1].start()
        for copy in copies:
            copy.wait()

    return pl.pallas_call(
        kernel,
        out_shape=[jax.ShapeDtypeStruct((rows, wide), jnp.bfloat16)] * (n + 1),
        in_specs=[SMEM, SMEM, SMEM, VMEM] + [HBM] * (m + len(after)),
        out_specs=[HBM] * (n + 1),
        scratch_shapes=[
            pltpu.VMEM((n * rows, wide), jnp.float32),
            pltpu.VMEM((rows, wide), jnp.bfloat16),
            pltpu.VMEM((n, rows, wide), jnp.bfloat16),
            pltpu.SemaphoreType.DMA((m,)),
            pltpu.SemaphoreType.DMA((n + 1,)),
        ],
        compiler_params=pltpu.CompilerParams(vmem_limit_bytes=40 * MIB),
        cost_estimate=cost(
            8 * blocks * slots * side * side * wide, 2 * n * rows * wide + 2 * rows * wide
        ),
        name="spread_tiles",
    )(order, src, inv, nbr, *pieces, *after)


def weight_grad(low, feat_t, grads, with_sum):
    width, rows = feat_t.shape
    wide = grads[0].shape[1]
    step = min(2048, rows)
    tall = width + (16 if with_sum else 0)
    half = tall // 2

    def kernel(low_ref, feat_ref, *rest):
        keep_ref, send_ref, total = rest[-3:]

        @pl.when(pl.program_id(0) == 0)
        def _():
            total[...] = jnp.zeros_like(total)

        value = rest[0][...]
        if len(grads) > 1:
            value = sum(ref[...].astype(jnp.float32) for ref in rest[:-3]).astype(jnp.bfloat16)
        total[:width, :] += jnp.dot(feat_ref[...], value, preferred_element_type=jnp.float32)
        if with_sum:
            total[width : width + 1, :] += jnp.sum(
                value.astype(jnp.float32), axis=0, keepdims=True
            )

        @pl.when(pl.program_id(0) == rows // step - 1)
        def _():
            low = low_ref[0]
            keep_ref[...] = total[pl.ds(pl.multiple_of(low * half, 8), half), :]
            send_ref[...] = total[pl.ds(pl.multiple_of((1 - low) * half, 8), half), :]

    return pl.pallas_call(
        kernel,
        grid=(rows // step,),
        in_specs=[SMEM, pl.BlockSpec((width, step), lambda i: (0, i))]
        + [pl.BlockSpec((step, wide), lambda i: (i, 0))] * len(grads),
        out_specs=[pl.BlockSpec((half, wide), lambda i: (0, 0))] * 2,
        out_shape=[jax.ShapeDtypeStruct((half, wide), jnp.float32)] * 2,
        scratch_shapes=[pltpu.VMEM((tall, wide), jnp.float32)],
        compiler_params=pltpu.CompilerParams(vmem_limit_bytes=16 * MIB),
        cost_estimate=cost(2 * width * rows * wide, 2 * rows * (width + wide)),
        name="weight_grad",
    )(low, feat_t, *grads)


def gather_shares(value, n, ring):
    if not ring:
        return [[lax.all_gather(value, "feat", axis=0, tiled=True)]]
    cut = value.shape[0] // RING_CUTS
    steps = [[value[h * cut : (h + 1) * cut] for h in range(RING_CUTS)]]
    for _ in range(n - 1):
        steps.append(
            [lax.ppermute(v, "feat", [(i, (i - 1) % n) for i in range(n)]) for v in steps[-1]]
        )
    return steps


def on_device(n_node, n_feat, feat_t, src_blocks, nbr_rows, tile_counts, w_neigh, w_self, bias, cotangent):
    width, rows = feat_t.shape
    hid = w_neigh.shape[1]
    blocks, slots = src_blocks.shape
    share = cotangent.shape[1]
    me = lax.axis_index("node")
    src = jnp.bitwise_xor(src_blocks // blocks, me) * blocks + src_blocks % blocks
    valid = jnp.arange(slots, dtype=jnp.int32)[None, :] < tile_counts[:, None]
    nbr = jnp.where(valid[:, :, None], nbr_rows, -1)
    inv = 1.0 / tile_counts.astype(jnp.float32)
    cot_rows = cotangent.reshape(share, hid)
    bias_row = bias[None, :]

    projected = project(feat_t, w_neigh, CHUNKS, jnp.bfloat16, [])
    own_terms = project(feat_t, w_self, CHUNKS, jnp.float32, projected[:1])

    ring = n_feat <= 4
    feat_index = jnp.reshape(lax.axis_index("feat"), (1,)).astype(jnp.int32)
    in_place = jnp.zeros((1,), jnp.int32)
    low = jnp.reshape(jnp.bitwise_and(me, 1), (1,)).astype(jnp.int32)
    part_pres = []
    for c in range(CHUNKS):
        held = {0: projected[c]}
        for mask in reversed(masks_of(n_node)):
            for k in list(held):
                value = held[k]
                if k:
                    behind = part_pres[-1] if part_pres else own_terms[0]
                    value, _ = lax.optimization_barrier((value, behind))
                held[k ^ mask] = swap(value, mask, n_node)
        gathered = [held[k] for k in range(n_node)]
        part_pres.append(
            mean_tiles(src, inv, nbr, gathered, own_terms[c], n_feat)
        )
    hidden = None
    grad_pres, pieces = [], []
    for c in range(CHUNKS):
        part_pre = part_pres[c]
        if pieces:
            steps = pieces[-1]
            near_end = steps[max(len(steps) - 2, 0)]
            part_pre, near_end[-1] = lax.optimization_barrier((part_pre, near_end[-1]))
        shares = [lax.psum_scatter(part_pre, "feat", scatter_dimension=0, tiled=True)]
        hidden, grad_pre = activate(
            shares, bias_row, cot_rows, hidden, c, part_pres[c + 1 : c + 2]
        )
        grad_pres.append(grad_pre)
        pieces.append(gather_shares(grad_pre, n_feat, ring and c < CHUNKS - 1))

    grads_n, grads_s, sums = [], [], []
    after = []
    arrived = None
    sent = []
    for c in range(CHUNKS):
        *tables, piece = spread_tiles(
            feat_index if len(pieces[c]) > 1 else in_place,
            src,
            inv,
            nbr,
            pieces[c],
            n_node,
            after,
        )
        held = {k: [v] for k, v in enumerate(tables)}
        for mask in masks_of(n_node):
            left = {}
            for k in reversed(list(held)):
                if k & mask:
                    mine = held[k ^ mask]
                    theirs = total_of(held[k])
                    if arrived is not None and mask == 1 and k != mask:
                        theirs, arrived = lax.optimization_barrier((theirs, arrived))
                        sent[c - 1][-1] = arrived
                    cut = rows // (NEAR_PIECES if mask == 1 and k != mask else 1)
                    got = [
                        swap(theirs[at : at + cut], mask, n_node) for at in range(0, rows, cut)
                    ]
                    left[k ^ mask] = mine + [got[0] if len(got) == 1 else jnp.concatenate(got)]
            held = left
            if mask == 1:
                after = [total_of(v) for k, v in held.items() if k]
                held = {k: [total_of(v)] if k else v for k, v in held.items()}
        arrived = held[0][-1]
        sent.append(held[0])
        both = sum_over_node(*weight_grad(low, feat_t, [piece], True), low, n_node)
        after = after + [both]
        grads_s.append(both[:width])
        sums.append(both[width])
    for terms in sent:
        grads_n.append(sum_over_node(*weight_grad(low, feat_t, terms, False), low, n_node))
    return (
        hidden.reshape(1, share, hid),
        jnp.concatenate(grads_n, axis=1),
        jnp.concatenate(grads_s, axis=1),
        jnp.concatenate(sums, axis=0),
    )


def solution(mesh):
    return jax.shard_map(
        functools.partial(on_device, mesh.shape["node"], mesh.shape["feat"]),
        mesh=mesh,
        in_specs=(
            P("feat", ("grp", "node")),
            P(("grp", "node"), None),
            P(("grp", "node"), None, None),
            P(("grp", "node")),
            P("feat", None),
            P("feat", None),
            P(),
            P(("grp", "node"), "feat", None),
        ),
        out_specs=(
            P(("grp", "node"), "feat", None),
            P(("grp", "feat"), None),
            P(("grp", "feat"), None),
            P("grp"),
        ),
        check_vma=False,
    )
```

```python
import functools

import jax
import jax.numpy as jnp
from jax import lax
from jax.experimental import pallas as pl
from jax.experimental.pallas import tpu as pltpu
from jax.sharding import PartitionSpec as P

CHUNKS = 2
NEAR_PIECES = 4
MIB = 1024 * 1024
HBM = pl.BlockSpec(memory_space=pl.ANY)
VMEM = pl.BlockSpec(memory_space=pltpu.VMEM)
SMEM = pl.BlockSpec(memory_space=pltpu.SMEM)
PARAMS = pltpu.CompilerParams(vmem_limit_bytes=24 * MIB)


def cost(flops, moved):
    return pl.CostEstimate(flops=flops, bytes_accessed=moved, transcendentals=0)


def swap(value, mask, n):
    return lax.ppermute(value, "node", [(i, i ^ mask) for i in range(n)])


def masks_of(n):
    assert n & (n - 1) == 0
    return [1 << i for i in range(n.bit_length() - 1)]


def sum_over_node(keep, send, low, n):
    near, *far = masks_of(n)
    total = keep + swap(send, near, n)
    for mask in far:
        total = total + swap(total, mask, n)
    other = swap(total, near, n)
    return jnp.where(
        low[0] == 0,
        jnp.concatenate([total, other], axis=0),
        jnp.concatenate([other, total], axis=0),
    )


def total_of(values):
    if len(values) == 1:
        return values[0]
    return sum(v.astype(jnp.float32) for v in values).astype(jnp.bfloat16)


def onehot_tile(row, ids):
    side = ids.shape[0]
    some = jnp.broadcast_to(row.astype(jnp.float32), (16, side)).astype(jnp.bfloat16)
    rows = jnp.concatenate([some] * (side // 16), axis=0)
    return jnp.where(ids == rows, jnp.bfloat16(1.0), jnp.bfloat16(0.0))


def side_ids(side):
    return lax.broadcasted_iota(jnp.int32, (side, side), 0).astype(jnp.float32).astype(jnp.bfloat16)


def project(feat_t, weight, n, dtype, after):
    width, rows = feat_t.shape
    hid = weight.shape[1]
    wide = hid // n
    step = min(1024, rows)

    def kernel(feat_ref, w_ref, *rest):
        outs, turned = rest[len(after) : len(after) + n], rest[-1]

        @pl.when(pl.program_id(0) == 0)
        def _():
            turned[...] = w_ref[...].astype(jnp.float32).T.astype(jnp.bfloat16)

        value = jnp.dot(turned[...], feat_ref[...], preferred_element_type=jnp.float32)
        for c in range(n):
            outs[c][...] = value[c * wide : (c + 1) * wide, :].astype(dtype)

    return pl.pallas_call(
        kernel,
        grid=(rows // step,),
        in_specs=[
            pl.BlockSpec((width, step), lambda i: (0, i)),
            pl.BlockSpec(weight.shape, lambda i: (0, 0)),
        ]
        + [HBM] * len(after),
        out_specs=[pl.BlockSpec((wide, step), lambda i: (0, i))] * n,
        out_shape=[jax.ShapeDtypeStruct((wide, rows), dtype)] * n,
        scratch_shapes=[pltpu.VMEM((hid, width), jnp.bfloat16)],
        compiler_params=pltpu.CompilerParams(vmem_limit_bytes=24 * MIB),
        cost_estimate=cost(2 * width * rows * hid, 2 * width * rows + 4 * hid * rows),
        name="project",
    )(feat_t, weight, *after)


def mean_tiles(src, inv, nbr, parts, self_term, n_feat):
    n = len(parts)
    wide, rows = self_term.shape
    blocks, slots, side = nbr.shape
    share = rows // n_feat
    per_share = blocks // n_feat

    def kernel(src_ref, inv_ref, nbr_ref, self_hbm, *rest):
        part_refs = rest[:n]
        out_hbm, table, self_ref, ready, sems, out_sems = rest[n:]
        copies = [
            pltpu.make_async_copy(ref, table.at[:, pl.ds(k * rows, rows)], sems.at[k])
            for k, ref in enumerate(part_refs)
        ]
        copies.append(pltpu.make_async_copy(self_hbm, self_ref, sems.at[n]))
        for copy in copies:
            copy.start()
        for copy in copies:
            copy.wait()
        ids = side_ids(side)

        def out_copy(s):
            at = pl.ds(pl.multiple_of(s * share, share), share)
            return pltpu.make_async_copy(ready.at[at, :], out_hbm.at[at, :], out_sems.at[s])

        @pl.loop(0, n_feat)
        def _(s):
            @pl.loop(0, per_share, unroll=2)
            def _(i):
                b = s * per_share + i
                picked = []
                tiles = []
                for t in range(slots):
                    at = pl.multiple_of(src_ref[b, t] * side, side)
                    picked.append(table[:, pl.ds(at, side)])
                    tiles.append(onehot_tile(nbr_ref[b, t : t + 1, :], ids))
                total = jnp.dot(
                    jnp.concatenate(picked, axis=1),
                    jnp.concatenate(tiles, axis=0),
                    preferred_element_type=jnp.float32,
                )
                own = self_ref[:, pl.ds(pl.multiple_of(b * side, side), side)]
                pre_t = total * inv_ref[b] + own
                at = pl.multiple_of(b * side, side)
                ready[pl.ds(at, side), :] = pre_t.T.astype(jnp.bfloat16)

            out_copy(s).start()

        @pl.loop(0, n_feat)
        def _(s):
            out_copy(s).wait()

    return pl.pallas_call(
        kernel,
        out_shape=jax.ShapeDtypeStruct((rows, wide), jnp.bfloat16),
        in_specs=[SMEM, SMEM, VMEM, HBM] + [HBM] * n,
        out_specs=HBM,
        scratch_shapes=[
            pltpu.VMEM((wide, n * rows), jnp.bfloat16),
            pltpu.VMEM((wide, rows), jnp.float32),
            pltpu.VMEM((rows, wide), jnp.bfloat16),
            pltpu.SemaphoreType.DMA((n + 1,)),
            pltpu.SemaphoreType.DMA((n_feat,)),
        ],
        compiler_params=pltpu.CompilerParams(vmem_limit_bytes=56 * MIB),
        cost_estimate=cost(
            8 * blocks * slots * side * side * wide, 2 * n * rows * wide + 6 * rows * wide
        ),
        name="mean_tiles",
    )(src, inv, nbr, self_term, *parts)


def activate(pre, bias, cot, hidden, c):
    share, wide = pre.shape
    hid = cot.shape[1]
    chunk = pl.BlockSpec((share, wide), lambda i: (0, c))
    whole = pl.BlockSpec((share, wide), lambda i: (0, 0))
    held = [] if hidden is None else [hidden]

    def kernel(bias_ref, cot_ref, pre_ref, *rest):
        hidden_ref, grad_ref = rest[-2:]
        value = pre_ref[...].astype(jnp.float32) + bias_ref[...]
        sigma = jax.nn.sigmoid(value)
        hidden_ref[...] = (value * sigma).astype(jnp.bfloat16)
        slope = sigma * (1.0 + value * (1.0 - sigma))
        grad_ref[...] = (cot_ref[...].astype(jnp.float32) * slope).astype(jnp.bfloat16)

    return pl.pallas_call(
        kernel,
        grid=(1,),
        in_specs=[pl.BlockSpec((1, wide), lambda i: (0, c)), chunk, whole] + [HBM] * len(held),
        out_specs=[chunk, whole],
        out_shape=[
            jax.ShapeDtypeStruct((share, hid), jnp.bfloat16),
            jax.ShapeDtypeStruct((share, wide), jnp.bfloat16),
        ],
        input_output_aliases={3: 0} if held else {},
        compiler_params=pltpu.CompilerParams(vmem_limit_bytes=24 * MIB),
        cost_estimate=cost(20 * share * wide, 8 * share * wide),
        name="activate",
    )(bias, cot, pre, *held)


def spread_tiles(src, inv, nbr, grad, n, after):
    rows, wide = grad.shape
    blocks, slots, side = nbr.shape
    step = 512
    assert slots % 2 == 0

    def kernel(src_ref, inv_ref, nbr_ref, grad_hbm, *rest):
        outs = rest[len(after) : len(after) + n]
        table, grad_ref, ready, sem, out_sems = rest[len(after) + n :]
        load = pltpu.make_async_copy(grad_hbm, grad_ref, sem)
        load.start()
        ids = side_ids(side)

        @pl.loop(0, n * rows // step)
        def _(i):
            table[pl.ds(pl.multiple_of(i * step, step), step), :] = jnp.zeros(
                (step, wide), jnp.float32
            )

        load.wait()

        @pl.loop(0, blocks, unroll=2)
        def _(b):
            g = grad_ref[pl.ds(pl.multiple_of(b * side, side), side), :]
            scale = inv_ref[b]
            tiles = [onehot_tile(nbr_ref[b, t : t + 1, :], ids) for t in range(slots)]
            terms = jnp.dot(
                jnp.concatenate(tiles, axis=0), g, preferred_element_type=jnp.float32
            )
            for t in range(0, slots, 2):
                one, two = src_ref[b, t], src_ref[b, t + 1]
                same = jnp.where(one == two, scale, 0.0)
                at_one = pl.ds(pl.multiple_of(one * side, side), side)
                at_two = pl.ds(pl.multiple_of(two * side, side), side)
                term_one = terms[t * side : (t + 1) * side, :]
                term_two = terms[(t + 1) * side : (t + 2) * side, :]
                new_one = table[at_one, :] + (term_one * scale + term_two * same)
                new_two = table[at_two, :] + (term_two * scale + term_one * same)
                table[at_one, :] = new_one
                table[at_two, :] = new_two

        copies = []
        for k in reversed(range(n)):

            @pl.loop(0, rows // step)
            def _(i, k=k):
                at = pl.multiple_of(i * step, step)
                ready[k, pl.ds(at, step), :] = table[pl.ds(k * rows + at, step), :].astype(
                    jnp.bfloat16
                )

            copies.append(pltpu.make_async_copy(ready.at[k], outs[k], out_sems.at[k]))
            copies[-1].start()
        for copy in copies:
            copy.wait()

    return pl.pallas_call(
        kernel,
        out_shape=[jax.ShapeDtypeStruct((rows, wide), jnp.bfloat16)] * n,
        in_specs=[SMEM, SMEM, VMEM, HBM] + [HBM] * len(after),
        out_specs=[HBM] * n,
        scratch_shapes=[
            pltpu.VMEM((n * rows, wide), jnp.float32),
            pltpu.VMEM((rows, wide), jnp.bfloat16),
            pltpu.VMEM((n, rows, wide), jnp.bfloat16),
            pltpu.SemaphoreType.DMA,
            pltpu.SemaphoreType.DMA((n,)),
        ],
        compiler_params=pltpu.CompilerParams(vmem_limit_bytes=40 * MIB),
        cost_estimate=cost(
            8 * blocks * slots * side * side * wide, 2 * n * rows * wide + 2 * rows * wide
        ),
        name="spread_tiles",
    )(src, inv, nbr, grad, *after)


def weight_grad(low, feat_t, grads, with_sum):
    width, rows = feat_t.shape
    wide = grads[0].shape[1]
    step = min(2048, rows)
    tall = width + (16 if with_sum else 0)
    half = tall // 2

    def kernel(low_ref, feat_ref, *rest):
        keep_ref, send_ref, total = rest[-3:]

        @pl.when(pl.program_id(0) == 0)
        def _():
            total[...] = jnp.zeros_like(total)

        value = rest[0][...]
        if len(grads) > 1:
            value = sum(ref[...].astype(jnp.float32) for ref in rest[:-3]).astype(jnp.bfloat16)
        total[:width, :] += jnp.dot(feat_ref[...], value, preferred_element_type=jnp.float32)
        if with_sum:
            total[width : width + 1, :] += jnp.sum(
                value.astype(jnp.float32), axis=0, keepdims=True
            )

        @pl.when(pl.program_id(0) == rows // step - 1)
        def _():
            low = low_ref[0]
            keep_ref[...] = total[pl.ds(pl.multiple_of(low * half, 8), half), :]
            send_ref[...] = total[pl.ds(pl.multiple_of((1 - low) * half, 8), half), :]

    return pl.pallas_call(
        kernel,
        grid=(rows // step,),
        in_specs=[SMEM, pl.BlockSpec((width, step), lambda i: (0, i))]
        + [pl.BlockSpec((step, wide), lambda i: (i, 0))] * len(grads),
        out_specs=[pl.BlockSpec((half, wide), lambda i: (0, 0))] * 2,
        out_shape=[jax.ShapeDtypeStruct((half, wide), jnp.float32)] * 2,
        scratch_shapes=[pltpu.VMEM((tall, wide), jnp.float32)],
        compiler_params=pltpu.CompilerParams(vmem_limit_bytes=16 * MIB),
        cost_estimate=cost(2 * width * rows * wide, 2 * rows * (width + wide)),
        name="weight_grad",
    )(low, feat_t, *grads)


def on_device(n_node, n_feat, feat_t, src_blocks, nbr_rows, tile_counts, w_neigh, w_self, bias, cotangent):
    width, rows = feat_t.shape
    hid = w_neigh.shape[1]
    blocks, slots = src_blocks.shape
    share = cotangent.shape[1]
    me = lax.axis_index("node")
    src = jnp.bitwise_xor(src_blocks // blocks, me) * blocks + src_blocks % blocks
    valid = jnp.arange(slots, dtype=jnp.int32)[None, :] < tile_counts[:, None]
    nbr = jnp.where(valid[:, :, None], nbr_rows, -1)
    inv = 1.0 / tile_counts.astype(jnp.float32)
    cot_rows = cotangent.reshape(share, hid)
    bias_row = bias[None, :]

    projected = project(feat_t, w_neigh, CHUNKS, jnp.bfloat16, [])
    own_terms = project(feat_t, w_self, CHUNKS, jnp.float32, projected[:1])

    low = jnp.reshape(jnp.bitwise_and(me, 1), (1,)).astype(jnp.int32)
    hidden = None
    part_pres, pieces = [], []
    for c in range(CHUNKS):
        held = {0: projected[c]}
        for mask in reversed(masks_of(n_node)):
            for k in list(held):
                value = held[k]
                if k:
                    behind = part_pres[-1] if part_pres else own_terms[0]
                    value, _ = lax.optimization_barrier((value, behind))
                held[k ^ mask] = swap(value, mask, n_node)
        gathered = [held[k] for k in range(n_node)]
        own_term = own_terms[c]
        if pieces:
            own_term, _ = lax.optimization_barrier((own_term, grad_pre))
        part_pre = mean_tiles(src, inv, nbr, gathered, own_term, n_feat)
        part_pres.append(part_pre)
        if pieces:
            part_pre, pieces[-1] = lax.optimization_barrier((part_pre, pieces[-1]))
        pre = lax.psum_scatter(part_pre, "feat", scatter_dimension=0, tiled=True)
        hidden, grad_pre = activate(pre, bias_row, cot_rows, hidden, c)
        pieces.append(lax.all_gather(grad_pre, "feat", axis=0, tiled=True))

    grads_n, grads_s, sums = [], [], []
    after = []
    arrived = None
    sent = []
    for c in range(CHUNKS):
        tables = spread_tiles(src, inv, nbr, pieces[c], n_node, after)
        held = {k: [v] for k, v in enumerate(tables)}
        for mask in masks_of(n_node):
            left = {}
            for k in reversed(list(held)):
                if k & mask:
                    mine = held[k ^ mask]
                    theirs = total_of(held[k])
                    if arrived is not None and mask == 1 and k != mask:
                        theirs, arrived = lax.optimization_barrier((theirs, arrived))
                        sent[c - 1][-1] = arrived
                    cut = rows // (NEAR_PIECES if mask == 1 and k != mask else 1)
                    got = [
                        swap(theirs[at : at + cut], mask, n_node) for at in range(0, rows, cut)
                    ]
                    left[k ^ mask] = mine + [got[0] if len(got) == 1 else jnp.concatenate(got)]
            held = left
            if mask == 1:
                after = [total_of(v) for k, v in held.items() if k]
                held = {k: [total_of(v)] if k else v for k, v in held.items()}
        arrived = held[0][-1]
        sent.append(held[0])
        both = sum_over_node(*weight_grad(low, feat_t, [pieces[c]], True), low, n_node)
        grads_s.append(both[:width])
        sums.append(both[width])
    for terms in sent:
        grads_n.append(sum_over_node(*weight_grad(low, feat_t, terms, False), low, n_node))
    return (
        hidden.reshape(1, share, hid),
        jnp.concatenate(grads_n, axis=1),
        jnp.concatenate(grads_s, axis=1),
        jnp.concatenate(sums, axis=0),
    )


def solution(mesh):
    return jax.shard_map(
        functools.partial(on_device, mesh.shape["node"], mesh.shape["feat"]),
        mesh=mesh,
        in_specs=(
            P("feat", ("grp", "node")),
            P(("grp", "node"), None),
            P(("grp", "node"), None, None),
            P(("grp", "node")),
            P("feat", None),
            P("feat", None),
            P(),
            P(("grp", "node"), "feat", None),
        ),
        out_specs=(
            P(("grp", "node"), "feat", None),
            P(("grp", "feat"), None),
            P(("grp", "feat"), None),
            P("grp"),
        ),
        check_vma=False,
    )
```

```python
import functools

import jax
import jax.numpy as jnp
from jax import lax
from jax.experimental import pallas as pl
from jax.experimental.pallas import tpu as pltpu
from jax.sharding import PartitionSpec as P

CHUNKS = 2
NEAR_PIECES = 4
MIB = 1024 * 1024
HBM = pl.BlockSpec(memory_space=pl.ANY)
VMEM = pl.BlockSpec(memory_space=pltpu.VMEM)
SMEM = pl.BlockSpec(memory_space=pltpu.SMEM)
PARAMS = pltpu.CompilerParams(vmem_limit_bytes=24 * MIB)


def cost(flops, moved):
    return pl.CostEstimate(flops=flops, bytes_accessed=moved, transcendentals=0)


def swap(value, mask, n):
    return lax.ppermute(value, "node", [(i, i ^ mask) for i in range(n)])


def masks_of(n):
    assert n & (n - 1) == 0
    return [1 << i for i in range(n.bit_length() - 1)]


def sum_near(keep, send, n):
    return keep + swap(send, masks_of(n)[0], n)


def sum_far(total, low, n):
    near, *far = masks_of(n)
    for mask in far:
        total = total + swap(total, mask, n)
    other = swap(total, near, n)
    return jnp.where(
        low[0] == 0,
        jnp.concatenate([total, other], axis=0),
        jnp.concatenate([other, total], axis=0),
    )


def total_of(values):
    if len(values) == 1:
        return values[0]
    return sum(v.astype(jnp.float32) for v in values).astype(jnp.bfloat16)


def onehot_tile(row, ids):
    side = ids.shape[0]
    some = jnp.broadcast_to(row.astype(jnp.float32), (16, side)).astype(jnp.bfloat16)
    rows = jnp.concatenate([some] * (side // 16), axis=0)
    return jnp.where(ids == rows, jnp.bfloat16(1.0), jnp.bfloat16(0.0))


def side_ids(side):
    return lax.broadcasted_iota(jnp.int32, (side, side), 0).astype(jnp.float32).astype(jnp.bfloat16)


def project(feat_t, weight, n, dtype, after):
    width, rows = feat_t.shape
    hid = weight.shape[1]
    wide = hid // n
    step = min(1024, rows)

    def kernel(feat_ref, w_ref, *rest):
        outs, turned = rest[len(after) : len(after) + n], rest[-1]

        @pl.when(pl.program_id(0) == 0)
        def _():
            turned[...] = w_ref[...].astype(jnp.float32).T.astype(jnp.bfloat16)

        value = jnp.dot(turned[...], feat_ref[...], preferred_element_type=jnp.float32)
        for c in range(n):
            outs[c][...] = value[c * wide : (c + 1) * wide, :].astype(dtype)

    return pl.pallas_call(
        kernel,
        grid=(rows // step,),
        in_specs=[
            pl.BlockSpec((width, step), lambda i: (0, i)),
            pl.BlockSpec(weight.shape, lambda i: (0, 0)),
        ]
        + [HBM] * len(after),
        out_specs=[pl.BlockSpec((wide, step), lambda i: (0, i))] * n,
        out_shape=[jax.ShapeDtypeStruct((wide, rows), dtype)] * n,
        scratch_shapes=[pltpu.VMEM((hid, width), jnp.bfloat16)],
        compiler_params=pltpu.CompilerParams(vmem_limit_bytes=24 * MIB),
        cost_estimate=cost(2 * width * rows * hid, 2 * width * rows + 4 * hid * rows),
        name="project",
    )(feat_t, weight, *after)


def mean_tiles(src, inv, nbr, parts, self_term, n_feat):
    n = len(parts)
    wide, rows = self_term.shape
    blocks, slots, side = nbr.shape
    share = rows // n_feat
    per_share = blocks // n_feat

    def kernel(src_ref, inv_ref, nbr_ref, self_hbm, *rest):
        part_refs = rest[:n]
        out_hbm, table, self_ref, ready, sems, out_sems = rest[n:]
        copies = [
            pltpu.make_async_copy(ref, table.at[:, pl.ds(k * rows, rows)], sems.at[k])
            for k, ref in enumerate(part_refs)
        ]
        copies.append(pltpu.make_async_copy(self_hbm, self_ref, sems.at[n]))
        for copy in copies:
            copy.start()
        for copy in copies:
            copy.wait()
        ids = side_ids(side)

        def out_copy(s):
            at = pl.ds(pl.multiple_of(s * share, share), share)
            return pltpu.make_async_copy(ready.at[at, :], out_hbm.at[at, :], out_sems.at[s])

        @pl.loop(0, n_feat)
        def _(s):
            @pl.loop(0, per_share, unroll=2)
            def _(i):
                b = s * per_share + i
                picked = []
                tiles = []
                for t in range(slots):
                    at = pl.multiple_of(src_ref[b, t] * side, side)
                    picked.append(table[:, pl.ds(at, side)])
                    tiles.append(onehot_tile(nbr_ref[b, t : t + 1, :], ids))
                total = jnp.dot(
                    jnp.concatenate(picked, axis=1),
                    jnp.concatenate(tiles, axis=0),
                    preferred_element_type=jnp.float32,
                )
                own = self_ref[:, pl.ds(pl.multiple_of(b * side, side), side)]
                pre_t = total * inv_ref[b] + own
                at = pl.multiple_of(b * side, side)
                ready[pl.ds(at, side), :] = pre_t.T.astype(jnp.bfloat16)

            out_copy(s).start()

        @pl.loop(0, n_feat)
        def _(s):
            out_copy(s).wait()

    return pl.pallas_call(
        kernel,
        out_shape=jax.ShapeDtypeStruct((rows, wide), jnp.bfloat16),
        in_specs=[SMEM, SMEM, VMEM, HBM] + [HBM] * n,
        out_specs=HBM,
        scratch_shapes=[
            pltpu.VMEM((wide, n * rows), jnp.bfloat16),
            pltpu.VMEM((wide, rows), jnp.float32),
            pltpu.VMEM((rows, wide), jnp.bfloat16),
            pltpu.SemaphoreType.DMA((n + 1,)),
            pltpu.SemaphoreType.DMA((n_feat,)),
        ],
        compiler_params=pltpu.CompilerParams(vmem_limit_bytes=56 * MIB),
        cost_estimate=cost(
            8 * blocks * slots * side * side * wide, 2 * n * rows * wide + 6 * rows * wide
        ),
        name="mean_tiles",
    )(src, inv, nbr, self_term, *parts)


def activate(pre, bias, cot, hidden, c):
    share, wide = pre.shape
    hid = cot.shape[1]
    chunk = pl.BlockSpec((share, wide), lambda i: (0, c))
    whole = pl.BlockSpec((share, wide), lambda i: (0, 0))
    held = [] if hidden is None else [hidden]

    def kernel(bias_ref, cot_ref, pre_ref, *rest):
        hidden_ref, grad_ref = rest[-2:]
        value = pre_ref[...].astype(jnp.float32) + bias_ref[...]
        sigma = jax.nn.sigmoid(value)
        hidden_ref[...] = (value * sigma).astype(jnp.bfloat16)
        slope = sigma * (1.0 + value * (1.0 - sigma))
        grad_ref[...] = (cot_ref[...].astype(jnp.float32) * slope).astype(jnp.bfloat16)

    return pl.pallas_call(
        kernel,
        grid=(1,),
        in_specs=[pl.BlockSpec((1, wide), lambda i: (0, c)), chunk, whole] + [HBM] * len(held),
        out_specs=[chunk, whole],
        out_shape=[
            jax.ShapeDtypeStruct((share, hid), jnp.bfloat16),
            jax.ShapeDtypeStruct((share, wide), jnp.bfloat16),
        ],
        input_output_aliases={3: 0} if held else {},
        compiler_params=pltpu.CompilerParams(vmem_limit_bytes=24 * MIB),
        cost_estimate=cost(20 * share * wide, 8 * share * wide),
        name="activate",
    )(bias, cot, pre, *held)


def spread_tiles(src, inv, nbr, grad, n, after):
    rows, wide = grad.shape
    blocks, slots, side = nbr.shape
    step = 512
    assert slots % 2 == 0

    def kernel(src_ref, inv_ref, nbr_ref, grad_hbm, *rest):
        outs = rest[len(after) : len(after) + n]
        table, grad_ref, ready, sem, out_sems = rest[len(after) + n :]
        load = pltpu.make_async_copy(grad_hbm, grad_ref, sem)
        load.start()
        ids = side_ids(side)

        @pl.loop(0, n * rows // step)
        def _(i):
            table[pl.ds(pl.multiple_of(i * step, step), step), :] = jnp.zeros(
                (step, wide), jnp.float32
            )

        load.wait()

        @pl.loop(0, blocks, unroll=2)
        def _(b):
            g = grad_ref[pl.ds(pl.multiple_of(b * side, side), side), :]
            scale = inv_ref[b]
            tiles = [onehot_tile(nbr_ref[b, t : t + 1, :], ids) for t in range(slots)]
            terms = jnp.dot(
                jnp.concatenate(tiles, axis=0), g, preferred_element_type=jnp.float32
            )
            for t in range(0, slots, 2):
                one, two = src_ref[b, t], src_ref[b, t + 1]
                same = jnp.where(one == two, scale, 0.0)
                at_one = pl.ds(pl.multiple_of(one * side, side), side)
                at_two = pl.ds(pl.multiple_of(two * side, side), side)
                term_one = terms[t * side : (t + 1) * side, :]
                term_two = terms[(t + 1) * side : (t + 2) * side, :]
                new_one = table[at_one, :] + (term_one * scale + term_two * same)
                new_two = table[at_two, :] + (term_two * scale + term_one * same)
                table[at_one, :] = new_one
                table[at_two, :] = new_two

        copies = []
        for k in reversed(range(n)):

            @pl.loop(0, rows // step)
            def _(i, k=k):
                at = pl.multiple_of(i * step, step)
                ready[k, pl.ds(at, step), :] = table[pl.ds(k * rows + at, step), :].astype(
                    jnp.bfloat16
                )

            copies.append(pltpu.make_async_copy(ready.at[k], outs[k], out_sems.at[k]))
            copies[-1].start()
        for copy in copies:
            copy.wait()

    return pl.pallas_call(
        kernel,
        out_shape=[jax.ShapeDtypeStruct((rows, wide), jnp.bfloat16)] * n,
        in_specs=[SMEM, SMEM, VMEM, HBM] + [HBM] * len(after),
        out_specs=[HBM] * n,
        scratch_shapes=[
            pltpu.VMEM((n * rows, wide), jnp.float32),
            pltpu.VMEM((rows, wide), jnp.bfloat16),
            pltpu.VMEM((n, rows, wide), jnp.bfloat16),
            pltpu.SemaphoreType.DMA,
            pltpu.SemaphoreType.DMA((n,)),
        ],
        compiler_params=pltpu.CompilerParams(vmem_limit_bytes=40 * MIB),
        cost_estimate=cost(
            8 * blocks * slots * side * side * wide, 2 * n * rows * wide + 2 * rows * wide
        ),
        name="spread_tiles",
    )(src, inv, nbr, grad, *after)


def weight_grad(low, feat_t, groups, with_sum):
    width, rows = feat_t.shape
    wide = groups[0][0].shape[1]
    step = min(2048, rows)
    tall = width + (16 if with_sum else 0)
    half = tall // 2
    flat = [array for group in groups for array in group]

    def kernel(low_ref, feat_ref, *rest):
        keep_ref, send_ref, total = rest[-3:]

        @pl.when(pl.program_id(0) == 0)
        def _():
            total[...] = jnp.zeros_like(total)

        at = 0
        values = []
        for group in groups:
            refs = rest[at : at + len(group)]
            at += len(group)
            values.append(refs[0][...])
            if len(group) > 1:
                values[-1] = sum(ref[...].astype(jnp.float32) for ref in refs).astype(jnp.bfloat16)
        value = jnp.concatenate(values, axis=1)
        total[:width, :] += jnp.dot(feat_ref[...], value, preferred_element_type=jnp.float32)
        if with_sum:
            total[width : width + 1, :] += jnp.sum(
                value.astype(jnp.float32), axis=0, keepdims=True
            )

        @pl.when(pl.program_id(0) == rows // step - 1)
        def _():
            low = low_ref[0]
            keep_ref[...] = total[pl.ds(pl.multiple_of(low * half, 8), half), :]
            send_ref[...] = total[pl.ds(pl.multiple_of((1 - low) * half, 8), half), :]

    all_wide = wide * len(groups)
    return pl.pallas_call(
        kernel,
        grid=(rows // step,),
        in_specs=[SMEM, pl.BlockSpec((width, step), lambda i: (0, i))]
        + [pl.BlockSpec((step, wide), lambda i: (i, 0))] * len(flat),
        out_specs=[pl.BlockSpec((half, all_wide), lambda i: (0, 0))] * 2,
        out_shape=[jax.ShapeDtypeStruct((half, all_wide), jnp.float32)] * 2,
        scratch_shapes=[pltpu.VMEM((tall, all_wide), jnp.float32)],
        compiler_params=pltpu.CompilerParams(vmem_limit_bytes=24 * MIB),
        cost_estimate=cost(2 * width * rows * all_wide, 2 * rows * (width + wide * len(flat))),
        name="weight_grad",
    )(low, feat_t, *flat)


def on_device(n_node, n_feat, feat_t, src_blocks, nbr_rows, tile_counts, w_neigh, w_self, bias, cotangent):
    width, rows = feat_t.shape
    hid = w_neigh.shape[1]
    blocks, slots = src_blocks.shape
    share = cotangent.shape[1]
    me = lax.axis_index("node")
    src = jnp.bitwise_xor(src_blocks // blocks, me) * blocks + src_blocks % blocks
    valid = jnp.arange(slots, dtype=jnp.int32)[None, :] < tile_counts[:, None]
    nbr = jnp.where(valid[:, :, None], nbr_rows, -1)
    inv = 1.0 / tile_counts.astype(jnp.float32)
    cot_rows = cotangent.reshape(share, hid)
    bias_row = bias[None, :]

    projected = project(feat_t, w_neigh, CHUNKS, jnp.bfloat16, [])
    own_terms = project(feat_t, w_self, CHUNKS, jnp.float32, projected[:1])

    low = jnp.reshape(jnp.bitwise_and(me, 1), (1,)).astype(jnp.int32)
    hidden = None
    part_pres, pieces = [], []
    for c in range(CHUNKS):
        held = {0: projected[c]}
        for mask in reversed(masks_of(n_node)):
            for k in list(held):
                value = held[k]
                if k:
                    behind = part_pres[-1] if part_pres else own_terms[0]
                    value, _ = lax.optimization_barrier((value, behind))
                held[k ^ mask] = swap(value, mask, n_node)
        gathered = [held[k] for k in range(n_node)]
        own_term = own_terms[c]
        if pieces:
            own_term, _ = lax.optimization_barrier((own_term, grad_pre))
        part_pre = mean_tiles(src, inv, nbr, gathered, own_term, n_feat)
        part_pres.append(part_pre)
        if pieces:
            part_pre, pieces[-1] = lax.optimization_barrier((part_pre, pieces[-1]))
        pre = lax.psum_scatter(part_pre, "feat", scatter_dimension=0, tiled=True)
        hidden, grad_pre = activate(pre, bias_row, cot_rows, hidden, c)
        pieces.append(lax.all_gather(grad_pre, "feat", axis=0, tiled=True))

    after = []
    arrived = None
    sent = []
    for c in range(CHUNKS):
        tables = spread_tiles(src, inv, nbr, pieces[c], n_node, after)
        held = {k: [v] for k, v in enumerate(tables)}
        for mask in masks_of(n_node):
            left = {}
            for k in reversed(list(held)):
                if k & mask:
                    mine = held[k ^ mask]
                    theirs = total_of(held[k])
                    if arrived is not None and mask == 1 and k != mask:
                        theirs, arrived = lax.optimization_barrier((theirs, arrived))
                        sent[c - 1][-1] = arrived
                    cut = rows // (NEAR_PIECES if mask == 1 and k != mask else 1)
                    got = [
                        swap(theirs[at : at + cut], mask, n_node) for at in range(0, rows, cut)
                    ]
                    left[k ^ mask] = mine + [got[0] if len(got) == 1 else jnp.concatenate(got)]
            held = left
            if mask == 1:
                after = [total_of(v) for k, v in held.items() if k]
                held = {k: [total_of(v)] if k else v for k, v in held.items()}
        arrived = held[0][-1]
        sent.append(held[0])
    early = [[piece] for piece in pieces] + sent[:-1]
    early = sum_near(*weight_grad(low, feat_t, early, True), n_node)
    last, early = lax.optimization_barrier((sent[-1], early))
    late = sum_near(*weight_grad(low, feat_t, [last], False), n_node)
    early = sum_far(early, low, n_node)
    late = sum_far(late, low, n_node)
    return (
        hidden.reshape(1, share, hid),
        jnp.concatenate([early[:width, hid:], late], axis=1),
        early[:width, :hid],
        early[width, :hid],
    )


def solution(mesh):
    return jax.shard_map(
        functools.partial(on_device, mesh.shape["node"], mesh.shape["feat"]),
        mesh=mesh,
        in_specs=(
            P("feat", ("grp", "node")),
            P(("grp", "node"), None),
            P(("grp", "node"), None, None),
            P(("grp", "node")),
            P("feat", None),
            P("feat", None),
            P(),
            P(("grp", "node"), "feat", None),
        ),
        out_specs=(
            P(("grp", "node"), "feat", None),
            P(("grp", "feat"), None),
            P(("grp", "feat"), None),
            P("grp"),
        ),
        check_vma=False,
    )
```

```python
import functools

import jax
import jax.numpy as jnp
from jax import lax
from jax.experimental import pallas as pl
from jax.experimental.pallas import tpu as pltpu
from jax.sharding import PartitionSpec as P

CHUNKS = 2
NEAR_PIECES = 4
MIB = 1024 * 1024
HBM = pl.BlockSpec(memory_space=pl.ANY)
VMEM = pl.BlockSpec(memory_space=pltpu.VMEM)
SMEM = pl.BlockSpec(memory_space=pltpu.SMEM)
PARAMS = pltpu.CompilerParams(vmem_limit_bytes=56 * MIB)


def cost(flops, moved):
    return pl.CostEstimate(flops=flops, bytes_accessed=moved, transcendentals=0)


def swap(value, mask, n):
    return lax.ppermute(value, "node", [(i, i ^ mask) for i in range(n)])


def masks_of(n):
    assert n & (n - 1) == 0
    return [1 << i for i in range(n.bit_length() - 1)]


def sum_near(keep, send, n):
    return keep + swap(send, masks_of(n)[0], n)


def sum_far(total, low, n):
    near, *far = masks_of(n)
    for mask in far:
        total = total + swap(total, mask, n)
    other = swap(total, near, n)
    return jnp.where(
        low[0] == 0,
        jnp.concatenate([total, other], axis=0),
        jnp.concatenate([other, total], axis=0),
    )


def total_of(values):
    if len(values) == 1:
        return values[0]
    return sum(v.astype(jnp.float32) for v in values).astype(jnp.bfloat16)


def onehot_tile(row, ids):
    side = ids.shape[0]
    some = jnp.broadcast_to(row.astype(jnp.float32), (16, side)).astype(jnp.bfloat16)
    rows = jnp.concatenate([some] * (side // 16), axis=0)
    return jnp.where(ids == rows, jnp.bfloat16(1.0), jnp.bfloat16(0.0))


def side_ids(side):
    return lax.broadcasted_iota(jnp.int32, (side, side), 0).astype(jnp.float32).astype(jnp.bfloat16)


def project(feat_t, weight, n, dtype, after):
    width, rows = feat_t.shape
    hid = weight.shape[1]
    wide = hid // n
    step = min(1024, rows)

    def kernel(feat_ref, w_ref, *rest):
        outs, turned = rest[len(after) : len(after) + n], rest[-1]

        @pl.when(pl.program_id(0) == 0)
        def _():
            turned[...] = w_ref[...].astype(jnp.float32).T.astype(jnp.bfloat16)

        value = jnp.dot(turned[...], feat_ref[...], preferred_element_type=jnp.float32)
        for c in range(n):
            outs[c][...] = value[c * wide : (c + 1) * wide, :].astype(dtype)

    return pl.pallas_call(
        kernel,
        grid=(rows // step,),
        in_specs=[
            pl.BlockSpec((width, step), lambda i: (0, i)),
            pl.BlockSpec(weight.shape, lambda i: (0, 0)),
        ]
        + [HBM] * len(after),
        out_specs=[pl.BlockSpec((wide, step), lambda i: (0, i))] * n,
        out_shape=[jax.ShapeDtypeStruct((wide, rows), dtype)] * n,
        scratch_shapes=[pltpu.VMEM((hid, width), jnp.bfloat16)],
        compiler_params=PARAMS,
        cost_estimate=cost(2 * width * rows * hid, 2 * width * rows + 4 * hid * rows),
        name="project",
    )(feat_t, weight, *after)


def mean_tiles(src, inv, nbr, parts, self_term, n_feat):
    n = len(parts)
    wide, rows = self_term.shape
    blocks, slots, side = nbr.shape
    share = rows // n_feat
    per_share = blocks // n_feat

    def kernel(src_ref, inv_ref, nbr_ref, self_hbm, *rest):
        part_refs = rest[:n]
        out_hbm, table, self_ref, ready, sems, out_sems = rest[n:]
        copies = [
            pltpu.make_async_copy(ref, table.at[:, pl.ds(k * rows, rows)], sems.at[k])
            for k, ref in enumerate(part_refs)
        ]
        copies.append(pltpu.make_async_copy(self_hbm, self_ref, sems.at[n]))
        for copy in copies:
            copy.start()
        for copy in copies:
            copy.wait()
        ids = side_ids(side)

        def out_copy(s):
            at = pl.ds(pl.multiple_of(s * share, share), share)
            return pltpu.make_async_copy(ready.at[at, :], out_hbm.at[at, :], out_sems.at[s])

        @pl.loop(0, n_feat)
        def _(s):
            @pl.loop(0, per_share, unroll=min(4, per_share))
            def _(i):
                b = s * per_share + i
                picked = []
                tiles = []
                for t in range(slots):
                    at = pl.multiple_of(src_ref[b, t] * side, side)
                    picked.append(table[:, pl.ds(at, side)])
                    tiles.append(onehot_tile(nbr_ref[b, t : t + 1, :], ids))
                total = jnp.dot(
                    jnp.concatenate(picked, axis=1),
                    jnp.concatenate(tiles, axis=0),
                    preferred_element_type=jnp.float32,
                )
                own = self_ref[:, pl.ds(pl.multiple_of(b * side, side), side)]
                pre_t = total * inv_ref[b] + own
                at = pl.multiple_of(b * side, side)
                ready[pl.ds(at, side), :] = pre_t.T.astype(jnp.bfloat16)

            out_copy(s).start()

        @pl.loop(0, n_feat)
        def _(s):
            out_copy(s).wait()

    return pl.pallas_call(
        kernel,
        out_shape=jax.ShapeDtypeStruct((rows, wide), jnp.bfloat16),
        in_specs=[SMEM, SMEM, VMEM, HBM] + [HBM] * n,
        out_specs=HBM,
        scratch_shapes=[
            pltpu.VMEM((wide, n * rows), jnp.bfloat16),
            pltpu.VMEM((wide, rows), jnp.float32),
            pltpu.VMEM((rows, wide), jnp.bfloat16),
            pltpu.SemaphoreType.DMA((n + 1,)),
            pltpu.SemaphoreType.DMA((n_feat,)),
        ],
        compiler_params=PARAMS,
        cost_estimate=cost(
            8 * blocks * slots * side * side * wide, 2 * n * rows * wide + 6 * rows * wide
        ),
        name="mean_tiles",
    )(src, inv, nbr, self_term, *parts)


def activate(pre, bias, cot, hidden, c):
    share, wide = pre.shape
    hid = cot.shape[1]
    chunk = pl.BlockSpec((share, wide), lambda i: (0, c))
    whole = pl.BlockSpec((share, wide), lambda i: (0, 0))
    held = [] if hidden is None else [hidden]

    def kernel(bias_ref, cot_ref, pre_ref, *rest):
        hidden_ref, grad_ref = rest[-2:]
        value = pre_ref[...].astype(jnp.float32) + bias_ref[...]
        sigma = jax.nn.sigmoid(value)
        hidden_ref[...] = (value * sigma).astype(jnp.bfloat16)
        slope = sigma * (1.0 + value * (1.0 - sigma))
        grad_ref[...] = (cot_ref[...].astype(jnp.float32) * slope).astype(jnp.bfloat16)

    return pl.pallas_call(
        kernel,
        grid=(1,),
        in_specs=[pl.BlockSpec((1, wide), lambda i: (0, c)), chunk, whole] + [HBM] * len(held),
        out_specs=[chunk, whole],
        out_shape=[
            jax.ShapeDtypeStruct((share, hid), jnp.bfloat16),
            jax.ShapeDtypeStruct((share, wide), jnp.bfloat16),
        ],
        input_output_aliases={3: 0} if held else {},
        compiler_params=PARAMS,
        cost_estimate=cost(20 * share * wide, 8 * share * wide),
        name="activate",
    )(bias, cot, pre, *held)


def spread_tiles(src, inv, nbr, grad, n, after):
    rows, wide = grad.shape
    blocks, slots, side = nbr.shape
    step = 512
    assert slots % 2 == 0

    def kernel(src_ref, inv_ref, nbr_ref, grad_hbm, *rest):
        outs = rest[len(after) : len(after) + n]
        table, grad_ref, ready, sem, out_sems = rest[len(after) + n :]
        load = pltpu.make_async_copy(grad_hbm, grad_ref, sem)
        load.start()
        ids = side_ids(side)

        @pl.loop(0, n * rows // step)
        def _(i):
            table[pl.ds(pl.multiple_of(i * step, step), step), :] = jnp.zeros(
                (step, wide), jnp.float32
            )

        load.wait()

        @pl.loop(0, blocks, unroll=min(4, blocks))
        def _(b):
            g = grad_ref[pl.ds(pl.multiple_of(b * side, side), side), :]
            scale = inv_ref[b]
            tiles = [onehot_tile(nbr_ref[b, t : t + 1, :], ids) for t in range(slots)]
            terms = jnp.dot(
                jnp.concatenate(tiles, axis=0), g, preferred_element_type=jnp.float32
            )
            for t in range(0, slots, 2):
                one, two = src_ref[b, t], src_ref[b, t + 1]
                same = jnp.where(one == two, scale, 0.0)
                at_one = pl.ds(pl.multiple_of(one * side, side), side)
                at_two = pl.ds(pl.multiple_of(two * side, side), side)
                term_one = terms[t * side : (t + 1) * side, :]
                term_two = terms[(t + 1) * side : (t + 2) * side, :]
                new_one = table[at_one, :] + (term_one * scale + term_two * same)
                new_two = table[at_two, :] + (term_two * scale + term_one * same)
                table[at_one, :] = new_one
                table[at_two, :] = new_two

        copies = []
        for k in reversed(range(n)):

            @pl.loop(0, rows // step)
            def _(i, k=k):
                at = pl.multiple_of(i * step, step)
                ready[k, pl.ds(at, step), :] = table[pl.ds(k * rows + at, step), :].astype(
                    jnp.bfloat16
                )

            copies.append(pltpu.make_async_copy(ready.at[k], outs[k], out_sems.at[k]))
            copies[-1].start()
        for copy in copies:
            copy.wait()

    return pl.pallas_call(
        kernel,
        out_shape=[jax.ShapeDtypeStruct((rows, wide), jnp.bfloat16)] * n,
        in_specs=[SMEM, SMEM, VMEM, HBM] + [HBM] * len(after),
        out_specs=[HBM] * n,
        scratch_shapes=[
            pltpu.VMEM((n * rows, wide), jnp.float32),
            pltpu.VMEM((rows, wide), jnp.bfloat16),
            pltpu.VMEM((n, rows, wide), jnp.bfloat16),
            pltpu.SemaphoreType.DMA,
            pltpu.SemaphoreType.DMA((n,)),
        ],
        compiler_params=PARAMS,
        cost_estimate=cost(
            8 * blocks * slots * side * side * wide, 2 * n * rows * wide + 2 * rows * wide
        ),
        name="spread_tiles",
    )(src, inv, nbr, grad, *after)


def weight_grad(low, feat_t, groups, with_sum):
    width, rows = feat_t.shape
    wide = groups[0][0].shape[1]
    step = min(2048, rows)
    tall = width + (16 if with_sum else 0)
    half = tall // 2
    flat = [array for group in groups for array in group]

    def kernel(low_ref, feat_ref, *rest):
        keep_ref, send_ref, total = rest[-3:]

        @pl.when(pl.program_id(0) == 0)
        def _():
            total[...] = jnp.zeros_like(total)

        at = 0
        values = []
        for group in groups:
            refs = rest[at : at + len(group)]
            at += len(group)
            values.append(refs[0][...])
            if len(group) > 1:
                values[-1] = sum(ref[...].astype(jnp.float32) for ref in refs).astype(jnp.bfloat16)
        value = jnp.concatenate(values, axis=1)
        total[:width, :] += jnp.dot(feat_ref[...], value, preferred_element_type=jnp.float32)
        if with_sum:
            total[width : width + 1, :] += jnp.sum(
                value.astype(jnp.float32), axis=0, keepdims=True
            )

        @pl.when(pl.program_id(0) == rows // step - 1)
        def _():
            low = low_ref[0]
            keep_ref[...] = total[pl.ds(pl.multiple_of(low * half, 8), half), :]
            send_ref[...] = total[pl.ds(pl.multiple_of((1 - low) * half, 8), half), :]

    all_wide = wide * len(groups)
    return pl.pallas_call(
        kernel,
        grid=(rows // step,),
        in_specs=[SMEM, pl.BlockSpec((width, step), lambda i: (0, i))]
        + [pl.BlockSpec((step, wide), lambda i: (i, 0))] * len(flat),
        out_specs=[pl.BlockSpec((half, all_wide), lambda i: (0, 0))] * 2,
        out_shape=[jax.ShapeDtypeStruct((half, all_wide), jnp.float32)] * 2,
        scratch_shapes=[pltpu.VMEM((tall, all_wide), jnp.float32)],
        compiler_params=pltpu.CompilerParams(vmem_limit_bytes=24 * MIB),
        cost_estimate=cost(2 * width * rows * all_wide, 2 * rows * (width + wide * len(flat))),
        name="weight_grad",
    )(low, feat_t, *flat)


def on_device(n_node, n_feat, feat_t, src_blocks, nbr_rows, tile_counts, w_neigh, w_self, bias, cotangent):
    width, rows = feat_t.shape
    hid = w_neigh.shape[1]
    blocks, slots = src_blocks.shape
    share = cotangent.shape[1]
    me = lax.axis_index("node")
    src = jnp.bitwise_xor(src_blocks // blocks, me) * blocks + src_blocks % blocks
    valid = jnp.arange(slots, dtype=jnp.int32)[None, :] < tile_counts[:, None]
    nbr = jnp.where(valid[:, :, None], nbr_rows, -1)
    inv = 1.0 / tile_counts.astype(jnp.float32)
    cot_rows = cotangent.reshape(share, hid)
    bias_row = bias[None, :]

    projected = project(feat_t, w_neigh, CHUNKS, jnp.bfloat16, [])
    own_terms = project(feat_t, w_self, CHUNKS, jnp.float32, projected[:1])

    low = jnp.reshape(jnp.bitwise_and(me, 1), (1,)).astype(jnp.int32)
    hidden = None
    part_pres, pieces = [], []
    for c in range(CHUNKS):
        held = {0: projected[c]}
        for mask in reversed(masks_of(n_node)):
            for k in list(held):
                value = held[k]
                if k:
                    behind = part_pres[-1] if part_pres else own_terms[0]
                    value, _ = lax.optimization_barrier((value, behind))
                held[k ^ mask] = swap(value, mask, n_node)
        gathered = [held[k] for k in range(n_node)]
        own_term = own_terms[c]
        if pieces:
            own_term, _ = lax.optimization_barrier((own_term, grad_pre))
        part_pre = mean_tiles(src, inv, nbr, gathered, own_term, n_feat)
        part_pres.append(part_pre)
        if pieces:
            part_pre, pieces[-1] = lax.optimization_barrier((part_pre, pieces[-1]))
        pre = lax.psum_scatter(part_pre, "feat", scatter_dimension=0, tiled=True)
        hidden, grad_pre = activate(pre, bias_row, cot_rows, hidden, c)
        pieces.append(lax.all_gather(grad_pre, "feat", axis=0, tiled=True))

    after = []
    arrived = None
    sent = []
    for c in range(CHUNKS):
        tables = spread_tiles(src, inv, nbr, pieces[c], n_node, after)
        held = {k: [v] for k, v in enumerate(tables)}
        for mask in masks_of(n_node):
            left = {}
            for k in reversed(list(held)):
                if k & mask:
                    mine = held[k ^ mask]
                    theirs = total_of(held[k])
                    if arrived is not None and mask == 1 and k != mask:
                        theirs, arrived = lax.optimization_barrier((theirs, arrived))
                        sent[c - 1][-1] = arrived
                    cut = rows // (NEAR_PIECES if mask == 1 and k != mask else 1)
                    got = [
                        swap(theirs[at : at + cut], mask, n_node) for at in range(0, rows, cut)
                    ]
                    left[k ^ mask] = mine + [got[0] if len(got) == 1 else jnp.concatenate(got)]
            held = left
            if mask == 1:
                after = [total_of(v) for k, v in held.items() if k]
                held = {k: [total_of(v)] if k else v for k, v in held.items()}
        arrived = held[0][-1]
        sent.append(held[0])
    early = [[piece] for piece in pieces] + sent[:-1]
    early = sum_near(*weight_grad(low, feat_t, early, True), n_node)
    last, early = lax.optimization_barrier((sent[-1], early))
    late = sum_near(*weight_grad(low, feat_t, [last], False), n_node)
    early = sum_far(early, low, n_node)
    late = sum_far(late, low, n_node)
    return (
        hidden.reshape(1, share, hid),
        jnp.concatenate([early[:width, hid:], late], axis=1),
        early[:width, :hid],
        early[width, :hid],
    )


def solution(mesh):
    return jax.shard_map(
        functools.partial(on_device, mesh.shape["node"], mesh.shape["feat"]),
        mesh=mesh,
        in_specs=(
            P("feat", ("grp", "node")),
            P(("grp", "node"), None),
            P(("grp", "node"), None, None),
            P(("grp", "node")),
            P("feat", None),
            P("feat", None),
            P(),
            P(("grp", "node"), "feat", None),
        ),
        out_specs=(
            P(("grp", "node"), "feat", None),
            P(("grp", "feat"), None),
            P(("grp", "feat"), None),
            P("grp"),
        ),
        check_vma=False,
    )
```

```python
import functools

import jax
import jax.numpy as jnp
from jax import lax
from jax.experimental import pallas as pl
from jax.experimental.pallas import tpu as pltpu
from jax.sharding import PartitionSpec as P

CHUNKS = 2
NEAR_PIECES = 4
MIB = 1024 * 1024
HBM = pl.BlockSpec(memory_space=pl.ANY)
VMEM = pl.BlockSpec(memory_space=pltpu.VMEM)
SMEM = pl.BlockSpec(memory_space=pltpu.SMEM)
PARAMS = pltpu.CompilerParams(vmem_limit_bytes=56 * MIB)


def cost(flops, moved):
    return pl.CostEstimate(flops=flops, bytes_accessed=moved, transcendentals=0)


def swap(value, mask, n):
    return lax.ppermute(value, "node", [(i, i ^ mask) for i in range(n)])


def masks_of(n):
    assert n & (n - 1) == 0
    return [1 << i for i in range(n.bit_length() - 1)]


def sum_near(keep, send, n):
    return keep + swap(send, masks_of(n)[0], n)


def sum_far(total, low, n):
    near, *far = masks_of(n)
    for mask in far:
        total = total + swap(total, mask, n)
    other = swap(total, near, n)
    return jnp.where(
        low[0] == 0,
        jnp.concatenate([total, other], axis=0),
        jnp.concatenate([other, total], axis=0),
    )


def total_of(values):
    if len(values) == 1:
        return values[0]
    return sum(v.astype(jnp.float32) for v in values).astype(jnp.bfloat16)


def onehot_tile(row, ids):
    side = ids.shape[0]
    some = jnp.broadcast_to(row.astype(jnp.float32), (16, side)).astype(jnp.bfloat16)
    rows = jnp.concatenate([some] * (side // 16), axis=0)
    return jnp.where(ids == rows, jnp.bfloat16(1.0), jnp.bfloat16(0.0))


def side_ids(side):
    return lax.broadcasted_iota(jnp.int32, (side, side), 0).astype(jnp.float32).astype(jnp.bfloat16)


def project(feat_t, weight, n, dtype, after):
    width, rows = feat_t.shape
    hid = weight.shape[1]
    wide = hid // n
    step = min(1024, rows)

    def kernel(feat_ref, w_ref, *rest):
        outs, turned = rest[len(after) : len(after) + n], rest[-1]

        @pl.when(pl.program_id(0) == 0)
        def _():
            turned[...] = w_ref[...].astype(jnp.float32).T.astype(jnp.bfloat16)

        value = jnp.dot(turned[...], feat_ref[...], preferred_element_type=jnp.float32)
        for c in range(n):
            outs[c][...] = value[c * wide : (c + 1) * wide, :].astype(dtype)

    return pl.pallas_call(
        kernel,
        grid=(rows // step,),
        in_specs=[
            pl.BlockSpec((width, step), lambda i: (0, i)),
            pl.BlockSpec(weight.shape, lambda i: (0, 0)),
        ]
        + [HBM] * len(after),
        out_specs=[pl.BlockSpec((wide, step), lambda i: (0, i))] * n,
        out_shape=[jax.ShapeDtypeStruct((wide, rows), dtype)] * n,
        scratch_shapes=[pltpu.VMEM((hid, width), jnp.bfloat16)],
        compiler_params=PARAMS,
        cost_estimate=cost(2 * width * rows * hid, 2 * width * rows + 4 * hid * rows),
        name="project",
    )(feat_t, weight, *after)


def mean_tiles(src, inv, nbr, parts, self_term, n_feat):
    n = len(parts)
    wide, rows = self_term.shape
    blocks, slots, side = nbr.shape
    share = rows // n_feat
    per_share = blocks // n_feat

    def kernel(src_ref, inv_ref, nbr_ref, self_hbm, *rest):
        part_refs = rest[:n]
        out_hbm, table, self_ref, ready, sems, out_sems = rest[n:]
        copies = [
            pltpu.make_async_copy(ref, table.at[:, pl.ds(k * rows, rows)], sems.at[k])
            for k, ref in enumerate(part_refs)
        ]
        copies.append(pltpu.make_async_copy(self_hbm, self_ref, sems.at[n]))
        for copy in copies:
            copy.start()
        for copy in copies:
            copy.wait()
        ids = side_ids(side)

        def out_copy(s):
            at = pl.ds(pl.multiple_of(s * share, share), share)
            return pltpu.make_async_copy(ready.at[at, :], out_hbm.at[at, :], out_sems.at[s])

        @pl.loop(0, n_feat)
        def _(s):
            @pl.loop(0, per_share, unroll=min(8, per_share))
            def _(i):
                b = s * per_share + i
                picked = []
                tiles = []
                for t in range(slots):
                    at = pl.multiple_of(src_ref[b, t] * side, side)
                    picked.append(table[:, pl.ds(at, side)])
                    tiles.append(onehot_tile(nbr_ref[b, t : t + 1, :], ids))
                total = jnp.dot(
                    jnp.concatenate(picked, axis=1),
                    jnp.concatenate(tiles, axis=0),
                    preferred_element_type=jnp.float32,
                )
                own = self_ref[:, pl.ds(pl.multiple_of(b * side, side), side)]
                pre_t = total * inv_ref[b] + own
                at = pl.multiple_of(b * side, side)
                ready[pl.ds(at, side), :] = pre_t.T.astype(jnp.bfloat16)

            out_copy(s).start()

        @pl.loop(0, n_feat)
        def _(s):
            out_copy(s).wait()

    return pl.pallas_call(
        kernel,
        out_shape=jax.ShapeDtypeStruct((rows, wide), jnp.bfloat16),
        in_specs=[SMEM, SMEM, VMEM, HBM] + [HBM] * n,
        out_specs=HBM,
        scratch_shapes=[
            pltpu.VMEM((wide, n * rows), jnp.bfloat16),
            pltpu.VMEM((wide, rows), jnp.float32),
            pltpu.VMEM((rows, wide), jnp.bfloat16),
            pltpu.SemaphoreType.DMA((n + 1,)),
            pltpu.SemaphoreType.DMA((n_feat,)),
        ],
        compiler_params=PARAMS,
        cost_estimate=cost(
            8 * blocks * slots * side * side * wide, 2 * n * rows * wide + 6 * rows * wide
        ),
        name="mean_tiles",
    )(src, inv, nbr, self_term, *parts)


def activate(pre, bias, cot, hidden, c):
    share, wide = pre.shape
    hid = cot.shape[1]
    chunk = pl.BlockSpec((share, wide), lambda i: (0, c))
    whole = pl.BlockSpec((share, wide), lambda i: (0, 0))
    held = [] if hidden is None else [hidden]

    def kernel(bias_ref, cot_ref, pre_ref, *rest):
        hidden_ref, grad_ref = rest[-2:]
        value = pre_ref[...].astype(jnp.float32) + bias_ref[...]
        sigma = jax.nn.sigmoid(value)
        hidden_ref[...] = (value * sigma).astype(jnp.bfloat16)
        slope = sigma * (1.0 + value * (1.0 - sigma))
        grad_ref[...] = (cot_ref[...].astype(jnp.float32) * slope).astype(jnp.bfloat16)

    return pl.pallas_call(
        kernel,
        grid=(1,),
        in_specs=[pl.BlockSpec((1, wide), lambda i: (0, c)), chunk, whole] + [HBM] * len(held),
        out_specs=[chunk, whole],
        out_shape=[
            jax.ShapeDtypeStruct((share, hid), jnp.bfloat16),
            jax.ShapeDtypeStruct((share, wide), jnp.bfloat16),
        ],
        input_output_aliases={3: 0} if held else {},
        compiler_params=PARAMS,
        cost_estimate=cost(20 * share * wide, 8 * share * wide),
        name="activate",
    )(bias, cot, pre, *held)


def spread_tiles(src, inv, nbr, grad, n, after):
    rows, wide = grad.shape
    blocks, slots, side = nbr.shape
    step = 512
    assert slots % 2 == 0

    def kernel(src_ref, inv_ref, nbr_ref, grad_hbm, *rest):
        outs = rest[len(after) : len(after) + n]
        table, grad_ref, ready, sem, out_sems = rest[len(after) + n :]
        load = pltpu.make_async_copy(grad_hbm, grad_ref, sem)
        load.start()
        ids = side_ids(side)

        @pl.loop(0, n * rows // step)
        def _(i):
            table[pl.ds(pl.multiple_of(i * step, step), step), :] = jnp.zeros(
                (step, wide), jnp.float32
            )

        load.wait()

        @pl.loop(0, blocks, unroll=min(2, blocks))
        def _(b):
            g = grad_ref[pl.ds(pl.multiple_of(b * side, side), side), :]
            scale = inv_ref[b]
            tiles = [onehot_tile(nbr_ref[b, t : t + 1, :], ids) for t in range(slots)]
            terms = jnp.dot(
                jnp.concatenate(tiles, axis=0), g, preferred_element_type=jnp.float32
            )
            for t in range(0, slots, 2):
                one, two = src_ref[b, t], src_ref[b, t + 1]
                same = jnp.where(one == two, scale, 0.0)
                at_one = pl.ds(pl.multiple_of(one * side, side), side)
                at_two = pl.ds(pl.multiple_of(two * side, side), side)
                term_one = terms[t * side : (t + 1) * side, :]
                term_two = terms[(t + 1) * side : (t + 2) * side, :]
                new_one = table[at_one, :] + (term_one * scale + term_two * same)
                new_two = table[at_two, :] + (term_two * scale + term_one * same)
                table[at_one, :] = new_one
                table[at_two, :] = new_two

        copies = []
        for k in reversed(range(n)):

            @pl.loop(0, rows // step)
            def _(i, k=k):
                at = pl.multiple_of(i * step, step)
                ready[k, pl.ds(at, step), :] = table[pl.ds(k * rows + at, step), :].astype(
                    jnp.bfloat16
                )

            copies.append(pltpu.make_async_copy(ready.at[k], outs[k], out_sems.at[k]))
            copies[-1].start()
        for copy in copies:
            copy.wait()

    return pl.pallas_call(
        kernel,
        out_shape=[jax.ShapeDtypeStruct((rows, wide), jnp.bfloat16)] * n,
        in_specs=[SMEM, SMEM, VMEM, HBM] + [HBM] * len(after),
        out_specs=[HBM] * n,
        scratch_shapes=[
            pltpu.VMEM((n * rows, wide), jnp.float32),
            pltpu.VMEM((rows, wide), jnp.bfloat16),
            pltpu.VMEM((n, rows, wide), jnp.bfloat16),
            pltpu.SemaphoreType.DMA,
            pltpu.SemaphoreType.DMA((n,)),
        ],
        compiler_params=PARAMS,
        cost_estimate=cost(
            8 * blocks * slots * side * side * wide, 2 * n * rows * wide + 2 * rows * wide
        ),
        name="spread_tiles",
    )(src, inv, nbr, grad, *after)


def weight_grad(low, feat_t, groups, with_sum):
    width, rows = feat_t.shape
    wide = groups[0][0].shape[1]
    step = min(2048, rows)
    tall = width + (16 if with_sum else 0)
    half = tall // 2
    flat = [array for group in groups for array in group]

    def kernel(low_ref, feat_ref, *rest):
        keep_ref, send_ref, total = rest[-3:]

        @pl.when(pl.program_id(0) == 0)
        def _():
            total[...] = jnp.zeros_like(total)

        at = 0
        values = []
        for group in groups:
            refs = rest[at : at + len(group)]
            at += len(group)
            values.append(refs[0][...])
            if len(group) > 1:
                values[-1] = sum(ref[...].astype(jnp.float32) for ref in refs).astype(jnp.bfloat16)
        value = jnp.concatenate(values, axis=1)
        total[:width, :] += jnp.dot(feat_ref[...], value, preferred_element_type=jnp.float32)
        if with_sum:
            total[width : width + 1, :] += jnp.sum(
                value.astype(jnp.float32), axis=0, keepdims=True
            )

        @pl.when(pl.program_id(0) == rows // step - 1)
        def _():
            low = low_ref[0]
            keep_ref[...] = total[pl.ds(pl.multiple_of(low * half, 8), half), :]
            send_ref[...] = total[pl.ds(pl.multiple_of((1 - low) * half, 8), half), :]

    all_wide = wide * len(groups)
    return pl.pallas_call(
        kernel,
        grid=(rows // step,),
        in_specs=[SMEM, pl.BlockSpec((width, step), lambda i: (0, i))]
        + [pl.BlockSpec((step, wide), lambda i: (i, 0))] * len(flat),
        out_specs=[pl.BlockSpec((half, all_wide), lambda i: (0, 0))] * 2,
        out_shape=[jax.ShapeDtypeStruct((half, all_wide), jnp.float32)] * 2,
        scratch_shapes=[pltpu.VMEM((tall, all_wide), jnp.float32)],
        compiler_params=pltpu.CompilerParams(vmem_limit_bytes=24 * MIB),
        cost_estimate=cost(2 * width * rows * all_wide, 2 * rows * (width + wide * len(flat))),
        name="weight_grad",
    )(low, feat_t, *flat)


def on_device(n_node, n_feat, feat_t, src_blocks, nbr_rows, tile_counts, w_neigh, w_self, bias, cotangent):
    width, rows = feat_t.shape
    hid = w_neigh.shape[1]
    blocks, slots = src_blocks.shape
    share = cotangent.shape[1]
    me = lax.axis_index("node")
    src = jnp.bitwise_xor(src_blocks // blocks, me) * blocks + src_blocks % blocks
    valid = jnp.arange(slots, dtype=jnp.int32)[None, :] < tile_counts[:, None]
    nbr = jnp.where(valid[:, :, None], nbr_rows, -1)
    inv = 1.0 / tile_counts.astype(jnp.float32)
    cot_rows = cotangent.reshape(share, hid)
    bias_row = bias[None, :]

    wide = hid // CHUNKS
    projected = []
    for c in range(CHUNKS):
        columns = w_neigh[:, c * wide : (c + 1) * wide]
        projected += project(feat_t, columns, 1, jnp.bfloat16, projected[-1:])
    own_terms = project(feat_t, w_self, CHUNKS, jnp.float32, projected[-1:])

    low = jnp.reshape(jnp.bitwise_and(me, 1), (1,)).astype(jnp.int32)
    hidden = None
    part_pres, pieces = [], []
    for c in range(CHUNKS):
        held = {0: projected[c]}
        for mask in reversed(masks_of(n_node)):
            for k in list(held):
                value = held[k]
                if k:
                    behind = part_pres[-1] if part_pres else own_terms[0]
                    value, _ = lax.optimization_barrier((value, behind))
                held[k ^ mask] = swap(value, mask, n_node)
        gathered = [held[k] for k in range(n_node)]
        own_term = own_terms[c]
        if pieces:
            own_term, _ = lax.optimization_barrier((own_term, grad_pre))
        part_pre = mean_tiles(src, inv, nbr, gathered, own_term, n_feat)
        part_pres.append(part_pre)
        if pieces:
            part_pre, pieces[-1] = lax.optimization_barrier((part_pre, pieces[-1]))
        pre = lax.psum_scatter(part_pre, "feat", scatter_dimension=0, tiled=True)
        hidden, grad_pre = activate(pre, bias_row, cot_rows, hidden, c)
        pieces.append(lax.all_gather(grad_pre, "feat", axis=0, tiled=True))

    after = []
    arrived = None
    sent = []
    for c in range(CHUNKS):
        tables = spread_tiles(src, inv, nbr, pieces[c], n_node, after)
        held = {k: [v] for k, v in enumerate(tables)}
        for mask in masks_of(n_node):
            left = {}
            for k in reversed(list(held)):
                if k & mask:
                    mine = held[k ^ mask]
                    theirs = total_of(held[k])
                    if arrived is not None and mask == 1 and k != mask:
                        theirs, arrived = lax.optimization_barrier((theirs, arrived))
                        sent[c - 1][-1] = arrived
                    split = mask == 1 and k != mask and c < CHUNKS - 1
                    cut = rows // (NEAR_PIECES if split else 1)
                    got = [
                        swap(theirs[at : at + cut], mask, n_node) for at in range(0, rows, cut)
                    ]
                    left[k ^ mask] = mine + [got[0] if len(got) == 1 else jnp.concatenate(got)]
            held = left
            if mask == 1:
                after = [total_of(v) for k, v in held.items() if k]
                held = {k: [total_of(v)] if k else v for k, v in held.items()}
        arrived = held[0][-1]
        sent.append(held[0])
    early = [[piece] for piece in pieces] + sent[:-1]
    early = sum_near(*weight_grad(low, feat_t, early, True), n_node)
    last, early = lax.optimization_barrier((sent[-1], early))
    late = sum_near(*weight_grad(low, feat_t, [last], False), n_node)
    early = sum_far(early, low, n_node)
    late = sum_far(late, low, n_node)
    return (
        hidden.reshape(1, share, hid),
        jnp.concatenate([early[:width, hid:], late], axis=1),
        early[:width, :hid],
        early[width, :hid],
    )


def solution(mesh):
    return jax.shard_map(
        functools.partial(on_device, mesh.shape["node"], mesh.shape["feat"]),
        mesh=mesh,
        in_specs=(
            P("feat", ("grp", "node")),
            P(("grp", "node"), None),
            P(("grp", "node"), None, None),
            P(("grp", "node")),
            P("feat", None),
            P("feat", None),
            P(),
            P(("grp", "node"), "feat", None),
        ),
        out_specs=(
            P(("grp", "node"), "feat", None),
            P(("grp", "feat"), None),
            P(("grp", "feat"), None),
            P("grp"),
        ),
        check_vma=False,
    )
```

```python
import functools

import jax
import jax.numpy as jnp
from jax import lax
from jax.experimental import pallas as pl
from jax.experimental.pallas import tpu as pltpu
from jax.sharding import PartitionSpec as P

CHUNKS = 2
NEAR_PIECES = 4
MIB = 1024 * 1024
HBM = pl.BlockSpec(memory_space=pl.ANY)
VMEM = pl.BlockSpec(memory_space=pltpu.VMEM)
SMEM = pl.BlockSpec(memory_space=pltpu.SMEM)
PARAMS = pltpu.CompilerParams(vmem_limit_bytes=56 * MIB)


def cost(flops, moved):
    return pl.CostEstimate(flops=flops, bytes_accessed=moved, transcendentals=0)


def swap(value, mask, n):
    return lax.ppermute(value, "node", [(i, i ^ mask) for i in range(n)])


def masks_of(n):
    assert n & (n - 1) == 0
    return [1 << i for i in range(n.bit_length() - 1)]


def sum_near(keep, send, n):
    return keep + swap(send, masks_of(n)[0], n)


def sum_far(total, n):
    for mask in masks_of(n)[1:]:
        total = total + swap(total, mask, n)
    return total


def both_halves(total, low, n):
    other = swap(total, masks_of(n)[0], n)
    return jnp.where(
        low[0] == 0,
        jnp.concatenate([total, other], axis=0),
        jnp.concatenate([other, total], axis=0),
    )


def total_of(values):
    if len(values) == 1:
        return values[0]
    return sum(v.astype(jnp.float32) for v in values).astype(jnp.bfloat16)


def onehot_tile(row, ids):
    side = ids.shape[0]
    some = jnp.broadcast_to(row.astype(jnp.float32), (16, side)).astype(jnp.bfloat16)
    rows = jnp.concatenate([some] * (side // 16), axis=0)
    return jnp.where(ids == rows, jnp.bfloat16(1.0), jnp.bfloat16(0.0))


def side_ids(side):
    return lax.broadcasted_iota(jnp.int32, (side, side), 0).astype(jnp.float32).astype(jnp.bfloat16)


def project(feat_t, weight, n, dtype, after):
    width, rows = feat_t.shape
    hid = weight.shape[1]
    wide = hid // n
    step = min(1024, rows)

    def kernel(feat_ref, w_ref, *rest):
        outs, turned = rest[len(after) : len(after) + n], rest[-1]

        @pl.when(pl.program_id(0) == 0)
        def _():
            turned[...] = w_ref[...].astype(jnp.float32).T.astype(jnp.bfloat16)

        value = jnp.dot(turned[...], feat_ref[...], preferred_element_type=jnp.float32)
        for c in range(n):
            outs[c][...] = value[c * wide : (c + 1) * wide, :].astype(dtype)

    return pl.pallas_call(
        kernel,
        grid=(rows // step,),
        in_specs=[
            pl.BlockSpec((width, step), lambda i: (0, i)),
            pl.BlockSpec(weight.shape, lambda i: (0, 0)),
        ]
        + [HBM] * len(after),
        out_specs=[pl.BlockSpec((wide, step), lambda i: (0, i))] * n,
        out_shape=[jax.ShapeDtypeStruct((wide, rows), dtype)] * n,
        scratch_shapes=[pltpu.VMEM((hid, width), jnp.bfloat16)],
        compiler_params=PARAMS,
        cost_estimate=cost(2 * width * rows * hid, 2 * width * rows + 4 * hid * rows),
        name="project",
    )(feat_t, weight, *after)


def mean_tiles(src, inv, nbr, parts, self_term, n_feat):
    n = len(parts)
    wide, rows = self_term.shape
    blocks, slots, side = nbr.shape
    share = rows // n_feat
    per_share = blocks // n_feat

    def kernel(src_ref, inv_ref, nbr_ref, self_hbm, *rest):
        part_refs = rest[:n]
        out_hbm, table, self_ref, ready, sems, out_sems = rest[n:]
        copies = [
            pltpu.make_async_copy(ref, table.at[:, pl.ds(k * rows, rows)], sems.at[k])
            for k, ref in enumerate(part_refs)
        ]
        copies.append(pltpu.make_async_copy(self_hbm, self_ref, sems.at[n]))
        for copy in copies:
            copy.start()
        for copy in copies:
            copy.wait()
        ids = side_ids(side)

        def out_copy(s):
            at = pl.ds(pl.multiple_of(s * share, share), share)
            return pltpu.make_async_copy(ready.at[at, :], out_hbm.at[at, :], out_sems.at[s])

        @pl.loop(0, n_feat)
        def _(s):
            @pl.loop(0, per_share, unroll=min(8, per_share))
            def _(i):
                b = s * per_share + i
                picked = []
                tiles = []
                for t in range(slots):
                    at = pl.multiple_of(src_ref[b, t] * side, side)
                    picked.append(table[:, pl.ds(at, side)])
                    tiles.append(onehot_tile(nbr_ref[b, t : t + 1, :], ids))
                total = jnp.dot(
                    jnp.concatenate(picked, axis=1),
                    jnp.concatenate(tiles, axis=0),
                    preferred_element_type=jnp.float32,
                )
                own = self_ref[:, pl.ds(pl.multiple_of(b * side, side), side)]
                pre_t = total * inv_ref[b] + own
                at = pl.multiple_of(b * side, side)
                ready[pl.ds(at, side), :] = pre_t.T.astype(jnp.bfloat16)

            out_copy(s).start()

        @pl.loop(0, n_feat)
        def _(s):
            out_copy(s).wait()

    return pl.pallas_call(
        kernel,
        out_shape=jax.ShapeDtypeStruct((rows, wide), jnp.bfloat16),
        in_specs=[SMEM, SMEM, VMEM, HBM] + [HBM] * n,
        out_specs=HBM,
        scratch_shapes=[
            pltpu.VMEM((wide, n * rows), jnp.bfloat16),
            pltpu.VMEM((wide, rows), jnp.float32),
            pltpu.VMEM((rows, wide), jnp.bfloat16),
            pltpu.SemaphoreType.DMA((n + 1,)),
            pltpu.SemaphoreType.DMA((n_feat,)),
        ],
        compiler_params=PARAMS,
        cost_estimate=cost(
            8 * blocks * slots * side * side * wide, 2 * n * rows * wide + 6 * rows * wide
        ),
        name="mean_tiles",
    )(src, inv, nbr, self_term, *parts)


def activate(pre, bias, cot, hidden, c):
    share, wide = pre.shape
    hid = cot.shape[1]
    chunk = pl.BlockSpec((share, wide), lambda i: (0, c))
    whole = pl.BlockSpec((share, wide), lambda i: (0, 0))
    held = [] if hidden is None else [hidden]

    def kernel(bias_ref, cot_ref, pre_ref, *rest):
        hidden_ref, grad_ref = rest[-2:]
        value = pre_ref[...].astype(jnp.float32) + bias_ref[...]
        sigma = jax.nn.sigmoid(value)
        hidden_ref[...] = (value * sigma).astype(jnp.bfloat16)
        slope = sigma * (1.0 + value * (1.0 - sigma))
        grad_ref[...] = (cot_ref[...].astype(jnp.float32) * slope).astype(jnp.bfloat16)

    return pl.pallas_call(
        kernel,
        grid=(1,),
        in_specs=[pl.BlockSpec((1, wide), lambda i: (0, c)), chunk, whole] + [HBM] * len(held),
        out_specs=[chunk, whole],
        out_shape=[
            jax.ShapeDtypeStruct((share, hid), jnp.bfloat16),
            jax.ShapeDtypeStruct((share, wide), jnp.bfloat16),
        ],
        input_output_aliases={3: 0} if held else {},
        compiler_params=PARAMS,
        cost_estimate=cost(20 * share * wide, 8 * share * wide),
        name="activate",
    )(bias, cot, pre, *held)


def spread_tiles(src, inv, nbr, grad, n, after):
    rows, wide = grad.shape
    blocks, slots, side = nbr.shape
    step = 512
    assert slots % 2 == 0

    def kernel(src_ref, inv_ref, nbr_ref, grad_hbm, *rest):
        outs = rest[len(after) : len(after) + n]
        table, grad_ref, ready, sem, out_sems = rest[len(after) + n :]
        load = pltpu.make_async_copy(grad_hbm, grad_ref, sem)
        load.start()
        ids = side_ids(side)

        @pl.loop(0, n * rows // step)
        def _(i):
            table[pl.ds(pl.multiple_of(i * step, step), step), :] = jnp.zeros(
                (step, wide), jnp.float32
            )

        load.wait()

        @pl.loop(0, blocks, unroll=min(4, blocks))
        def _(b):
            g = grad_ref[pl.ds(pl.multiple_of(b * side, side), side), :]
            scale = inv_ref[b]
            tiles = [onehot_tile(nbr_ref[b, t : t + 1, :], ids) for t in range(slots)]
            terms = jnp.dot(
                jnp.concatenate(tiles, axis=0), g, preferred_element_type=jnp.float32
            )
            for t in range(0, slots, 2):
                one, two = src_ref[b, t], src_ref[b, t + 1]
                same = jnp.where(one == two, scale, 0.0)
                at_one = pl.ds(pl.multiple_of(one * side, side), side)
                at_two = pl.ds(pl.multiple_of(two * side, side), side)
                term_one = terms[t * side : (t + 1) * side, :]
                term_two = terms[(t + 1) * side : (t + 2) * side, :]
                new_one = table[at_one, :] + (term_one * scale + term_two * same)
                new_two = table[at_two, :] + (term_two * scale + term_one * same)
                table[at_one, :] = new_one
                table[at_two, :] = new_two

        copies = []
        for k in reversed(range(n)):

            @pl.loop(0, rows // step)
            def _(i, k=k):
                at = pl.multiple_of(i * step, step)
                ready[k, pl.ds(at, step), :] = table[pl.ds(k * rows + at, step), :].astype(
                    jnp.bfloat16
                )

            copies.append(pltpu.make_async_copy(ready.at[k], outs[k], out_sems.at[k]))
            copies[-1].start()
        for copy in copies:
            copy.wait()

    return pl.pallas_call(
        kernel,
        out_shape=[jax.ShapeDtypeStruct((rows, wide), jnp.bfloat16)] * n,
        in_specs=[SMEM, SMEM, VMEM, HBM] + [HBM] * len(after),
        out_specs=[HBM] * n,
        scratch_shapes=[
            pltpu.VMEM((n * rows, wide), jnp.float32),
            pltpu.VMEM((rows, wide), jnp.bfloat16),
            pltpu.VMEM((n, rows, wide), jnp.bfloat16),
            pltpu.SemaphoreType.DMA,
            pltpu.SemaphoreType.DMA((n,)),
        ],
        compiler_params=PARAMS,
        cost_estimate=cost(
            8 * blocks * slots * side * side * wide, 2 * n * rows * wide + 2 * rows * wide
        ),
        name="spread_tiles",
    )(src, inv, nbr, grad, *after)


def weight_grad(low, feat_t, groups, with_sum):
    width, rows = feat_t.shape
    wide = groups[0][0].shape[1]
    step = min(2048, rows)
    tall = width + (16 if with_sum else 0)
    half = tall // 2
    flat = [array for group in groups for array in group]

    def kernel(low_ref, feat_ref, *rest):
        keep_ref, send_ref, total = rest[-3:]

        @pl.when(pl.program_id(0) == 0)
        def _():
            total[...] = jnp.zeros_like(total)

        at = 0
        values = []
        for group in groups:
            refs = rest[at : at + len(group)]
            at += len(group)
            values.append(refs[0][...])
            if len(group) > 1:
                values[-1] = sum(ref[...].astype(jnp.float32) for ref in refs).astype(jnp.bfloat16)
        value = jnp.concatenate(values, axis=1)
        total[:width, :] += jnp.dot(feat_ref[...], value, preferred_element_type=jnp.float32)
        if with_sum:
            total[width : width + 1, :] += jnp.sum(
                value.astype(jnp.float32), axis=0, keepdims=True
            )

        @pl.when(pl.program_id(0) == rows // step - 1)
        def _():
            low = low_ref[0]
            keep_ref[...] = total[pl.ds(pl.multiple_of(low * half, 8), half), :]
            send_ref[...] = total[pl.ds(pl.multiple_of((1 - low) * half, 8), half), :]

    all_wide = wide * len(groups)
    return pl.pallas_call(
        kernel,
        grid=(rows // step,),
        in_specs=[SMEM, pl.BlockSpec((width, step), lambda i: (0, i))]
        + [pl.BlockSpec((step, wide), lambda i: (i, 0))] * len(flat),
        out_specs=[pl.BlockSpec((half, all_wide), lambda i: (0, 0))] * 2,
        out_shape=[jax.ShapeDtypeStruct((half, all_wide), jnp.float32)] * 2,
        scratch_shapes=[pltpu.VMEM((tall, all_wide), jnp.float32)],
        compiler_params=pltpu.CompilerParams(vmem_limit_bytes=24 * MIB),
        cost_estimate=cost(2 * width * rows * all_wide, 2 * rows * (width + wide * len(flat))),
        name="weight_grad",
    )(low, feat_t, *flat)


def on_device(n_node, n_feat, feat_t, src_blocks, nbr_rows, tile_counts, w_neigh, w_self, bias, cotangent):
    width, rows = feat_t.shape
    hid = w_neigh.shape[1]
    blocks, slots = src_blocks.shape
    share = cotangent.shape[1]
    me = lax.axis_index("node")
    src = jnp.bitwise_xor(src_blocks // blocks, me) * blocks + src_blocks % blocks
    valid = jnp.arange(slots, dtype=jnp.int32)[None, :] < tile_counts[:, None]
    nbr = jnp.where(valid[:, :, None], nbr_rows, -1)
    inv = 1.0 / tile_counts.astype(jnp.float32)
    cot_rows = cotangent.reshape(share, hid)
    bias_row = bias[None, :]

    projected = project(feat_t, w_neigh, CHUNKS, jnp.bfloat16, [])
    own_terms = project(feat_t, w_self, CHUNKS, jnp.float32, projected[:1])

    low = jnp.reshape(jnp.bitwise_and(me, 1), (1,)).astype(jnp.int32)
    hidden = None
    part_pres, pieces = [], []
    for c in range(CHUNKS):
        held = {0: projected[c]}
        for mask in reversed(masks_of(n_node)):
            for k in list(held):
                value = held[k]
                if k:
                    behind = part_pres[-1] if part_pres else own_terms[0]
                    value, _ = lax.optimization_barrier((value, behind))
                held[k ^ mask] = swap(value, mask, n_node)
        gathered = [held[k] for k in range(n_node)]
        own_term = own_terms[c]
        if pieces:
            own_term, _ = lax.optimization_barrier((own_term, grad_pre))
        part_pre = mean_tiles(src, inv, nbr, gathered, own_term, n_feat)
        part_pres.append(part_pre)
        if pieces:
            part_pre, pieces[-1] = lax.optimization_barrier((part_pre, pieces[-1]))
        pre = lax.psum_scatter(part_pre, "feat", scatter_dimension=0, tiled=True)
        if c == 1:
            first = sum_near(*weight_grad(low, feat_t, [[pieces[0]]], True), n_node)
            pre, first = lax.optimization_barrier((pre, first))
            first = sum_far(first, n_node)
        hidden, grad_pre = activate(pre, bias_row, cot_rows, hidden, c)
        pieces.append(lax.all_gather(grad_pre, "feat", axis=0, tiled=True))

    after = []
    arrived = None
    sent = []
    for c in range(CHUNKS):
        tables = spread_tiles(src, inv, nbr, pieces[c], n_node, after)
        held = {k: [v] for k, v in enumerate(tables)}
        for mask in masks_of(n_node):
            left = {}
            for k in reversed(list(held)):
                if k & mask:
                    mine = held[k ^ mask]
                    theirs = total_of(held[k])
                    if arrived is not None and mask == 1 and k != mask:
                        theirs, arrived = lax.optimization_barrier((theirs, arrived))
                        sent[c - 1][-1] = arrived
                    cut = rows // (NEAR_PIECES if mask == 1 and k != mask else 1)
                    got = [
                        swap(theirs[at : at + cut], mask, n_node) for at in range(0, rows, cut)
                    ]
                    left[k ^ mask] = mine + [got[0] if len(got) == 1 else jnp.concatenate(got)]
            held = left
            if mask == 1:
                after = [total_of(v) for k, v in held.items() if k]
                held = {k: [total_of(v)] if k else v for k, v in held.items()}
                if c == 0 and CHUNKS > 1:
                    behind = {k: v for k, v in held.items() if k}
                    behind, first = lax.optimization_barrier((behind, first))
                    held.update(behind)
        arrived = held[0][-1]
        sent.append(held[0])
    early = [[piece] for piece in pieces[1:]] + sent[:-1]
    early = sum_near(*weight_grad(low, feat_t, early, True), n_node)
    last, early = lax.optimization_barrier((sent[-1], early))
    late = sum_near(*weight_grad(low, feat_t, [last], False), n_node)
    early = both_halves(sum_far(early, n_node), low, n_node)
    late = both_halves(sum_far(late, n_node), low, n_node)
    first = both_halves(first, low, n_node)
    rest = hid - first.shape[1]
    grad_self = jnp.concatenate([first, early[:, :rest]], axis=1)
    return (
        hidden.reshape(1, share, hid),
        jnp.concatenate([early[:width, rest:], late], axis=1),
        grad_self[:width],
        grad_self[width],
    )


def solution(mesh):
    return jax.shard_map(
        functools.partial(on_device, mesh.shape["node"], mesh.shape["feat"]),
        mesh=mesh,
        in_specs=(
            P("feat", ("grp", "node")),
            P(("grp", "node"), None),
            P(("grp", "node"), None, None),
            P(("grp", "node")),
            P("feat", None),
            P("feat", None),
            P(),
            P(("grp", "node"), "feat", None),
        ),
        out_specs=(
            P(("grp", "node"), "feat", None),
            P(("grp", "feat"), None),
            P(("grp", "feat"), None),
            P("grp"),
        ),
        check_vma=False,
    )
```

```python
import functools

import jax
import jax.numpy as jnp
from jax import lax
from jax.experimental import pallas as pl
from jax.experimental.pallas import tpu as pltpu
from jax.sharding import PartitionSpec as P

CHUNKS = 2
NEAR_PIECES = 4
MIB = 1024 * 1024
HBM = pl.BlockSpec(memory_space=pl.ANY)
VMEM = pl.BlockSpec(memory_space=pltpu.VMEM)
SMEM = pl.BlockSpec(memory_space=pltpu.SMEM)
PARAMS = pltpu.CompilerParams(vmem_limit_bytes=56 * MIB)


def cost(flops, moved):
    return pl.CostEstimate(flops=flops, bytes_accessed=moved, transcendentals=0)


def swap(value, mask, n):
    return lax.ppermute(value, "node", [(i, i ^ mask) for i in range(n)])


def masks_of(n):
    assert n & (n - 1) == 0
    return [1 << i for i in range(n.bit_length() - 1)]


def sum_near(keep, send, n):
    return keep + swap(send, masks_of(n)[0], n)


def sum_far(total, n):
    for mask in masks_of(n)[1:]:
        total = total + swap(total, mask, n)
    return total


def both_halves(total, low, n):
    other = swap(total, masks_of(n)[0], n)
    return jnp.where(
        low[0] == 0,
        jnp.concatenate([total, other], axis=0),
        jnp.concatenate([other, total], axis=0),
    )


def total_of(values):
    if len(values) == 1:
        return values[0]
    return sum(v.astype(jnp.float32) for v in values).astype(jnp.bfloat16)


def onehot_tile(row, ids):
    side = ids.shape[0]
    some = jnp.broadcast_to(row.astype(jnp.float32), (16, side)).astype(jnp.bfloat16)
    rows = jnp.concatenate([some] * (side // 16), axis=0)
    return jnp.where(ids == rows, jnp.bfloat16(1.0), jnp.bfloat16(0.0))


def side_ids(side):
    return lax.broadcasted_iota(jnp.int32, (side, side), 0).astype(jnp.float32).astype(jnp.bfloat16)


def project(feat_t, weight, n, dtype, after):
    width, rows = feat_t.shape
    hid = weight.shape[1]
    wide = hid // n
    step = min(1024, rows)

    def kernel(feat_ref, w_ref, *rest):
        outs, turned = rest[len(after) : len(after) + n], rest[-1]

        @pl.when(pl.program_id(0) == 0)
        def _():
            turned[...] = w_ref[...].astype(jnp.float32).T.astype(jnp.bfloat16)

        value = jnp.dot(turned[...], feat_ref[...], preferred_element_type=jnp.float32)
        for c in range(n):
            outs[c][...] = value[c * wide : (c + 1) * wide, :].astype(dtype)

    return pl.pallas_call(
        kernel,
        grid=(rows // step,),
        in_specs=[
            pl.BlockSpec((width, step), lambda i: (0, i)),
            pl.BlockSpec(weight.shape, lambda i: (0, 0)),
        ]
        + [HBM] * len(after),
        out_specs=[pl.BlockSpec((wide, step), lambda i: (0, i))] * n,
        out_shape=[jax.ShapeDtypeStruct((wide, rows), dtype)] * n,
        scratch_shapes=[pltpu.VMEM((hid, width), jnp.bfloat16)],
        compiler_params=PARAMS,
        cost_estimate=cost(2 * width * rows * hid, 2 * width * rows + 4 * hid * rows),
        name="project",
    )(feat_t, weight, *after)


def mean_tiles(src, inv, nbr, parts, self_term, n_feat):
    n = len(parts)
    wide, rows = self_term.shape
    blocks, slots, side = nbr.shape
    share = rows // n_feat
    per_share = blocks // n_feat

    def kernel(src_ref, inv_ref, nbr_ref, self_hbm, *rest):
        part_refs = rest[:n]
        out_hbm, table, self_ref, ready, sems, out_sems = rest[n:]
        copies = [
            pltpu.make_async_copy(ref, table.at[:, pl.ds(k * rows, rows)], sems.at[k])
            for k, ref in enumerate(part_refs)
        ]
        copies.append(pltpu.make_async_copy(self_hbm, self_ref, sems.at[n]))
        for copy in copies:
            copy.start()
        for copy in copies:
            copy.wait()
        ids = side_ids(side)

        def out_copy(s):
            at = pl.ds(pl.multiple_of(s * share, share), share)
            return pltpu.make_async_copy(ready.at[at, :], out_hbm.at[at, :], out_sems.at[s])

        @pl.loop(0, n_feat)
        def _(s):
            @pl.loop(0, per_share, unroll=min(16, per_share))
            def _(i):
                b = s * per_share + i
                picked = []
                tiles = []
                for t in range(slots):
                    at = pl.multiple_of(src_ref[b, t] * side, side)
                    picked.append(table[:, pl.ds(at, side)])
                    tiles.append(onehot_tile(nbr_ref[b, t : t + 1, :], ids))
                total = jnp.dot(
                    jnp.concatenate(picked, axis=1),
                    jnp.concatenate(tiles, axis=0),
                    preferred_element_type=jnp.float32,
                )
                own = self_ref[:, pl.ds(pl.multiple_of(b * side, side), side)]
                pre_t = total * inv_ref[b] + own
                at = pl.multiple_of(b * side, side)
                ready[pl.ds(at, side), :] = pre_t.T.astype(jnp.bfloat16)

            out_copy(s).start()

        @pl.loop(0, n_feat)
        def _(s):
            out_copy(s).wait()

    return pl.pallas_call(
        kernel,
        out_shape=jax.ShapeDtypeStruct((rows, wide), jnp.bfloat16),
        in_specs=[SMEM, SMEM, VMEM, HBM] + [HBM] * n,
        out_specs=HBM,
        scratch_shapes=[
            pltpu.VMEM((wide, n * rows), jnp.bfloat16),
            pltpu.VMEM((wide, rows), jnp.float32),
            pltpu.VMEM((rows, wide), jnp.bfloat16),
            pltpu.SemaphoreType.DMA((n + 1,)),
            pltpu.SemaphoreType.DMA((n_feat,)),
        ],
        compiler_params=PARAMS,
        cost_estimate=cost(
            8 * blocks * slots * side * side * wide, 2 * n * rows * wide + 6 * rows * wide
        ),
        name="mean_tiles",
    )(src, inv, nbr, self_term, *parts)


def activate(pre, bias, cot, hidden, c):
    share, wide = pre.shape
    hid = cot.shape[1]
    chunk = pl.BlockSpec((share, wide), lambda i: (0, c))
    whole = pl.BlockSpec((share, wide), lambda i: (0, 0))
    held = [] if hidden is None else [hidden]

    def kernel(bias_ref, cot_ref, pre_ref, *rest):
        hidden_ref, grad_ref = rest[-2:]
        value = pre_ref[...].astype(jnp.float32) + bias_ref[...]
        sigma = jax.nn.sigmoid(value)
        hidden_ref[...] = (value * sigma).astype(jnp.bfloat16)
        slope = sigma * (1.0 + value * (1.0 - sigma))
        grad_ref[...] = (cot_ref[...].astype(jnp.float32) * slope).astype(jnp.bfloat16)

    return pl.pallas_call(
        kernel,
        grid=(1,),
        in_specs=[pl.BlockSpec((1, wide), lambda i: (0, c)), chunk, whole] + [HBM] * len(held),
        out_specs=[chunk, whole],
        out_shape=[
            jax.ShapeDtypeStruct((share, hid), jnp.bfloat16),
            jax.ShapeDtypeStruct((share, wide), jnp.bfloat16),
        ],
        input_output_aliases={3: 0} if held else {},
        compiler_params=PARAMS,
        cost_estimate=cost(20 * share * wide, 8 * share * wide),
        name="activate",
    )(bias, cot, pre, *held)


def spread_tiles(src, inv, nbr, grad, n, after):
    rows, wide = grad.shape
    blocks, slots, side = nbr.shape
    step = 512
    assert slots % 2 == 0

    def kernel(src_ref, inv_ref, nbr_ref, grad_hbm, *rest):
        outs = rest[len(after) : len(after) + n]
        table, grad_ref, ready, sem, out_sems = rest[len(after) + n :]
        load = pltpu.make_async_copy(grad_hbm, grad_ref, sem)
        load.start()
        ids = side_ids(side)

        @pl.loop(0, n * rows // step)
        def _(i):
            table[pl.ds(pl.multiple_of(i * step, step), step), :] = jnp.zeros(
                (step, wide), jnp.float32
            )

        load.wait()

        @pl.loop(0, blocks, unroll=min(8, blocks))
        def _(b):
            g = grad_ref[pl.ds(pl.multiple_of(b * side, side), side), :]
            scale = inv_ref[b]
            tiles = [onehot_tile(nbr_ref[b, t : t + 1, :], ids) for t in range(slots)]
            terms = jnp.dot(
                jnp.concatenate(tiles, axis=0), g, preferred_element_type=jnp.float32
            )
            for t in range(0, slots, 2):
                one, two = src_ref[b, t], src_ref[b, t + 1]
                same = jnp.where(one == two, scale, 0.0)
                at_one = pl.ds(pl.multiple_of(one * side, side), side)
                at_two = pl.ds(pl.multiple_of(two * side, side), side)
                term_one = terms[t * side : (t + 1) * side, :]
                term_two = terms[(t + 1) * side : (t + 2) * side, :]
                new_one = table[at_one, :] + (term_one * scale + term_two * same)
                new_two = table[at_two, :] + (term_two * scale + term_one * same)
                table[at_one, :] = new_one
                table[at_two, :] = new_two

        copies = []
        for k in reversed(range(n)):

            @pl.loop(0, rows // step)
            def _(i, k=k):
                at = pl.multiple_of(i * step, step)
                ready[k, pl.ds(at, step), :] = table[pl.ds(k * rows + at, step), :].astype(
                    jnp.bfloat16
                )

            copies.append(pltpu.make_async_copy(ready.at[k], outs[k], out_sems.at[k]))
            copies[-1].start()
        for copy in copies:
            copy.wait()

    return pl.pallas_call(
        kernel,
        out_shape=[jax.ShapeDtypeStruct((rows, wide), jnp.bfloat16)] * n,
        in_specs=[SMEM, SMEM, VMEM, HBM] + [HBM] * len(after),
        out_specs=[HBM] * n,
        scratch_shapes=[
            pltpu.VMEM((n * rows, wide), jnp.float32),
            pltpu.VMEM((rows, wide), jnp.bfloat16),
            pltpu.VMEM((n, rows, wide), jnp.bfloat16),
            pltpu.SemaphoreType.DMA,
            pltpu.SemaphoreType.DMA((n,)),
        ],
        compiler_params=PARAMS,
        cost_estimate=cost(
            8 * blocks * slots * side * side * wide, 2 * n * rows * wide + 2 * rows * wide
        ),
        name="spread_tiles",
    )(src, inv, nbr, grad, *after)


def weight_grad(low, feat_t, groups, with_sum):
    width, rows = feat_t.shape
    wide = groups[0][0].shape[1]
    step = min(2048, rows)
    tall = width + (16 if with_sum else 0)
    half = tall // 2
    flat = [array for group in groups for array in group]

    def kernel(low_ref, feat_ref, *rest):
        keep_ref, send_ref, total = rest[-3:]

        @pl.when(pl.program_id(0) == 0)
        def _():
            total[...] = jnp.zeros_like(total)

        at = 0
        values = []
        for group in groups:
            refs = rest[at : at + len(group)]
            at += len(group)
            values.append(refs[0][...])
            if len(group) > 1:
                values[-1] = sum(ref[...].astype(jnp.float32) for ref in refs).astype(jnp.bfloat16)
        value = jnp.concatenate(values, axis=1)
        total[:width, :] += jnp.dot(feat_ref[...], value, preferred_element_type=jnp.float32)
        if with_sum:
            total[width : width + 1, :] += jnp.sum(
                value.astype(jnp.float32), axis=0, keepdims=True
            )

        @pl.when(pl.program_id(0) == rows // step - 1)
        def _():
            low = low_ref[0]
            keep_ref[...] = total[pl.ds(pl.multiple_of(low * half, 8), half), :]
            send_ref[...] = total[pl.ds(pl.multiple_of((1 - low) * half, 8), half), :]

    all_wide = wide * len(groups)
    return pl.pallas_call(
        kernel,
        grid=(rows // step,),
        in_specs=[SMEM, pl.BlockSpec((width, step), lambda i: (0, i))]
        + [pl.BlockSpec((step, wide), lambda i: (i, 0))] * len(flat),
        out_specs=[pl.BlockSpec((half, all_wide), lambda i: (0, 0))] * 2,
        out_shape=[jax.ShapeDtypeStruct((half, all_wide), jnp.float32)] * 2,
        scratch_shapes=[pltpu.VMEM((tall, all_wide), jnp.float32)],
        compiler_params=pltpu.CompilerParams(vmem_limit_bytes=24 * MIB),
        cost_estimate=cost(2 * width * rows * all_wide, 2 * rows * (width + wide * len(flat))),
        name="weight_grad",
    )(low, feat_t, *flat)


def on_device(n_node, n_feat, feat_t, src_blocks, nbr_rows, tile_counts, w_neigh, w_self, bias, cotangent):
    width, rows = feat_t.shape
    hid = w_neigh.shape[1]
    blocks, slots = src_blocks.shape
    share = cotangent.shape[1]
    me = lax.axis_index("node")
    src = jnp.bitwise_xor(src_blocks // blocks, me) * blocks + src_blocks % blocks
    valid = jnp.arange(slots, dtype=jnp.int32)[None, :] < tile_counts[:, None]
    nbr = jnp.where(valid[:, :, None], nbr_rows, -1)
    inv = 1.0 / tile_counts.astype(jnp.float32)
    cot_rows = cotangent.reshape(share, hid)
    bias_row = bias[None, :]

    projected = project(feat_t, w_neigh, CHUNKS, jnp.bfloat16, [])
    own_terms = project(feat_t, w_self, CHUNKS, jnp.float32, projected[:1])

    low = jnp.reshape(jnp.bitwise_and(me, 1), (1,)).astype(jnp.int32)
    hidden = None
    part_pres, pieces = [], []
    for c in range(CHUNKS):
        held = {0: projected[c]}
        for mask in reversed(masks_of(n_node)):
            for k in list(held):
                value = held[k]
                if k:
                    behind = part_pres[-1] if part_pres else own_terms[0]
                    value, _ = lax.optimization_barrier((value, behind))
                held[k ^ mask] = swap(value, mask, n_node)
        gathered = [held[k] for k in range(n_node)]
        own_term = own_terms[c]
        if pieces:
            own_term, _ = lax.optimization_barrier((own_term, grad_pre))
        part_pre = mean_tiles(src, inv, nbr, gathered, own_term, n_feat)
        part_pres.append(part_pre)
        if pieces:
            part_pre, pieces[-1] = lax.optimization_barrier((part_pre, pieces[-1]))
        pre = lax.psum_scatter(part_pre, "feat", scatter_dimension=0, tiled=True)
        if c == 1:
            first = sum_near(*weight_grad(low, feat_t, [[pieces[0]]], True), n_node)
            pre, first = lax.optimization_barrier((pre, first))
            first = sum_far(first, n_node)
        hidden, grad_pre = activate(pre, bias_row, cot_rows, hidden, c)
        pieces.append(lax.all_gather(grad_pre, "feat", axis=0, tiled=True))

    after = []
    arrived = None
    sent = []
    for c in range(CHUNKS):
        tables = spread_tiles(src, inv, nbr, pieces[c], n_node, after)
        held = {k: [v] for k, v in enumerate(tables)}
        for mask in masks_of(n_node):
            left = {}
            for k in reversed(list(held)):
                if k & mask:
                    mine = held[k ^ mask]
                    theirs = total_of(held[k])
                    if arrived is not None and mask == 1 and k != mask:
                        theirs, arrived = lax.optimization_barrier((theirs, arrived))
                        sent[c - 1][-1] = arrived
                    cut = rows // (NEAR_PIECES if mask == 1 and k != mask else 1)
                    got = [
                        swap(theirs[at : at + cut], mask, n_node) for at in range(0, rows, cut)
                    ]
                    left[k ^ mask] = mine + [got[0] if len(got) == 1 else jnp.concatenate(got)]
            held = left
            if mask == 1:
                after = [total_of(v) for k, v in held.items() if k]
                held = {k: [total_of(v)] if k else v for k, v in held.items()}
                if c == 0 and CHUNKS > 1:
                    behind = {k: v for k, v in held.items() if k}
                    behind, first = lax.optimization_barrier((behind, first))
                    held.update(behind)
        arrived = held[0][-1]
        sent.append(held[0])
    early = [[piece] for piece in pieces[1:]] + sent[:-1]
    early = sum_near(*weight_grad(low, feat_t, early, True), n_node)
    last, early = lax.optimization_barrier((sent[-1], early))
    late = sum_near(*weight_grad(low, feat_t, [last], False), n_node)
    early = both_halves(sum_far(early, n_node), low, n_node)
    late = both_halves(sum_far(late, n_node), low, n_node)
    first = both_halves(first, low, n_node)
    rest = hid - first.shape[1]
    grad_self = jnp.concatenate([first, early[:, :rest]], axis=1)
    return (
        hidden.reshape(1, share, hid),
        jnp.concatenate([early[:width, rest:], late], axis=1),
        grad_self[:width],
        grad_self[width],
    )


def solution(mesh):
    return jax.shard_map(
        functools.partial(on_device, mesh.shape["node"], mesh.shape["feat"]),
        mesh=mesh,
        in_specs=(
            P("feat", ("grp", "node")),
            P(("grp", "node"), None),
            P(("grp", "node"), None, None),
            P(("grp", "node")),
            P("feat", None),
            P("feat", None),
            P(),
            P(("grp", "node"), "feat", None),
        ),
        out_specs=(
            P(("grp", "node"), "feat", None),
            P(("grp", "feat"), None),
            P(("grp", "feat"), None),
            P("grp"),
        ),
        check_vma=False,
    )
```
